32 devices in a mesh: rows: 4 (over y, x), seq: 8 (over z, core).
Axes of the slice: x: 2, y: 2, z: 4, core: 2. Of those that a mesh axis runs over, the one named last changes fastest.
Arguments:
- tokens: bfloat16 [8, 1024, 2048], P('rows', 'seq'), may hold values from -6 to 6
- kv_cache: bfloat16 [8, 1024, 2, 512], P('rows', 'seq'), may hold values from -6 to 6
- lengths: int32 [8], P('rows'), may hold values from 1 to 1024, as said below
- norm_gains: float32 [2, 2048], replicated, may hold values from 0.5 to 1.5
- query_weight: bfloat16 [2048, 2048], P('seq'), may hold values from -0.125 to 0.125
- output_weight: bfloat16 [2048, 2048], P('seq'), may hold values from -1 to 1
- ffn_in_weight: bfloat16 [8192, 2, 2048], P('seq'), may hold values from -0.125 to 0.125
- down_weight: bfloat16 [8192, 2048], P('seq'), may hold values from -0.0625 to 0.0625
- cotangent: bfloat16 [8, 1024, 2048], P('rows', 'seq'), may hold values from -6 to 6
Outputs:
- layer_out: bfloat16 [8, 1024, 2048], P('rows', 'seq')
- input_grad: float32 [8, 1024, 2048], P('rows', 'seq')
- cache_grad: float32 [8, 1024, 2, 512], P('rows', 'seq')
- gain_grad: float32 [2, 2048], replicated
- query_weight_grad: float32 [2048, 2048], P('seq')
- output_weight_grad: float32 [2048, 2048], P('seq')
- ffn_in_grad: float32 [8192, 2, 2048], P('seq')
- down_grad: float32 [8192, 2048], P('seq')
The draws below stay inside these ranges and needn't reach their ends.
Inputs may be any that keep to these rules, and one draw needn't show every extreme that they name: `lengths`: in every aligned group of 2 rows at least one row has length 1024; the others are heavy-tailed.
All inputs are finite; a program needn't handle non-finite values.
Results may differ from the reference program's by a relative error of at most 0.024.
Values may be sent and summed in bfloat16 or wider, within the bound.
No kernel may reach another device: no remote copies, remote signals or barrier semaphores. Data moves between devices by JAX's collectives and lax.ppermute only.
A program may use at most 384 MiB of HBM per device.

```python
import jax
import jax.numpy as jnp
from jax import lax

D = 2048
HEADS = 16
HEAD = 128
KV = 4
FF = 8192
ROWS_DEV = 2
HQ = 2048
KVW = 512
GROUP = 4
LENGTH = 1024
BATCH = 8


def draw_lengths(key, part):
    key_spread = jax.random.fold_in(key, 11)
    key_chosen = jax.random.fold_in(key, 12)
    spread = jax.random.randint(key_spread, (BATCH,), 1, 65, dtype=jnp.int32)
    partial_len = jnp.maximum(LENGTH * spread * spread // 4096, 1)
    chosen = jax.random.randint(key_chosen, (BATCH // ROWS_DEV,), 0, ROWS_DEV, dtype=jnp.int32)
    slot_index = jnp.arange(BATCH, dtype=jnp.int32) % ROWS_DEV
    full_row = slot_index == jnp.repeat(chosen, ROWS_DEV)
    return jnp.where(full_row, LENGTH, partial_len).astype(jnp.int32)


def levels(key, dims, split, low, high):
    def one(dim, parts):
        heights = jax.random.uniform(jax.random.fold_in(jax.random.fold_in(key, 6), dim), (parts,), jnp.float32, low / len(split), high / len(split))
        return jnp.repeat(jnp.exp(heights), dims[dim] // parts).reshape((-1,) + (1,) * (len(dims) - dim - 1))

    level = one(*split[0])
    for cut in split[1:]:
        level = level * one(*cut)
    return level


def normal_values(key, extent, scale, bound, shards=(), kind=jnp.bfloat16):
    level = levels(key, extent, shards, -0.22, 0.18) if shards else 1.0
    array = jax.random.normal(key, extent, jnp.float32) * scale * level
    return jnp.minimum(jnp.maximum(array, -bound), bound).astype(kind)


def setup_inputs(seed: int = 0) -> dict:
    streams_of = jax.random.split(jax.random.key(seed), 10)
    tokens = normal_values(streams_of[0], (BATCH, LENGTH, D), 1.0, 6.0, ((0, 4), (1, 8)))
    kv_cache = normal_values(streams_of[1], (BATCH, LENGTH, 2, KVW), 1.0, 6.0, ((0, 4), (1, 8)))
    lengths = draw_lengths(jax.random.fold_in(streams_of[9], 71), 0)
    norm_gains = jnp.clip(1.0 + 0.1 * jax.random.normal(streams_of[3], (2, D), jnp.float32), 0.5, 1.5)
    query_weight = normal_values(streams_of[4], (HQ, D), D ** -0.5, 0.125, ((0, 8),))
    output_weight = normal_values(streams_of[5], (HQ, D), (max(1, HQ * 16 // LENGTH)) ** -0.5, 1.0, ((0, 8),))
    ffn_in_weight = normal_values(streams_of[6], (FF, 2, D), D ** -0.5, 0.125, ((0, 8),))
    down_weight = normal_values(streams_of[7], (FF, D), FF ** -0.5, 0.0625, ((0, 8),))
    cotangent = normal_values(streams_of[8], (BATCH, LENGTH, D), 1.0, 6.0, ((0, 4), (1, 8)))
    return dict(tokens=tokens, kv_cache=kv_cache, lengths=lengths, norm_gains=norm_gains, query_weight=query_weight, output_weight=output_weight, ffn_in_weight=ffn_in_weight, down_weight=down_weight, cotangent=cotangent)


EPS = 1e-05
NEG = -1e+30
HIGH = lax.Precision.HIGHEST

@jax.custom_vjp
def low(v):
    return lax.optimization_barrier(v.astype(jnp.bfloat16)).astype(jnp.float32)

@jax.custom_vjp
def low_back(v):
    return v

def low_keep(v):
    return (low(v), None)

def low_pass(kept, grad):
    return (grad,)

def back_keep(v):
    return (v, None)

def back_low(kept, grad):
    return (low(grad),)
low.defvjp(low_keep, low_pass)
low_back.defvjp(back_keep, back_low)

def norm_rows(values, gain):
    inverse = lax.rsqrt(lax.optimization_barrier(jnp.mean(values * values, axis=-1, keepdims=True)) + EPS)
    return values * inverse * gain

def attend_block(query_block, block_start, keys, values, length):
    count = query_block.shape[0]
    query_pos = block_start + jnp.arange(count, dtype=jnp.int32)
    key_pos = jnp.arange(keys.shape[0], dtype=jnp.int32)
    scores = jnp.einsum('qkgd,rkd->kgqr', query_block, keys, precision=HIGH) * HEAD ** (-0.5)
    scores = low_back(scores)
    limit = jnp.minimum(query_pos, length - 1)
    valid = key_pos[None, :] <= limit[:, None]
    scores = jnp.where(valid[None, None], scores, NEG)
    largest = lax.optimization_barrier(jnp.max(scores, axis=-1, keepdims=True))
    weights = jnp.exp(scores - largest)
    total = lax.optimization_barrier(jnp.sum(weights, axis=-1))
    mixed = jnp.einsum('kgqr,rkd->qkgd', low(weights), values, precision=HIGH)
    mixed = mixed / jnp.transpose(total, (2, 0, 1))[..., None]
    return mixed.reshape(count, HEADS * HEAD)

def layer_row(row_in, row_cache, length, gains, query_weight, output_weight, ffn_weight, down_weight):
    seq_len = row_in.shape[0]
    normed = low(norm_rows(row_in, gains[0]))
    query = low(low_back(jnp.dot(normed, query_weight.T, precision=HIGH)))
    keys = row_cache[:, 0].reshape(seq_len, KV, HEAD)
    values = row_cache[:, 1].reshape(seq_len, KV, HEAD)
    block = 512 if seq_len % 512 == 0 else seq_len
    blocks_count = seq_len // block
    blocks = query.reshape(blocks_count, block, KV, GROUP, HEAD)
    starts = jnp.arange(blocks_count, dtype=jnp.int32) * block

    def one_block(item):
        return attend_block(item[0], item[1], keys, values, length)
    mixed = lax.map(jax.checkpoint(one_block), (blocks, starts)).reshape(seq_len, HEADS * HEAD)
    mixed_low = low(low_back(mixed))
    branch = low_back(jnp.dot(mixed_low, output_weight, precision=HIGH))
    middle = row_in + branch
    normed_two = low(norm_rows(middle, gains[1]))
    gate = low_back(jnp.dot(normed_two, ffn_weight[:, 0].T, precision=HIGH))
    upper = low_back(jnp.dot(normed_two, ffn_weight[:, 1].T, precision=HIGH))
    hidden = low(jax.nn.silu(gate) * upper)
    ffn_out = low_back(jnp.dot(hidden, down_weight, precision=HIGH))
    live = (jnp.arange(seq_len, dtype=jnp.int32) < length).astype(row_in.dtype)
    return live[:, None] * (middle + ffn_out)

def reference(tokens, kv_cache, lengths, norm_gains, query_weight, output_weight, ffn_in_weight, down_weight, cotangent):

    def forward(token_vals, cache_vals, gains, weight_query, weight_output, weight_ffn, weight_down):

        def step(carry, item):
            row_in, row_cache, length = item
            result = jax.checkpoint(layer_row)(row_in, row_cache, length, gains, weight_query, weight_output, weight_ffn, weight_down)
            return (carry, result)
        unused, outputs = lax.scan(step, jnp.zeros((), jnp.float32), (token_vals, cache_vals, lengths))
        return outputs
    result, pullback = jax.vjp(forward, tokens.astype(jnp.float32), kv_cache.astype(jnp.float32), norm_gains, query_weight.astype(jnp.float32), output_weight.astype(jnp.float32), ffn_in_weight.astype(jnp.float32), down_weight.astype(jnp.float32))
    grads = pullback(cotangent.astype(jnp.float32))
    return (result.astype(jnp.bfloat16), grads[0], grads[1], grads[2], grads[3], grads[4], grads[5], grads[6])
```

```python
import jax
import jax.numpy as jnp
from jax import lax
from jax.sharding import PartitionSpec as P

HEADS = 16
HEAD = 128
KV = 4
GROUP = 4
EPS = 1e-05
NEG = -1e30
F32 = jnp.float32
BF16 = jnp.bfloat16


def dot(left, right, dims):
    return lax.dot_general(left, right, (dims, ((), ())), preferred_element_type=F32)


def tie(value, dep):
    if dep is None:
        return value
    return lax.optimization_barrier((value, dep))[0]


def norm_back(grad_normed, scaled, inverse, gain):
    inner = grad_normed * gain
    return inverse * (inner - scaled * jnp.mean(inner * scaled, axis=-1, keepdims=True))


def swap_core(value, seq):
    return lax.ppermute(value, "seq", [(s, s ^ 1) for s in range(seq)])


def ring(value, chips):
    pairs = [(2 * z + c, 2 * ((z + 1) % chips) + c) for z in range(chips) for c in range(2)]
    return lax.ppermute(value, "seq", pairs)


def swap_row(value, rows, mask):
    return lax.ppermute(value, "rows", [(r, r ^ mask) for r in range(rows)])


def ring_gather(own, chips, dep=None):
    got = [tie(own, dep)]
    for _ in range(1, chips):
        got.append(ring(got[-1], chips))
    return [own] + got[:0:-1], got[-2]


def ring_scatter(parts, chips, dep=None):
    moving = ring(tie(parts[chips - 1], dep), chips)
    for j in range(chips - 2, -1, -1):
        total = moving.astype(F32) + parts[j].astype(F32)
        if j:
            moving = ring(total.astype(BF16), chips)
    return total


def xor_order(value, at):
    shape = value.shape
    value = value.reshape(2, 2, *shape[1:])
    value = jnp.where(at % 2 == 1, value[:, ::-1], value)
    return jnp.where(at // 2 == 1, value[::-1], value).reshape(shape)


def own_order(value, chips, place, core):
    count = value.shape[0]
    value = value.reshape(count, chips, 2, -1)
    value = jnp.where(core == 0, value, value[:, :, ::-1])
    value = jnp.concatenate([value, value], axis=1)
    value = lax.dynamic_slice_in_dim(value, place, chips, axis=1)
    return value.transpose(0, 2, 1, 3).reshape(count, -1)


def index_order(value, chips, place, core):
    count = value.shape[0]
    value = value.reshape(count, 2, chips, -1).transpose(0, 2, 1, 3)
    value = jnp.concatenate([value, value], axis=1)
    value = lax.dynamic_slice_in_dim(value, (chips - place) % chips, chips, axis=1)
    value = jnp.where(core == 0, value, value[:, :, ::-1])
    return value.reshape(count, -1)


class Weight:
    def __init__(self, shard, chips, rows, row_at, order, dep=None):
        seq = 2 * chips
        self.chips, self.row_at, self.order = chips, row_at, order
        depth, width = shard.shape
        self.depth = depth
        self.split = rows == 4 and depth % 32 == 0 and width % 512 == 0
        if not self.split:
            self.whole = lax.all_gather(shard, "seq", axis=0, tiled=True)
            self.token = dep
            return
        part = width // rows
        half = depth // 2
        mine = lax.dynamic_slice_in_dim(shard, row_at * part, part, axis=1)
        slots, self.token = ring_gather(mine, chips, dep=dep)
        first = jnp.stack([v[:half] for v in slots[1:]])
        second = jnp.stack([v[half:] for v in slots[1:]])
        first_x = swap_row(first, rows, 1)
        second_y = swap_row(second, rows, 2)
        first_pair = swap_row(jnp.stack([first, first_x]), rows, 2)
        second_pair = swap_row(jnp.stack([second, second_y]), rows, 1)
        parts = jnp.stack(
            [
                jnp.stack([first, first_x, first_pair[0], first_pair[1]]),
                jnp.stack([second, second_pair[0], second_y, second_pair[1]]),
            ],
            axis=2,
        )
        parts = parts.reshape(rows, (chips - 1) * depth, part)
        self.far = [parts, swap_core(parts, seq)]
        self.near = [shard, swap_core(shard, seq)]

    def features(self, value):
        if not self.split:
            return own_order(dot(value, self.whole, ((1,), (1,))), *self.order)
        count = value.shape[0]
        blocks = value.reshape(count, 4, -1).transpose(1, 0, 2)
        blocks = xor_order(blocks, self.row_at)
        out = []
        for near, far in zip(self.near, self.far, strict=True):
            out.append(dot(value, near, ((1,), (1,))))
            term = jnp.einsum("ktc,kfc->ktf", blocks, far, preferred_element_type=F32)
            out.append(jnp.sum(term, axis=0))
        return jnp.concatenate(out, axis=1)

    def back(self, value):
        if not self.split:
            return dot(index_order(value, *self.order), self.whole, ((1,), (0,)))
        count = value.shape[0]
        half = value.shape[1] // 2
        near_sum = far_sum = 0.0
        for i in range(2):
            part = value[:, i * half : (i + 1) * half]
            near_sum += dot(part[:, : self.depth], self.near[i], ((1,), (0,)))
            far_sum += jnp.einsum(
                "tf,kfc->ktc", part[:, self.depth :], self.far[i], preferred_element_type=F32
            )
        far_sum = xor_order(far_sum, self.row_at).transpose(1, 0, 2).reshape(count, -1)
        return near_sum + far_sum


def gather_tokens(own, chips, dep=None):
    slots, token = ring_gather(own, chips, dep=dep)
    block = jnp.concatenate(slots, axis=0)
    return jnp.concatenate([block, swap_core(block, 2 * chips)], axis=0), token


def scatter_tokens(part, chips, dep=None):
    half = part.shape[0] // 2
    block = part[:half].astype(F32) + swap_core(part[half:], 2 * chips).astype(F32)
    block = block.astype(BF16)
    size = half // chips
    return ring_scatter([block[j * size : (j + 1) * size] for j in range(chips)], chips, dep=dep)


def sum_rows(value, rows):
    if rows != 4:
        return lax.psum(value.astype(BF16), "rows").astype(F32)
    half = value.shape[0] // 2
    first, second = value[:half].astype(BF16), value[half:].astype(BF16)

    def pair(item, mask):
        return item.astype(F32) + swap_row(item, rows, mask).astype(F32)

    first, second = pair(first, 1).astype(BF16), pair(second, 2).astype(BF16)
    return jnp.concatenate([pair(first, 2), pair(second, 1)], axis=0)


def sum_all(value, rows, seq):
    mask = 1
    while mask < seq:
        value = value + lax.ppermute(value, "seq", [(s, s ^ mask) for s in range(seq)])
        mask *= 2
    mask = 1
    while mask < rows:
        value = value + swap_row(value, rows, mask)
        mask *= 2
    return value


def local(
    tokens,
    kv_cache,
    lengths,
    norm_gains,
    query_weight,
    output_weight,
    ffn_in_weight,
    down_weight,
    cotangent,
):
    rows_here, seg_len, width = tokens.shape
    seq = lax.axis_size("seq")
    rows = lax.axis_size("rows")
    chips = seq // 2
    seq_at = lax.axis_index("seq")
    row_at = lax.axis_index("rows")
    place, core = seq_at // 2, seq_at % 2
    full_len = seg_len * seq
    units = down_weight.shape[0]
    scale = HEAD ** (-0.5)
    gain_one, gain_two = norm_gains[0], norm_gains[1]
    positions = jnp.arange(seg_len, dtype=jnp.int32)
    query_pos = seq_at * seg_len + positions
    chip_order = (place + jnp.arange(chips, dtype=jnp.int32)) % chips
    core_order = jnp.stack([core, 1 - core])
    key_pos = (
        (chip_order[None, :, None] * 2 + core_order[:, None, None]) * seg_len
        + positions[None, None, :]
    ).reshape(full_len)

    order = (chips, place, core)
    query_proj = Weight(query_weight, chips, rows, row_at, order)
    output_proj = Weight(output_weight, chips, rows, row_at, order, dep=query_proj.token)
    token = output_proj.token
    cache_own = jnp.stack([kv_cache[:, :, 0], kv_cache[:, :, 1]])
    cache_slots, token = ring_gather(cache_own, chips, dep=token)
    cache_block = jnp.stack(cache_slots)
    cache_all = jnp.stack([cache_block, swap_core(cache_block, seq)])

    live = [
        (query_pos < lengths[r]).astype(F32).reshape(seg_len, 1) for r in range(rows_here)
    ]
    grad_out = [cotangent[r].astype(F32) * live[r] for r in range(rows_here)]
    grad_group = [None] * rows_here
    grad_group[0], token = gather_tokens(grad_out[0].astype(BF16), chips, dep=token)

    inputs = [tokens[r].astype(F32) for r in range(rows_here)]
    inverse_one = [
        lax.rsqrt(jnp.mean(v * v, axis=-1, keepdims=True) + EPS) for v in inputs
    ]
    normed_one = [
        (v * i * gain_one).astype(BF16) for v, i in zip(inputs, inverse_one, strict=True)
    ]
    gate_up_weight = jnp.concatenate([ffn_in_weight[:, 0], ffn_in_weight[:, 1]], axis=0)
    normed_all = jnp.concatenate(normed_one, axis=0)
    query = index_order(query_proj.features(normed_all).astype(BF16), *order)

    def to_heads(value):
        value = value.reshape(seg_len, KV, GROUP, HEAD).transpose(1, 2, 0, 3)
        return value.reshape(KV, GROUP * seg_len, HEAD)

    def from_heads(value):
        value = value.reshape(KV, GROUP, seg_len, HEAD).transpose(2, 0, 1, 3)
        return value.reshape(seg_len, HEADS * HEAD)

    query_heads, keys, values, valid = [], [], [], []
    mixed_heads, lse, mixed_low, middle, inverse_two, normed_two = [], [], [], [], [], []
    for r in range(rows_here):
        query_heads.append(to_heads(query[r * seg_len : (r + 1) * seg_len]))
        keys.append(cache_all[:, :, 0, r].reshape(full_len, KV, HEAD))
        values.append(cache_all[:, :, 1, r].reshape(full_len, KV, HEAD))
        limit = jnp.minimum(query_pos, lengths[r] - 1)
        limit = jnp.broadcast_to(limit[None], (GROUP, seg_len)).reshape(GROUP * seg_len)
        valid.append((key_pos[None, :] <= limit[:, None])[None])
        scores = (
            jnp.einsum("kqd,rkd->kqr", query_heads[r], keys[r], preferred_element_type=F32)
            * scale
        )
        scores = jnp.where(valid[r], scores, NEG)
        best = jnp.max(scores, axis=-1)
        weights = jnp.exp(scores - best[..., None])
        total = jnp.sum(weights, axis=-1)
        accum = jnp.einsum(
            "kqr,rkd->kqd", weights.astype(BF16), values[r], preferred_element_type=F32
        )
        mixed_heads.append(accum / total[..., None])
        lse.append(best + jnp.log(total))
        mixed_low.append(own_order(from_heads(mixed_heads[r]).astype(BF16), *order))
        middle.append(inputs[r] + output_proj.back(mixed_low[r]))
        inverse_two.append(
            lax.rsqrt(jnp.mean(middle[r] * middle[r], axis=-1, keepdims=True) + EPS)
        )
        normed_two.append((middle[r] * inverse_two[r] * gain_two).astype(BF16))

    normed_group, hidden, grad_gate_up, ffn_part, grad_part = [], [], [], [], []
    for r in range(rows_here):
        group, token = gather_tokens(normed_two[r], chips, dep=token)
        normed_group.append(group)
        if r > 0:
            grad_group[r], token = gather_tokens(
                grad_out[r].astype(BF16), chips, dep=token
            )
    for r in range(rows_here):
        kept = dot(normed_group[r], gate_up_weight, ((1,), (1,)))
        gate, upper = kept[:, :units], kept[:, units:]
        sigma = jax.nn.sigmoid(gate)
        grad_hidden = dot(grad_group[r], down_weight, ((1,), (1,)))
        hidden.append((gate * sigma * upper).astype(BF16))
        grad_gate = grad_hidden * upper * sigma * (1.0 + gate * (1.0 - sigma))
        grad_up = grad_hidden * gate * sigma
        grad_gate_up.append(jnp.concatenate([grad_gate, grad_up], axis=1).astype(BF16))
        grad_part.append(dot(grad_gate_up[r], gate_up_weight, ((1,), (0,))).astype(BF16))
        ffn_part.append(dot(hidden[r], down_weight, ((1,), (0,))).astype(BF16))

    down_part = sum(
        dot(hidden[r], grad_group[r], ((0,), (0,))) for r in range(rows_here)
    ).astype(BF16)
    in_part = sum(
        dot(grad_gate_up[r], normed_group[r], ((0,), (0,))) for r in range(rows_here)
    ).astype(BF16)
    down_grad, in_grad = lax.psum((down_part, in_part), "rows")

    grad_middle, gain_two_terms, grad_branch = [], [], []
    query_terms, cache_terms = [], []
    for r in range(rows_here):
        grad_normed_two = scatter_tokens(grad_part[r], chips)
        scaled_two = middle[r] * inverse_two[r]
        gain_two_terms.append(jnp.sum(grad_normed_two * scaled_two, axis=0))
        grad_middle.append(
            grad_out[r] + norm_back(grad_normed_two, scaled_two, inverse_two[r], gain_two)
        )
        grad_branch.append(grad_middle[r].astype(BF16))
        grad_mixed = output_proj.features(grad_branch[r]).astype(BF16)
        grad_heads = to_heads(index_order(grad_mixed, *order))
        delta = jnp.sum(grad_heads.astype(F32) * mixed_heads[r], axis=-1)
        scores = (
            jnp.einsum("kqd,rkd->kqr", query_heads[r], keys[r], preferred_element_type=F32)
            * scale
        )
        probs = jnp.where(valid[r], jnp.exp(scores - lse[r][..., None]), 0.0)
        grad_probs = jnp.einsum(
            "kqd,rkd->kqr", grad_heads, values[r], preferred_element_type=F32
        )
        grad_scores = (probs * (grad_probs - delta[..., None])).astype(BF16)
        grad_query = (
            jnp.einsum("kqr,rkd->kqd", grad_scores, keys[r], preferred_element_type=F32)
            * scale
        )
        grad_keys = (
            jnp.einsum("kqr,kqd->rkd", grad_scores, query_heads[r], preferred_element_type=F32)
            * scale
        )
        grad_values = jnp.einsum(
            "kqr,kqd->rkd", probs.astype(BF16), grad_heads, preferred_element_type=F32
        )
        query_terms.append(own_order(from_heads(grad_query).astype(BF16), *order))
        cache_terms.append(
            jnp.stack([grad_keys, grad_values]).astype(BF16).reshape(2, 2, chips, seg_len, KV * HEAD)
        )

    layer_out = []
    for r in range(rows_here):
        ffn_out = scatter_tokens(ffn_part[r], chips)
        layer_out.append((live[r] * (middle[r] + ffn_out)).astype(BF16))

    branch_all = jnp.concatenate(grad_branch, axis=0)
    query_term = jnp.concatenate(query_terms, axis=0)
    output_part = dot(
        jnp.concatenate(mixed_low, axis=0), branch_all, ((0,), (0,))
    ).astype(BF16)
    output_grad = sum_rows(scatter_tokens(output_part, chips), rows)

    cache_part = jnp.stack(cache_terms, axis=3)
    cache_sum = cache_part[:, 0].astype(F32) + swap_core(cache_part[:, 1], seq).astype(F32)
    cache_sum = cache_sum.astype(BF16)
    cache_grad = ring_scatter([cache_sum[:, j] for j in range(chips)], chips)
    cache_grad = jnp.stack([cache_grad[0], cache_grad[1]], axis=2)

    query_part = dot(query_term, normed_all, ((0,), (0,))).astype(BF16)
    query_grad = sum_rows(scatter_tokens(query_part, chips), rows)
    grad_normed_one = query_proj.back(query_term)
    gain_one_terms, input_grad = [], []
    for r in range(rows_here):
        grad_r = grad_normed_one[r * seg_len : (r + 1) * seg_len]
        scaled_one = inputs[r] * inverse_one[r]
        gain_one_terms.append(jnp.sum(grad_r * scaled_one, axis=0))
        input_grad.append(
            grad_middle[r] + norm_back(grad_r, scaled_one, inverse_one[r], gain_one)
        )
    gain_grad = sum_all(jnp.stack([sum(gain_one_terms), sum(gain_two_terms)]), rows, seq)
    return (
        jnp.stack(layer_out),
        jnp.stack(input_grad),
        cache_grad,
        gain_grad,
        query_grad,
        output_grad,
        jnp.stack([in_grad[:units], in_grad[units:]], axis=1).astype(F32),
        down_grad.astype(F32),
    )


def solution(mesh):
    in_specs = (
        P("rows", "seq", None),
        P("rows", "seq", None, None),
        P("rows"),
        P(),
        P("seq", None),
        P("seq", None),
        P("seq", None, None),
        P("seq", None),
        P("rows", "seq", None),
    )
    out_specs = (
        P("rows", "seq", None),
        P("rows", "seq", None),
        P("rows", "seq", None, None),
        P(),
        P("seq", None),
        P("seq", None),
        P("seq", None, None),
        P("seq", None),
    )
    return jax.shard_map(local, mesh=mesh, in_specs=in_specs, out_specs=out_specs, check_vma=False)
```

```python
import jax
import jax.numpy as jnp
from jax import lax
from jax.experimental import pallas as pl
from jax.experimental.pallas import tpu as pltpu
from jax.sharding import PartitionSpec as P

HEADS = 16
HEAD = 128
KV = 4
GROUP = 4


EPS = 1e-05
NEG = -1e30


def dot_trans(left, right):
    return lax.dot_general(
        left, right, (((1,), (1,)), ((), ())), preferred_element_type=jnp.float32
    )


def norm_back(grad_normed, scaled, inverse, gain):
    inner = grad_normed * gain
    return inverse * (inner - scaled * jnp.mean(inner * scaled, axis=-1, keepdims=True))


def swiglu_back(gate_up, grad_hidden):
    gate = gate_up[:, 0]
    upper = gate_up[:, 1]
    sigma = jax.nn.sigmoid(gate)
    grad_gate = grad_hidden * upper * sigma * (1.0 + gate * (1.0 - sigma))
    grad_up = grad_hidden * gate * sigma
    return jnp.stack([grad_gate, grad_up], axis=1).astype(jnp.bfloat16)


def widen_pairs(part):
    units, width = part.shape[0] // 2, part.shape[1]
    block = min(units, 128)

    def kernel(gate_ref, up_ref, out_ref):
        out_ref[:, 0] = gate_ref[...].astype(jnp.float32)
        out_ref[:, 1] = up_ref[...].astype(jnp.float32)

    steps = units // block
    return pl.pallas_call(
        kernel,
        out_shape=jax.ShapeDtypeStruct((units, 2, width), jnp.float32),
        grid=(steps,),
        in_specs=[
            pl.BlockSpec((block, width), lambda i: (i, 0)),
            pl.BlockSpec((block, width), lambda i: (i + steps, 0)),
        ],
        out_specs=pl.BlockSpec((block, 2, width), lambda i: (i, 0, 0)),
        compiler_params=pltpu.CompilerParams(vmem_limit_bytes=32 * 2**20),
        cost_estimate=pl.CostEstimate(
            flops=0, bytes_accessed=12 * units * width, transcendentals=0
        ),
    )(part, part)


def sum_rows(value, rows):
    if rows != 4:
        return lax.psum(value.astype(BF16), "rows").astype(jnp.float32)
    half = value.shape[0] // 2
    first, second = value[:half].astype(BF16), value[half:].astype(BF16)

    def pair(item, mask):
        return item.astype(jnp.float32) + swap_row(item, rows, mask).astype(jnp.float32)

    first, second = pair(first, 1).astype(BF16), pair(second, 2).astype(BF16)
    return jnp.concatenate([pair(first, 2), pair(second, 1)], axis=0)


def sum_all(value, rows, seq):
    mask = 1
    while mask < seq:
        value = value + lax.ppermute(value, "seq", [(s, s ^ mask) for s in range(seq)])
        mask *= 2
    mask = 1
    while mask < rows:
        value = value + swap_row(value, rows, mask)
        mask *= 2
    return value


def local(
    tokens,
    kv_cache,
    lengths,
    norm_gains,
    query_weight,
    output_weight,
    ffn_in_weight,
    down_weight,
    cotangent,
):
    rows_here, seg_len, width = tokens.shape
    seq_count = lax.axis_size("seq")
    tok_count = rows_here * seg_len
    full_len = seg_len * seq_count
    feat_count = HEADS * HEAD
    scale = HEAD ** (-0.5)
    query_pos = lax.axis_index("seq") * seg_len + jnp.arange(seg_len, dtype=jnp.int32)
    limit = jnp.minimum(query_pos[None, :], lengths[:, None] - 1)
    live_rows = (query_pos[None, :] < lengths[:, None]).astype(jnp.float32).reshape(tok_count, 1)
    query_limit = jnp.broadcast_to(limit[:, None, :], (rows_here, GROUP, seg_len)).reshape(
        rows_here, GROUP * seg_len
    )
    inputs = tokens.astype(jnp.float32).reshape(tok_count, width)
    gain_one = norm_gains[0]
    gain_two = norm_gains[1]
    inverse_one = lax.rsqrt(jnp.mean(inputs * inputs, axis=-1, keepdims=True) + EPS)
    normed_one = (inputs * inverse_one * gain_one).astype(jnp.bfloat16)
    query_all, output_all = (
        lax.all_gather(query_weight, "seq", axis=0, tiled=True),
        lax.all_gather(output_weight, "seq", axis=0, tiled=True),
    )
    query_low = dot_trans(normed_one, query_all).astype(jnp.bfloat16)
    query_heads = query_low.reshape(rows_here, seg_len, KV, GROUP, HEAD).transpose(0, 2, 3, 1, 4)
    query_heads = query_heads.reshape(rows_here, KV, GROUP * seg_len, HEAD)
    start_best = jnp.full((rows_here, KV, GROUP * seg_len), NEG, jnp.float32)
    start_total = jnp.zeros((rows_here, KV, GROUP * seg_len), jnp.float32)
    start_accum = jnp.zeros((rows_here, KV, GROUP * seg_len, HEAD), jnp.float32)
    piece = lax.all_gather(kv_cache, "seq", axis=1, tiled=True)
    count = piece.shape[1]
    key_pos = jnp.arange(count, dtype=jnp.int32)
    keys = piece[:, :, 0].reshape(rows_here, count, KV, HEAD)
    values = piece[:, :, 1].reshape(rows_here, count, KV, HEAD)

    def one_row(item):
        query_row, key_row, value_row, limit_row, best_row, total_row, accum_row = item
        scores = (
            jnp.einsum("kqd,rkd->kqr", query_row, key_row, preferred_element_type=jnp.float32)
            * scale
        )
        scores = jnp.where(key_pos[None, None, :] <= limit_row[None, :, None], scores, NEG)
        best_new = jnp.maximum(best_row, jnp.max(scores, axis=-1))
        factor = jnp.exp(best_row - best_new)
        weights = jnp.exp(scores - best_new[..., None])
        total_new = total_row * factor + jnp.sum(weights, axis=-1)
        accum_new = accum_row * factor[..., None] + jnp.einsum(
            "kqr,rkd->kqd",
            weights.astype(jnp.bfloat16),
            value_row,
            preferred_element_type=jnp.float32,
        )
        return (best_new, total_new, accum_new)

    best, total, accum = lax.map(
        one_row, (query_heads, keys, values, query_limit, start_best, start_total, start_accum)
    )
    mixed_heads = accum / total[..., None]
    log_total = best + jnp.log(total)
    mixed_low = mixed_heads.reshape(rows_here, KV, GROUP, seg_len, HEAD).transpose(0, 3, 1, 2, 4)
    mixed_low = mixed_low.reshape(tok_count, feat_count).astype(jnp.bfloat16)
    middle = inputs + jnp.dot(mixed_low, output_all, preferred_element_type=jnp.float32)
    inverse_two = lax.rsqrt(jnp.mean(middle * middle, axis=-1, keepdims=True) + EPS)
    normed_two = (middle * inverse_two * gain_two).astype(jnp.bfloat16)
    grad_out = cotangent.astype(jnp.float32).reshape(tok_count, width) * live_rows
    grad_low = grad_out.astype(jnp.bfloat16)
    normed_group = lax.all_gather(normed_two, "seq", axis=0, tiled=True)
    kept = jnp.einsum(
        "td,nkd->tkn", normed_group, ffn_in_weight, preferred_element_type=jnp.float32
    )
    hidden_group = (jax.nn.silu(kept[:, 0]) * kept[:, 1]).astype(jnp.bfloat16)
    ffn_out = lax.psum_scatter(
        jnp.dot(hidden_group, down_weight, preferred_element_type=jnp.float32).astype(jnp.bfloat16),
        "seq",
        scatter_dimension=0,
        tiled=True,
    ).astype(jnp.float32)
    grad_group = lax.all_gather(grad_low, "seq", axis=0, tiled=True)
    grad_gate_up = swiglu_back(kept, dot_trans(grad_group, down_weight))
    grad_normed_two = lax.psum_scatter(
        jnp.einsum(
            "tkn,nkd->td", grad_gate_up, ffn_in_weight, preferred_element_type=jnp.float32
        ).astype(jnp.bfloat16),
        "seq",
        scatter_dimension=0,
        tiled=True,
    ).astype(jnp.float32)
    in_grad = jnp.einsum(
        "tkn,td->nkd", grad_gate_up, normed_group, preferred_element_type=jnp.float32
    )
    down_part = jnp.einsum(
        "tn,td->nd", hidden_group, grad_group, preferred_element_type=jnp.float32
    )
    layer_out = (
        (live_rows * (middle + ffn_out)).astype(jnp.bfloat16).reshape(rows_here, seg_len, width)
    )
    scaled_two = middle * inverse_two
    gain_two_grad = jnp.sum(grad_normed_two * scaled_two, axis=0)
    grad_middle = grad_out + norm_back(grad_normed_two, scaled_two, inverse_two, gain_two)
    grad_branch = grad_middle.astype(jnp.bfloat16)
    grad_mixed = dot_trans(grad_branch, output_all).astype(jnp.bfloat16)
    grad_heads = grad_mixed.reshape(rows_here, seg_len, KV, GROUP, HEAD).transpose(0, 2, 3, 1, 4)
    grad_heads = grad_heads.reshape(rows_here, KV, GROUP * seg_len, HEAD)
    delta = jnp.sum(grad_heads.astype(jnp.float32) * mixed_heads, axis=-1)
    cache_full = lax.all_gather(kv_cache, "seq", axis=1, tiled=True)
    key_all = jnp.arange(full_len, dtype=jnp.int32)

    def row_back(item):
        query_row, grad_row, delta_row, lse_row, limit_row, cache_row = item
        keys = cache_row[:, 0].reshape(full_len, KV, HEAD)
        values = cache_row[:, 1].reshape(full_len, KV, HEAD)
        scores = (
            jnp.einsum("kqd,rkd->kqr", query_row, keys, preferred_element_type=jnp.float32) * scale
        )
        valid = key_all[None, None, :] <= limit_row[None, :, None]
        probs = jnp.where(valid, jnp.exp(scores - lse_row[..., None]), 0.0)
        grad_probs = jnp.einsum(
            "kqd,rkd->kqr", grad_row, values, preferred_element_type=jnp.float32
        )
        grad_scores = (probs * (grad_probs - delta_row[..., None])).astype(jnp.bfloat16)
        grad_query = (
            jnp.einsum("kqr,rkd->kqd", grad_scores, keys, preferred_element_type=jnp.float32)
            * scale
        )
        grad_keys = (
            jnp.einsum("kqr,kqd->rkd", grad_scores, query_row, preferred_element_type=jnp.float32)
            * scale
        )
        grad_values = jnp.einsum(
            "kqr,kqd->rkd", probs.astype(jnp.bfloat16), grad_row, preferred_element_type=jnp.float32
        )
        return (
            grad_query,
            jnp.stack(
                [grad_keys.reshape(full_len, KV * HEAD), grad_values.reshape(full_len, KV * HEAD)],
                axis=1,
            ),
        )

    grad_query_heads, cache_terms = lax.map(
        row_back, (query_heads, grad_heads, delta, log_total, query_limit, cache_full)
    )
    cache_grad = lax.psum_scatter(
        cache_terms.astype(jnp.bfloat16), "seq", scatter_dimension=1, tiled=True
    ).astype(jnp.float32)
    grad_query = grad_query_heads.reshape(rows_here, KV, GROUP, seg_len, HEAD).transpose(
        0, 3, 1, 2, 4
    )
    grad_query = grad_query.reshape(tok_count, feat_count).astype(jnp.bfloat16)
    grad_normed_one = jnp.dot(grad_query, query_all, preferred_element_type=jnp.float32)
    query_grad_rows = jnp.einsum(
        "tn,td->nd", grad_query, normed_one, preferred_element_type=jnp.float32
    )
    output_grad_rows = jnp.einsum(
        "tn,td->nd", mixed_low, grad_branch, preferred_element_type=jnp.float32
    )
    attn_grad = lax.psum_scatter(
        jnp.stack([query_grad_rows, output_grad_rows], axis=1).astype(jnp.bfloat16),
        "seq",
        scatter_dimension=0,
        tiled=True,
    ).astype(jnp.float32)
    scaled_one = inputs * inverse_one
    gain_one_grad = jnp.sum(grad_normed_one * scaled_one, axis=0)
    input_grad = grad_middle + norm_back(grad_normed_one, scaled_one, inverse_one, gain_one)
    gain_grad = lax.psum(jnp.stack([gain_one_grad, gain_two_grad]), ("rows", "seq"))
    query_grad, output_grad, ffn_in_grad, down_grad = (
        lax.psum(attn_grad[:, 0].astype(jnp.bfloat16), "rows").astype(jnp.float32),
        lax.psum(attn_grad[:, 1].astype(jnp.bfloat16), "rows").astype(jnp.float32),
        widen_pairs(lax.psum(in_grad.astype(jnp.bfloat16).transpose(1, 0, 2).reshape(-1, width), "rows")),
        lax.psum(down_part.astype(jnp.bfloat16), "rows").astype(jnp.float32),
    )
    return (
        layer_out,
        input_grad.reshape(rows_here, seg_len, width),
        cache_grad,
        gain_grad,
        query_grad,
        output_grad,
        ffn_in_grad,
        down_grad,
    )


def solution(mesh):
    in_specs = (
        P("rows", "seq", None),
        P("rows", "seq", None, None),
        P("rows"),
        P(),
        P("seq", None),
        P("seq", None),
        P("seq", None, None),
        P("seq", None),
        P("rows", "seq", None),
    )
    out_specs = (
        P("rows", "seq", None),
        P("rows", "seq", None),
        P("rows", "seq", None, None),
        P(),
        P("seq", None),
        P("seq", None),
        P("seq", None, None),
        P("seq", None),
    )
    return jax.shard_map(local, mesh=mesh, in_specs=in_specs, out_specs=out_specs, check_vma=False)
```

```python
import jax
import jax.numpy as jnp
from jax import lax
from jax.sharding import PartitionSpec as P

HEADS = 16
HEAD = 128
KV = 4
GROUP = 4
EPS = 1e-05
NEG = -1e30
F32 = jnp.float32
BF16 = jnp.bfloat16


def dot(left, right, dims):
    return lax.dot_general(left, right, (dims, ((), ())), preferred_element_type=F32)


def tie(value, dep):
    if dep is None:
        return value
    return lax.optimization_barrier((value, dep))[0]


def norm_back(grad_normed, scaled, inverse, gain):
    inner = grad_normed * gain
    return inverse * (inner - scaled * jnp.mean(inner * scaled, axis=-1, keepdims=True))


def swap_core(value, seq):
    return lax.ppermute(value, "seq", [(s, s ^ 1) for s in range(seq)])


def ring(value, chips):
    pairs = [(2 * z + c, 2 * ((z + 1) % chips) + c) for z in range(chips) for c in range(2)]
    return lax.ppermute(value, "seq", pairs)


def swap_row(value, rows, mask):
    return lax.ppermute(value, "rows", [(r, r ^ mask) for r in range(rows)])


def ring_gather(own, chips, dep=None):
    got = [tie(own, dep)]
    for _ in range(1, chips):
        got.append(ring(got[-1], chips))
    return [own] + got[:0:-1], got[-2]


def ring_scatter(parts, chips):
    sent = parts[chips - 1]
    for j in range(chips - 2, -1, -1):
        yield sent
        total = ring(sent, chips).astype(F32) + parts[j].astype(F32)
        sent = total.astype(BF16)
    return total


class Lane:
    def __init__(self):
        self.waiting, self.results, self.sent = [], {}, None

    def add(self, name, steps):
        self.waiting.append((name, steps))

    def step(self):
        if self.waiting:
            name, steps = self.waiting[0]
            try:
                sent = next(steps)
                self.sent = sent
                return sent
            except StopIteration as end:
                self.results[name] = end.value
                self.waiting.pop(0)
                return self.step()
        return None

    def result(self, name):
        while name not in self.results:
            self.step()
        return self.results[name]


def beside(value, *lanes):
    for lane in lanes:
        value = tie(value, lane.step())
    return value


def xor_order(value, at):
    shape = value.shape
    value = value.reshape(2, 2, *shape[1:])
    value = jnp.where(at % 2 == 1, value[:, ::-1], value)
    return jnp.where(at // 2 == 1, value[::-1], value).reshape(shape)


def own_order(value, chips, place, core):
    count = value.shape[0]
    value = value.reshape(count, chips, 2, -1)
    value = jnp.where(core == 0, value, value[:, :, ::-1])
    value = jnp.concatenate([value, value], axis=1)
    value = lax.dynamic_slice_in_dim(value, place, chips, axis=1)
    return value.transpose(0, 2, 1, 3).reshape(count, -1)


def index_order(value, chips, place, core):
    count = value.shape[0]
    value = value.reshape(count, 2, chips, -1).transpose(0, 2, 1, 3)
    value = jnp.concatenate([value, value], axis=1)
    value = lax.dynamic_slice_in_dim(value, (chips - place) % chips, chips, axis=1)
    value = jnp.where(core == 0, value, value[:, :, ::-1])
    return value.reshape(count, -1)


class Weight:
    def __init__(self, shard, chips, rows, row_at, order, dep=None):
        seq = 2 * chips
        self.chips, self.row_at, self.order = chips, row_at, order
        depth, width = shard.shape
        self.depth = depth
        self.split = rows == 4 and depth % 32 == 0 and width % 512 == 0
        if not self.split:
            self.whole = lax.all_gather(shard, "seq", axis=0, tiled=True)
            self.token = dep
            return
        part = width // rows
        half = depth // 2
        mine = lax.dynamic_slice_in_dim(shard, row_at * part, part, axis=1)
        slots, self.token = ring_gather(mine, chips, dep=dep)
        first = jnp.stack([v[:half] for v in slots[1:]])
        second = jnp.stack([v[half:] for v in slots[1:]])
        first_x = swap_row(first, rows, 1)
        second_y = swap_row(second, rows, 2)
        first_pair = swap_row(jnp.stack([first, first_x]), rows, 2)
        second_pair = swap_row(jnp.stack([second, second_y]), rows, 1)
        parts = jnp.stack(
            [
                jnp.stack([first, first_x, first_pair[0], first_pair[1]]),
                jnp.stack([second, second_pair[0], second_y, second_pair[1]]),
            ],
            axis=2,
        )
        parts = parts.reshape(rows, (chips - 1) * depth, part)
        self.far = [parts, swap_core(parts, seq)]
        self.near = [shard, swap_core(shard, seq)]

    def features(self, value):
        if not self.split:
            out = own_order(dot(value, self.whole, ((1,), (1,))), *self.order)
            half = out.shape[1] // 2
            return [out[:, :half].astype(BF16), out[:, half:].astype(BF16)]
        count = value.shape[0]
        blocks = value.reshape(count, 4, -1).transpose(1, 0, 2)
        blocks = xor_order(blocks, self.row_at)
        out = []
        for near, far in zip(self.near, self.far, strict=True):
            term = jnp.einsum("ktc,kfc->ktf", blocks, far, preferred_element_type=F32)
            term = jnp.sum(term, axis=0).astype(BF16)
            out.append(jnp.concatenate([dot(value, near, ((1,), (1,))).astype(BF16), term], axis=1))
        return out

    def back(self, halves):
        if not self.split:
            value = jnp.concatenate(halves, axis=1)
            return dot(index_order(value, *self.order), self.whole, ((1,), (0,)))
        count = halves[0].shape[0]
        near_sum = far_sum = 0.0
        for part, near, far in zip(halves, self.near, self.far, strict=True):
            near_sum += dot(part[:, : self.depth], near, ((1,), (0,)))
            far_sum += jnp.einsum(
                "tf,kfc->ktc", part[:, self.depth :], far, preferred_element_type=F32
            )
        far_sum = xor_order(far_sum, self.row_at).transpose(1, 0, 2).reshape(count, -1)
        return near_sum + far_sum


def scatter_halves(own, sib, got_at, chips):
    got = swap_core(sib, 2 * chips)
    parts = [own(j).astype(F32) + got_at(got, j).astype(F32) for j in range(chips)]
    return (yield from ring_scatter([p.astype(BF16) for p in parts], chips))


def block_of(value, j, chips):
    size = value.shape[0] // chips
    return value[j * size : (j + 1) * size]


def scatter_tokens(part, chips, place, core):
    size = part.shape[0] // (2 * chips)

    def block(j, at):
        start = (2 * ((place + j) % chips) + at) * size
        return lax.dynamic_slice_in_dim(part, start, size, axis=0)

    sib = jnp.concatenate([block(j, 1 - core) for j in range(chips)], axis=0)
    return scatter_halves(
        lambda j: block(j, core), sib, lambda got, j: block_of(got, j, chips), chips
    )


def sum_rows(value, rows):
    if rows != 4:
        return lax.psum(value.astype(BF16), "rows").astype(F32)
    half = value.shape[0] // 2
    first, second = value[:half].astype(BF16), value[half:].astype(BF16)

    def pair(item, mask):
        return item.astype(F32) + swap_row(item, rows, mask).astype(F32)

    first, second = pair(first, 1).astype(BF16), pair(second, 2).astype(BF16)
    return jnp.concatenate([pair(first, 2), pair(second, 1)], axis=0)


def sum_all(value, rows, seq):
    mask = 1
    while mask < seq:
        value = value + lax.ppermute(value, "seq", [(s, s ^ mask) for s in range(seq)])
        mask *= 2
    mask = 1
    while mask < rows:
        value = value + swap_row(value, rows, mask)
        mask *= 2
    return value


def local(
    tokens,
    kv_cache,
    lengths,
    norm_gains,
    query_weight,
    output_weight,
    ffn_in_weight,
    down_weight,
    cotangent,
):
    rows_here, seg_len, width = tokens.shape
    seq = lax.axis_size("seq")
    rows = lax.axis_size("rows")
    chips = seq // 2
    seq_at = lax.axis_index("seq")
    row_at = lax.axis_index("rows")
    place, core = seq_at // 2, seq_at % 2
    order = (chips, place, core)
    gain_one, gain_two = norm_gains[0], norm_gains[1]
    query_pos = seq_at * seg_len + jnp.arange(seg_len, dtype=jnp.int32)
    chip_range = jnp.arange(chips, dtype=jnp.int32)
    ring_at = (place + chip_range) % chips
    starts = jnp.concatenate([2 * ring_at + core, 2 * ring_at + 1 - core]) * seg_len

    live = [
        (query_pos < lengths[r]).astype(F32).reshape(seg_len, 1) for r in range(rows_here)
    ]
    grad_out = [cotangent[r].astype(F32) * live[r] for r in range(rows_here)]
    grad_group = [
        lax.all_gather(g.astype(BF16), "seq", axis=0, tiled=True) for g in grad_out
    ]

    query_proj = Weight(query_weight, chips, rows, row_at, order)
    cache_own = kv_cache.reshape(rows_here, seg_len, 2, KV, HEAD).transpose(2, 0, 3, 1, 4)
    cache_slots, token = ring_gather(cache_own, chips, dep=query_proj.token)
    cache_block = jnp.concatenate(cache_slots, axis=3)
    cache_all = jnp.concatenate([cache_block, swap_core(cache_block, seq)], axis=3)
    output_proj = Weight(output_weight, chips, rows, row_at, order, dep=token)
    per = chips // KV

    def to_slots(value):
        value = jnp.repeat(value, per, axis=2) if per > 1 else value
        value = jnp.concatenate([value, value], axis=2)
        return lax.dynamic_slice_in_dim(value, place, chips, axis=2)

    def from_slots(value):
        value = jnp.concatenate([value, value], axis=2)
        value = lax.dynamic_slice_in_dim(value, (chips - place) % chips, chips, axis=2)
        if per > 1:
            shape = value.shape
            value = value.reshape(*shape[:2], KV, per, *shape[3:]).astype(F32).sum(axis=3)
        return value.astype(BF16)

    def to_heads(halves):
        value = jnp.stack([h.reshape(rows_here, seg_len, chips, -1, HEAD) for h in halves])
        value = value.transpose(1, 3, 0, 4, 2, 5)
        return value.reshape(rows_here, chips, -1, HEAD)

    def from_heads(value):
        value = value.reshape(rows_here, chips, 2, -1, seg_len, HEAD).transpose(2, 0, 4, 1, 3, 5)
        value = value.reshape(2, rows_here * seg_len, -1)
        return [value[0], value[1]]

    def heads_dot(spec, left, right):
        return jnp.einsum(spec, left, right, preferred_element_type=F32)

    key_pos = (starts[:, None] + jnp.arange(seg_len, dtype=jnp.int32)).reshape(-1)
    limit = jnp.minimum(query_pos[None], lengths[:, None] - 1)
    limit = jnp.tile(limit, (1, HEADS // chips))
    valid = (key_pos[None, None] <= limit[:, :, None])[:, None]
    scale = HEAD ** (-0.5)

    inputs = tokens.astype(F32).reshape(rows_here * seg_len, width)
    inverse_one = lax.rsqrt(jnp.mean(inputs * inputs, axis=-1, keepdims=True) + EPS)
    normed_one = (inputs * inverse_one * gain_one).astype(BF16)
    query = tie(query_proj.features(normed_one), grad_group)
    cache_slot = to_slots(cache_all)
    keys, values = cache_slot[0], cache_slot[1]
    query_heads = to_heads(query)
    scores = heads_dot("rjqd,rjkd->rjqk", query_heads, keys) * scale
    scores = jnp.where(valid, scores, NEG)
    best = jnp.max(scores, axis=-1, keepdims=True)
    weights = jnp.exp(scores - best)
    total = jnp.sum(weights, axis=-1, keepdims=True)
    mixed_heads = heads_dot("rjqk,rjkd->rjqd", weights.astype(BF16), values) / total
    lse = best + jnp.log(total)
    mixed = from_heads(mixed_heads.astype(BF16))
    middle_all = inputs + output_proj.back(mixed)
    inverse_all = lax.rsqrt(jnp.mean(middle_all * middle_all, axis=-1, keepdims=True) + EPS)
    normed_all = (middle_all * inverse_all * gain_two).astype(BF16)

    def split(value):
        return [value[r * seg_len : (r + 1) * seg_len] for r in range(rows_here)]

    middle, inverse_two, normed_two = split(middle_all), split(inverse_all), split(normed_all)
    normed_group = [lax.all_gather(n, "seq", axis=0, tiled=True) for n in normed_two]

    main, fill = Lane(), Lane()
    hidden, grad_gate, grad_up = [], [], []
    for r in range(rows_here):
        kept = jnp.einsum(
            "td,nkd->tkn", beside(normed_group[r], main), ffn_in_weight, preferred_element_type=F32
        )
        gate, upper = kept[:, 0], kept[:, 1]
        sigma = jax.nn.sigmoid(gate)
        grad_hidden = dot(beside(grad_group[r], main), down_weight, ((1,), (1,)))
        hidden.append((gate * sigma * upper).astype(BF16))
        grad_gate.append(
            (grad_hidden * upper * sigma * (1.0 + gate * (1.0 - sigma))).astype(BF16)
        )
        grad_up.append((grad_hidden * gate * sigma).astype(BF16))
        pair = beside(jnp.stack([grad_gate[r], grad_up[r]], axis=1), main)
        part = jnp.einsum("tkn,nkd->td", pair, ffn_in_weight, preferred_element_type=F32)
        main.add(("grad", r), scatter_tokens(part.astype(BF16), chips, place, core))
        part = dot(hidden[r], down_weight, ((1,), (0,))).astype(BF16)
        fill.add(("ffn", r), scatter_tokens(part, chips, place, core))

    def over_tokens(left, right):
        return sum(
            dot(a, b, ((0,), (0,))) for a, b in zip(left, right, strict=True)
        ).astype(BF16)

    down_part = over_tokens(hidden, grad_group)
    gate_part = over_tokens(grad_gate, normed_group)
    up_part = over_tokens(grad_up, normed_group)
    gate_grad, up_grad = lax.psum((gate_part, up_part), "rows")

    grad_middle, gain_two_grad = [], 0.0
    for r in range(rows_here):
        grad_normed_two = main.result(("grad", r))
        scaled_two = middle[r] * inverse_two[r]
        gain_two_grad += jnp.sum(grad_normed_two * scaled_two, axis=0)
        grad_middle.append(
            grad_out[r] + norm_back(grad_normed_two, scaled_two, inverse_two[r], gain_two)
        )
    grad_middle = jnp.concatenate(grad_middle, axis=0)
    grad_branch = beside(grad_middle.astype(BF16), fill)
    output_part = [dot(half, grad_branch, ((0,), (0,))).astype(BF16) for half in mixed]

    def scatter_rows(parts):
        def take(value, j):
            return block_of(value, j, chips)

        return scatter_halves(lambda j: take(parts[0], j), parts[1], take, chips)

    main.add("output", scatter_rows(output_part))
    grad_heads = to_heads(output_proj.features(beside(grad_branch, main, fill)))
    grad_heads = beside(grad_heads, main, fill)
    delta = jnp.sum(grad_heads.astype(F32) * mixed_heads, axis=-1, keepdims=True)
    scores = heads_dot("rjqd,rjkd->rjqk", query_heads, keys) * scale
    probs = jnp.where(valid, jnp.exp(scores - lse), 0.0)
    grad_probs = heads_dot("rjqd,rjkd->rjqk", grad_heads, values)
    grad_scores = (probs * (grad_probs - delta)).astype(BF16)
    query_term = from_heads(
        (heads_dot("rjqk,rjkd->rjqd", grad_scores, keys) * scale).astype(BF16)
    )
    grad_keys = heads_dot("rjqk,rjqd->rjkd", grad_scores, query_heads) * scale
    grad_values = heads_dot("rjqk,rjqd->rjkd", probs.astype(BF16), grad_heads)
    cache_part = from_slots(jnp.stack([grad_keys.astype(BF16), grad_values.astype(BF16)]))
    half_len = cache_part.shape[3] // 2

    def positions_of(value, j):
        return value[:, :, :, j * seg_len : (j + 1) * seg_len]

    main.step()
    fill.step()
    fill.add(
        "cache",
        scatter_halves(
            lambda j: positions_of(cache_part, j), cache_part[:, :, :, half_len:], positions_of, chips
        ),
    )
    query_part = [dot(half, normed_one, ((0,), (0,))).astype(BF16) for half in query_term]
    main.add("query", scatter_rows(query_part))

    grad_normed_one = query_proj.back(query_term)
    scaled_one = inputs * inverse_one
    gain_one_grad = jnp.sum(grad_normed_one * scaled_one, axis=0)
    input_grad = grad_middle + norm_back(grad_normed_one, scaled_one, inverse_one, gain_one)
    gain_grad = sum_all(jnp.stack([gain_one_grad, gain_two_grad]), rows, seq)

    output_grad = sum_rows(main.result("output"), rows)
    layer_out = [
        (live[r] * (middle[r] + fill.result(("ffn", r)))).astype(BF16) for r in range(rows_here)
    ]
    cache_grad = fill.result("cache")
    cache_grad = cache_grad.transpose(1, 3, 0, 2, 4).reshape(rows_here, seg_len, 2, KV * HEAD)
    query_grad = sum_rows(main.result("query"), rows)
    down_grad = sum_rows(down_part, rows)
    gate_grad, up_grad = lax.optimization_barrier((gate_grad, up_grad, query_grad))[:2]
    in_grad = jnp.stack([gate_grad, up_grad], axis=1)
    return (
        jnp.stack(layer_out),
        input_grad.reshape(rows_here, seg_len, width),
        cache_grad,
        gain_grad,
        query_grad,
        output_grad,
        in_grad.astype(F32),
        down_grad,
    )


def solution(mesh):
    in_specs = (
        P("rows", "seq", None),
        P("rows", "seq", None, None),
        P("rows"),
        P(),
        P("seq", None),
        P("seq", None),
        P("seq", None, None),
        P("seq", None),
        P("rows", "seq", None),
    )
    out_specs = (
        P("rows", "seq", None),
        P("rows", "seq", None),
        P("rows", "seq", None, None),
        P(),
        P("seq", None),
        P("seq", None),
        P("seq", None, None),
        P("seq", None),
    )
    return jax.shard_map(local, mesh=mesh, in_specs=in_specs, out_specs=out_specs, check_vma=False)
```

```python
import jax
import jax.numpy as jnp
from jax import lax
from jax.sharding import PartitionSpec as P

HEADS = 16
HEAD = 128
KV = 4
GROUP = 4
EPS = 1e-05
NEG = -1e30
F32 = jnp.float32
BF16 = jnp.bfloat16


def dot(left, right, dims):
    return lax.dot_general(left, right, (dims, ((), ())), preferred_element_type=F32)


def tie(value, dep):
    if dep is None:
        return value
    return lax.optimization_barrier((value, dep))[0]


def norm_back(grad_normed, scaled, inverse, gain):
    inner = grad_normed * gain
    return inverse * (inner - scaled * jnp.mean(inner * scaled, axis=-1, keepdims=True))


def swap_core(value, seq):
    return lax.ppermute(value, "seq", [(s, s ^ 1) for s in range(seq)])


def ring(value, chips):
    pairs = [(2 * z + c, 2 * ((z + 1) % chips) + c) for z in range(chips) for c in range(2)]
    return lax.ppermute(value, "seq", pairs)


def swap_row(value, rows, mask):
    return lax.ppermute(value, "rows", [(r, r ^ mask) for r in range(rows)])


def ring_gather(own, chips, dep=None):
    got = [tie(own, dep)]
    for _ in range(1, chips):
        got.append(ring(got[-1], chips))
    return [own] + got[:0:-1], got[-2]


def ring_scatter(parts, chips):
    sent = parts[chips - 1]
    for j in range(chips - 2, -1, -1):
        yield sent
        total = ring(sent, chips).astype(F32) + parts[j].astype(F32)
        sent = total.astype(BF16)
    return total


class Lane:
    def __init__(self):
        self.waiting, self.results, self.sent = [], {}, None

    def add(self, name, steps):
        self.waiting.append((name, steps))

    def step(self):
        if self.waiting:
            name, steps = self.waiting[0]
            try:
                sent = next(steps)
                self.sent = sent
                return sent
            except StopIteration as end:
                self.results[name] = end.value
                self.waiting.pop(0)
                return self.step()
        return None

    def result(self, name):
        while name not in self.results:
            self.step()
        return self.results[name]


def beside(value, *lanes):
    for lane in lanes:
        value = tie(value, lane.step())
    return value


def xor_order(value, at):
    shape = value.shape
    value = value.reshape(2, 2, *shape[1:])
    value = jnp.where(at % 2 == 1, value[:, ::-1], value)
    return jnp.where(at // 2 == 1, value[::-1], value).reshape(shape)


def own_order(value, chips, place, core):
    count = value.shape[0]
    value = value.reshape(count, chips, 2, -1)
    value = jnp.where(core == 0, value, value[:, :, ::-1])
    value = jnp.concatenate([value, value], axis=1)
    value = lax.dynamic_slice_in_dim(value, place, chips, axis=1)
    return value.transpose(0, 2, 1, 3).reshape(count, -1)


def index_order(value, chips, place, core):
    count = value.shape[0]
    value = value.reshape(count, 2, chips, -1).transpose(0, 2, 1, 3)
    value = jnp.concatenate([value, value], axis=1)
    value = lax.dynamic_slice_in_dim(value, (chips - place) % chips, chips, axis=1)
    value = jnp.where(core == 0, value, value[:, :, ::-1])
    return value.reshape(count, -1)


class Weight:
    def __init__(self, shard, chips, rows, row_at, order, dep=None, beside=None):
        seq = 2 * chips
        self.chips, self.row_at, self.order = chips, row_at, order
        depth, width = shard.shape
        self.depth = depth
        self.split = rows == 4 and depth % 32 == 0 and width % 512 == 0
        self.beside = beside
        if not self.split:
            self.whole = lax.all_gather(shard, "seq", axis=0, tiled=True)
            self.token = dep
            return
        part = width // rows
        half = depth // 2
        mine = lax.dynamic_slice_in_dim(shard, row_at * part, part, axis=1)
        slots, self.token = ring_gather(mine, chips, dep=dep)
        first = jnp.stack([v[:half] for v in slots[1:]])
        self.beside = beside
        if beside is not None:
            first, self.beside = lax.optimization_barrier((first, beside))
        second = jnp.stack([v[half:] for v in slots[1:]])
        first_x = swap_row(first, rows, 1)
        second_y = swap_row(second, rows, 2)
        first_pair = swap_row(jnp.stack([first, first_x]), rows, 2)
        second_pair = swap_row(jnp.stack([second, second_y]), rows, 1)
        parts = jnp.stack(
            [
                jnp.stack([first, first_x, first_pair[0], first_pair[1]]),
                jnp.stack([second, second_pair[0], second_y, second_pair[1]]),
            ],
            axis=2,
        )
        parts = parts.reshape(rows, (chips - 1) * depth, part)
        self.far = [parts, swap_core(parts, seq)]
        self.near = [shard, swap_core(shard, seq)]

    def features(self, value):
        if not self.split:
            out = own_order(dot(value, self.whole, ((1,), (1,))), *self.order)
            half = out.shape[1] // 2
            return [out[:, :half].astype(BF16), out[:, half:].astype(BF16)]
        count = value.shape[0]
        blocks = value.reshape(count, 4, -1).transpose(1, 0, 2)
        blocks = xor_order(blocks, self.row_at)
        out = []
        for near, far in zip(self.near, self.far, strict=True):
            term = jnp.einsum("ktc,kfc->ktf", blocks, far, preferred_element_type=F32)
            term = jnp.sum(term, axis=0).astype(BF16)
            out.append(jnp.concatenate([dot(value, near, ((1,), (1,))).astype(BF16), term], axis=1))
        return out

    def back(self, halves):
        if not self.split:
            value = jnp.concatenate(halves, axis=1)
            return dot(index_order(value, *self.order), self.whole, ((1,), (0,)))
        count = halves[0].shape[0]
        near_sum = far_sum = 0.0
        for part, near, far in zip(halves, self.near, self.far, strict=True):
            near_sum += dot(part[:, : self.depth], near, ((1,), (0,)))
            far_sum += jnp.einsum(
                "tf,kfc->ktc", part[:, self.depth :], far, preferred_element_type=F32
            )
        far_sum = xor_order(far_sum, self.row_at).transpose(1, 0, 2).reshape(count, -1)
        return near_sum + far_sum


def scatter_halves(own, sib, got_at, chips):
    got = swap_core(sib, 2 * chips)
    parts = [own(j).astype(F32) + got_at(got, j).astype(F32) for j in range(chips)]
    return (yield from ring_scatter([p.astype(BF16) for p in parts], chips))


def block_of(value, j, chips):
    size = value.shape[0] // chips
    return value[j * size : (j + 1) * size]


def scatter_tokens(part, chips, place, core):
    size = part.shape[0] // (2 * chips)

    def block(j, at):
        start = (2 * ((place + j) % chips) + at) * size
        return lax.dynamic_slice_in_dim(part, start, size, axis=0)

    sib = jnp.concatenate([block(j, 1 - core) for j in range(chips)], axis=0)
    return scatter_halves(
        lambda j: block(j, core), sib, lambda got, j: block_of(got, j, chips), chips
    )


def sum_rows(value, rows):
    if rows != 4:
        return lax.psum(value.astype(BF16), "rows").astype(F32)
    half = value.shape[0] // 2
    first, second = value[:half].astype(BF16), value[half:].astype(BF16)

    def pair(item, mask):
        return item.astype(F32) + swap_row(item, rows, mask).astype(F32)

    first, second = pair(first, 1).astype(BF16), pair(second, 2).astype(BF16)
    return jnp.concatenate([pair(first, 2), pair(second, 1)], axis=0)


def sum_all(value, rows, seq):
    mask = 1
    while mask < seq:
        value = value + lax.ppermute(value, "seq", [(s, s ^ mask) for s in range(seq)])
        mask *= 2
    mask = 1
    while mask < rows:
        value = value + swap_row(value, rows, mask)
        mask *= 2
    return value


def local(
    tokens,
    kv_cache,
    lengths,
    norm_gains,
    query_weight,
    output_weight,
    ffn_in_weight,
    down_weight,
    cotangent,
):
    rows_here, seg_len, width = tokens.shape
    seq = lax.axis_size("seq")
    rows = lax.axis_size("rows")
    chips = seq // 2
    seq_at = lax.axis_index("seq")
    row_at = lax.axis_index("rows")
    place, core = seq_at // 2, seq_at % 2
    order = (chips, place, core)
    gain_one, gain_two = norm_gains[0], norm_gains[1]
    query_pos = seq_at * seg_len + jnp.arange(seg_len, dtype=jnp.int32)
    chip_range = jnp.arange(chips, dtype=jnp.int32)
    ring_at = (place + chip_range) % chips
    starts = jnp.concatenate([2 * ring_at + core, 2 * ring_at + 1 - core]) * seg_len

    live = [
        (query_pos < lengths[r]).astype(F32).reshape(seg_len, 1) for r in range(rows_here)
    ]
    grad_out = [cotangent[r].astype(F32) * live[r] for r in range(rows_here)]
    gate_up_weight = jnp.concatenate([ffn_in_weight[:, 0], ffn_in_weight[:, 1]], axis=0)
    query_proj = Weight(query_weight, chips, rows, row_at, order, beside=gate_up_weight)
    gate_up_weight = query_proj.beside
    cache_own = kv_cache.reshape(rows_here, seg_len, 2, KV, HEAD).transpose(2, 0, 3, 1, 4)
    cache_slots, token = ring_gather(cache_own, chips, dep=query_proj.token)
    cache_block = jnp.concatenate(cache_slots, axis=3)
    cache_all = jnp.concatenate([cache_block, swap_core(cache_block, seq)], axis=3)
    output_proj = Weight(output_weight, chips, rows, row_at, order, dep=token)
    grad_group = [
        lax.all_gather(g.astype(BF16), "seq", axis=0, tiled=True) for g in grad_out
    ]
    per = chips // KV

    def to_slots(value):
        value = jnp.repeat(value, per, axis=2) if per > 1 else value
        value = jnp.concatenate([value, value], axis=2)
        return lax.dynamic_slice_in_dim(value, place, chips, axis=2)

    def from_slots(value):
        value = jnp.concatenate([value, value], axis=2)
        value = lax.dynamic_slice_in_dim(value, (chips - place) % chips, chips, axis=2)
        if per > 1:
            shape = value.shape
            value = value.reshape(*shape[:2], KV, per, *shape[3:]).astype(F32).sum(axis=3)
        return value.astype(BF16)

    def to_heads(halves):
        value = jnp.stack([h.reshape(rows_here, seg_len, chips, -1, HEAD) for h in halves])
        value = value.transpose(1, 3, 0, 4, 2, 5)
        return value.reshape(rows_here, chips, -1, HEAD)

    def from_heads(value):
        value = value.reshape(rows_here, chips, 2, -1, seg_len, HEAD).transpose(2, 0, 4, 1, 3, 5)
        value = value.reshape(2, rows_here * seg_len, -1)
        return [value[0], value[1]]

    def heads_dot(spec, left, right):
        return jnp.einsum(spec, left, right, preferred_element_type=F32)

    key_pos = (starts[:, None] + jnp.arange(seg_len, dtype=jnp.int32)).reshape(-1)
    limit = jnp.minimum(query_pos[None], lengths[:, None] - 1)
    limit = jnp.tile(limit, (1, HEADS // chips))
    valid = (key_pos[None, None] <= limit[:, :, None])[:, None]
    scale = HEAD ** (-0.5)

    inputs = tokens.astype(F32).reshape(rows_here * seg_len, width)
    inverse_one = lax.rsqrt(jnp.mean(inputs * inputs, axis=-1, keepdims=True) + EPS)
    normed_one = (inputs * inverse_one * gain_one).astype(BF16)
    query = query_proj.features(normed_one)
    query, grad_group[0] = lax.optimization_barrier((query, grad_group[0]))
    cache_slot = to_slots(cache_all)
    keys, values = cache_slot[0], cache_slot[1]
    query_heads = to_heads(query)
    scores = heads_dot("rjqd,rjkd->rjqk", query_heads, keys) * scale
    scores = jnp.where(valid, scores, NEG)
    best = jnp.max(scores, axis=-1, keepdims=True)
    weights = jnp.exp(scores - best)
    total = jnp.sum(weights, axis=-1, keepdims=True)
    mixed_heads = heads_dot("rjqk,rjkd->rjqd", weights.astype(BF16), values) / total
    lse = best + jnp.log(total)
    mixed = from_heads(mixed_heads.astype(BF16))
    mixed, grad_group[1:] = lax.optimization_barrier((mixed, grad_group[1:]))
    middle_all = inputs + output_proj.back(mixed)
    inverse_all = lax.rsqrt(jnp.mean(middle_all * middle_all, axis=-1, keepdims=True) + EPS)
    normed_all = (middle_all * inverse_all * gain_two).astype(BF16)

    def split(value):
        return [value[r * seg_len : (r + 1) * seg_len] for r in range(rows_here)]

    middle, inverse_two, normed_two = split(middle_all), split(inverse_all), split(normed_all)
    normed_group = [lax.all_gather(n, "seq", axis=0, tiled=True) for n in normed_two]

    main, fill = Lane(), Lane()
    units = down_weight.shape[0]
    hidden, grad_gate_up, grad_part, ffn_part = [], [], [], []
    for r in range(rows_here):
        kept = dot(beside(normed_group[r], main), gate_up_weight, ((1,), (1,)))
        gate, upper = kept[:, :units], kept[:, units:]
        sigma = jax.nn.sigmoid(gate)
        grad_hidden = dot(beside(grad_group[r], main), down_weight, ((1,), (1,)))
        hidden.append((gate * sigma * upper).astype(BF16))
        grad_gate = grad_hidden * upper * sigma * (1.0 + gate * (1.0 - sigma))
        grad_up = grad_hidden * gate * sigma
        grad_gate_up.append(jnp.concatenate([grad_gate, grad_up], axis=1).astype(BF16))
        part = dot(beside(grad_gate_up[r], main), gate_up_weight, ((1,), (0,))).astype(BF16)
        grad_part.append(part)
        ffn_part.append(dot(hidden[r], down_weight, ((1,), (0,))).astype(BF16))
        main.add(("grad", r), scatter_tokens(part, chips, place, core))

    def over_tokens(left, right, start, size):
        total = 0.0
        for r in range(rows_here):
            part = left[r][:, start : start + size]
            total += dot(part, right[r], ((0,), (0,)))
        return total.astype(BF16)

    gate_part = over_tokens(grad_gate_up, normed_group, 0, units)
    up_part = over_tokens(grad_gate_up, normed_group, units, units)
    down_part = over_tokens(hidden, grad_group, 0, units)
    parts = (gate_part, up_part, down_part)
    summed = lax.psum(parts, "rows")

    grad_middle, gain_two_grad = [], 0.0
    for r in range(rows_here):
        grad_normed_two = main.result(("grad", r))
        if r:
            grad_normed_two, parts = lax.optimization_barrier((grad_normed_two, parts))
        scaled_two = middle[r] * inverse_two[r]
        gain_two_grad += jnp.sum(grad_normed_two * scaled_two, axis=0)
        grad_middle.append(
            grad_out[r] + norm_back(grad_normed_two, scaled_two, inverse_two[r], gain_two)
        )
    for r in range(rows_here):
        part = tie(ffn_part[r], grad_middle[-1]) if r else ffn_part[r]
        fill.add(("ffn", r), scatter_tokens(part, chips, place, core))
    grad_middle = jnp.concatenate(grad_middle, axis=0)
    grad_branch = beside(grad_middle.astype(BF16), fill)
    output_part = [dot(half, grad_branch, ((0,), (0,))).astype(BF16) for half in mixed]

    def scatter_rows(parts):
        def take(value, j):
            return block_of(value, j, chips)

        return scatter_halves(lambda j: take(parts[0], j), parts[1], take, chips)

    main.add("output", scatter_rows(output_part))
    grad_heads = to_heads(output_proj.features(beside(grad_branch, main, fill)))
    grad_heads = beside(grad_heads, main, fill)
    delta = jnp.sum(grad_heads.astype(F32) * mixed_heads, axis=-1, keepdims=True)
    scores = heads_dot("rjqd,rjkd->rjqk", query_heads, keys) * scale
    probs = jnp.where(valid, jnp.exp(scores - lse), 0.0)
    grad_probs = heads_dot("rjqd,rjkd->rjqk", grad_heads, values)
    grad_scores = (probs * (grad_probs - delta)).astype(BF16)
    query_term = from_heads(
        (heads_dot("rjqk,rjkd->rjqd", grad_scores, keys) * scale).astype(BF16)
    )
    grad_keys = heads_dot("rjqk,rjqd->rjkd", grad_scores, query_heads) * scale
    grad_values = heads_dot("rjqk,rjqd->rjkd", probs.astype(BF16), grad_heads)
    cache_part = from_slots(jnp.stack([grad_keys.astype(BF16), grad_values.astype(BF16)]))
    half_len = cache_part.shape[3] // 2

    def positions_of(value, j):
        return value[:, :, :, j * seg_len : (j + 1) * seg_len]

    main.step()
    fill.step()
    fill.add(
        "cache",
        scatter_halves(
            lambda j: positions_of(cache_part, j), cache_part[:, :, :, half_len:], positions_of, chips
        ),
    )
    query_part = [dot(half, normed_one, ((0,), (0,))).astype(BF16) for half in query_term]
    main.add("query", scatter_rows(query_part))

    grad_normed_one = query_proj.back(query_term)
    scaled_one = inputs * inverse_one
    gain_one_grad = jnp.sum(grad_normed_one * scaled_one, axis=0)
    input_grad = grad_middle + norm_back(grad_normed_one, scaled_one, inverse_one, gain_one)
    gain_grad = sum_all(jnp.stack([gain_one_grad, gain_two_grad]), rows, seq)

    layer_out = [
        (live[r] * (middle[r] + fill.result(("ffn", r)))).astype(BF16) for r in range(rows_here)
    ]
    cache_grad = fill.result("cache")
    cache_grad = cache_grad.transpose(1, 3, 0, 2, 4).reshape(rows_here, seg_len, 2, KV * HEAD)
    summed, output_sum, query_sum = lax.optimization_barrier(
        (summed, main.result("output").astype(BF16), main.result("query").astype(BF16))
    )
    gate_grad, up_grad, down_grad = summed
    output_grad, query_grad = sum_rows(output_sum, rows), sum_rows(query_sum, rows)
    in_grad = jnp.concatenate([gate_grad, up_grad], axis=1)
    in_grad = lax.optimization_barrier(in_grad.reshape(units, 2, width))
    return (
        jnp.stack(layer_out),
        input_grad.reshape(rows_here, seg_len, width),
        cache_grad,
        gain_grad,
        query_grad,
        output_grad,
        in_grad.astype(F32),
        down_grad.astype(F32),
    )


def solution(mesh):
    in_specs = (
        P("rows", "seq", None),
        P("rows", "seq", None, None),
        P("rows"),
        P(),
        P("seq", None),
        P("seq", None),
        P("seq", None, None),
        P("seq", None),
        P("rows", "seq", None),
    )
    out_specs = (
        P("rows", "seq", None),
        P("rows", "seq", None),
        P("rows", "seq", None, None),
        P(),
        P("seq", None),
        P("seq", None),
        P("seq", None, None),
        P("seq", None),
    )
    return jax.shard_map(local, mesh=mesh, in_specs=in_specs, out_specs=out_specs, check_vma=False)
```

```python
import jax
import jax.numpy as jnp
from jax import lax
from jax.sharding import PartitionSpec as P

HEADS = 16
HEAD = 128
KV = 4
GROUP = 4
EPS = 1e-05
NEG = -1e30
F32 = jnp.float32
BF16 = jnp.bfloat16


def dot(left, right, dims):
    return lax.dot_general(left, right, (dims, ((), ())), preferred_element_type=F32)


def tie(value, dep):
    if dep is None:
        return value
    return lax.optimization_barrier((value, dep))[0]


def norm_back(grad_normed, scaled, inverse, gain):
    inner = grad_normed * gain
    return inverse * (inner - scaled * jnp.mean(inner * scaled, axis=-1, keepdims=True))


def swap_core(value, seq):
    return lax.ppermute(value, "seq", [(s, s ^ 1) for s in range(seq)])


def ring(value, chips):
    pairs = [(2 * z + c, 2 * ((z + 1) % chips) + c) for z in range(chips) for c in range(2)]
    return lax.ppermute(value, "seq", pairs)


def swap_row(value, rows, mask):
    return lax.ppermute(value, "rows", [(r, r ^ mask) for r in range(rows)])


def ring_gather(own, chips, dep=None):
    got = [tie(own, dep)]
    for _ in range(1, chips):
        got.append(ring(got[-1], chips))
    return [own] + got[:0:-1], got[-2]


def ring_scatter(parts, chips):
    sent = parts[chips - 1]
    for j in range(chips - 2, -1, -1):
        yield sent
        total = ring(sent, chips).astype(F32) + parts[j].astype(F32)
        sent = total.astype(BF16)
    return total


class Lane:
    def __init__(self):
        self.waiting, self.results, self.sent = [], {}, None

    def add(self, name, steps):
        self.waiting.append((name, steps))

    def step(self):
        if self.waiting:
            name, steps = self.waiting[0]
            try:
                sent = next(steps)
                self.sent = sent
                return sent
            except StopIteration as end:
                self.results[name] = end.value
                self.waiting.pop(0)
                return self.step()
        return None

    def result(self, name):
        while name not in self.results:
            self.step()
        return self.results[name]


def beside(value, *lanes):
    for lane in lanes:
        value = tie(value, lane.step())
    return value


def xor_order(value, at):
    shape = value.shape
    value = value.reshape(2, 2, *shape[1:])
    value = jnp.where(at % 2 == 1, value[:, ::-1], value)
    return jnp.where(at // 2 == 1, value[::-1], value).reshape(shape)


def own_order(value, chips, place, core):
    count = value.shape[0]
    value = value.reshape(count, chips, 2, -1)
    value = jnp.where(core == 0, value, value[:, :, ::-1])
    value = jnp.concatenate([value, value], axis=1)
    value = lax.dynamic_slice_in_dim(value, place, chips, axis=1)
    return value.transpose(0, 2, 1, 3).reshape(count, -1)


def index_order(value, chips, place, core):
    count = value.shape[0]
    value = value.reshape(count, 2, chips, -1).transpose(0, 2, 1, 3)
    value = jnp.concatenate([value, value], axis=1)
    value = lax.dynamic_slice_in_dim(value, (chips - place) % chips, chips, axis=1)
    value = jnp.where(core == 0, value, value[:, :, ::-1])
    return value.reshape(count, -1)


class Weight:
    def __init__(self, shard, chips, rows, row_at, order, dep=None):
        seq = 2 * chips
        self.chips, self.row_at, self.order = chips, row_at, order
        depth, width = shard.shape
        self.depth = depth
        self.split = rows == 4 and depth % 32 == 0 and width % 512 == 0
        if not self.split:
            self.whole = lax.all_gather(shard, "seq", axis=0, tiled=True)
            self.token = dep
            return
        part = width // rows
        half = depth // 2
        mine = lax.dynamic_slice_in_dim(shard, row_at * part, part, axis=1)
        slots, self.token = ring_gather(mine, chips, dep=dep)
        first = jnp.stack([v[:half] for v in slots[1:]])
        second = jnp.stack([v[half:] for v in slots[1:]])
        first_x = swap_row(first, rows, 1)
        second_y = swap_row(second, rows, 2)
        first_pair = swap_row(jnp.stack([first, first_x]), rows, 2)
        second_pair = swap_row(jnp.stack([second, second_y]), rows, 1)
        parts = [first, second, first_x, second_pair[0]]
        parts += [first_pair[0], second_y, first_pair[1], second_pair[1]]
        parts = jnp.concatenate(parts, axis=0).reshape(rows, (chips - 1) * depth, part)
        self.far = [parts, swap_core(parts, seq)]
        self.near = [shard, swap_core(shard, seq)]

    def features(self, value):
        if not self.split:
            out = own_order(dot(value, self.whole, ((1,), (1,))), *self.order)
            half = out.shape[1] // 2
            return [out[:, :half].astype(BF16), out[:, half:].astype(BF16)]
        count = value.shape[0]
        blocks = value.reshape(count, 4, -1).transpose(1, 0, 2)
        blocks = xor_order(blocks, self.row_at)
        out = []
        for near, far in zip(self.near, self.far, strict=True):
            term = jnp.einsum("ktc,kfc->ktf", blocks, far, preferred_element_type=F32)
            term = jnp.sum(term, axis=0).astype(BF16)
            term = term.reshape(count, 2, self.chips - 1, -1).transpose(0, 2, 1, 3)
            term = term.reshape(count, -1)
            out.append(jnp.concatenate([dot(value, near, ((1,), (1,))).astype(BF16), term], axis=1))
        return out

    def back(self, halves):
        if not self.split:
            value = jnp.concatenate(halves, axis=1)
            return dot(index_order(value, *self.order), self.whole, ((1,), (0,)))
        count = halves[0].shape[0]
        near_sum = far_sum = 0.0
        for part, near, far in zip(halves, self.near, self.far, strict=True):
            near_sum += dot(part[:, : self.depth], near, ((1,), (0,)))
            rest = part[:, self.depth :].reshape(count, self.chips - 1, 2, -1)
            rest = rest.transpose(0, 2, 1, 3).reshape(count, -1)
            far_sum += jnp.einsum("tf,kfc->ktc", rest, far, preferred_element_type=F32)
        far_sum = xor_order(far_sum, self.row_at).transpose(1, 0, 2).reshape(count, -1)
        return near_sum + far_sum


def scatter_halves(own, sib, got_at, chips):
    got = swap_core(sib, 2 * chips)
    parts = [own(j).astype(F32) + got_at(got, j).astype(F32) for j in range(chips)]
    return (yield from ring_scatter([p.astype(BF16) for p in parts], chips))


def block_of(value, j, chips):
    size = value.shape[0] // chips
    return value[j * size : (j + 1) * size]


def scatter_tokens(part, chips, place, core):
    size = part.shape[0] // (2 * chips)

    def block(j, at):
        start = (2 * ((place + j) % chips) + at) * size
        return lax.dynamic_slice_in_dim(part, start, size, axis=0)

    sib = jnp.concatenate([block(j, 1 - core) for j in range(chips)], axis=0)
    return scatter_halves(
        lambda j: block(j, core), sib, lambda got, j: block_of(got, j, chips), chips
    )


def sum_rows(value, rows):
    if rows != 4:
        return lax.psum(value.astype(BF16), "rows").astype(F32)
    half = value.shape[0] // 2
    first, second = value[:half].astype(BF16), value[half:].astype(BF16)

    def pair(item, mask):
        return item.astype(F32) + swap_row(item, rows, mask).astype(F32)

    first, second = pair(first, 1).astype(BF16), pair(second, 2).astype(BF16)
    return jnp.concatenate([pair(first, 2), pair(second, 1)], axis=0)


def sum_all(value, rows, seq):
    mask = 1
    while mask < seq:
        value = value + lax.ppermute(value, "seq", [(s, s ^ mask) for s in range(seq)])
        mask *= 2
    mask = 1
    while mask < rows:
        value = value + swap_row(value, rows, mask)
        mask *= 2
    return value


def local(
    tokens,
    kv_cache,
    lengths,
    norm_gains,
    query_weight,
    output_weight,
    ffn_in_weight,
    down_weight,
    cotangent,
):
    rows_here, seg_len, width = tokens.shape
    seq = lax.axis_size("seq")
    rows = lax.axis_size("rows")
    chips = seq // 2
    seq_at = lax.axis_index("seq")
    row_at = lax.axis_index("rows")
    place, core = seq_at // 2, seq_at % 2
    order = (chips, place, core)
    gain_one, gain_two = norm_gains[0], norm_gains[1]
    query_pos = seq_at * seg_len + jnp.arange(seg_len, dtype=jnp.int32)
    chip_range = jnp.arange(chips, dtype=jnp.int32)
    ring_at = (place + chip_range) % chips
    starts = jnp.concatenate([2 * ring_at + core, 2 * ring_at + 1 - core]) * seg_len

    live = [
        (query_pos < lengths[r]).astype(F32).reshape(seg_len, 1) for r in range(rows_here)
    ]
    grad_out = [cotangent[r].astype(F32) * live[r] for r in range(rows_here)]
    gate_up_weight = jnp.concatenate([ffn_in_weight[:, 0], ffn_in_weight[:, 1]], axis=0)
    query_proj = Weight(query_weight, chips, rows, row_at, order)
    cache_own = kv_cache.reshape(rows_here, seg_len, 2, KV, HEAD).transpose(2, 0, 3, 1, 4)
    cache_slots, token = ring_gather(cache_own, chips, dep=query_proj.token)
    cache_block = jnp.concatenate(cache_slots, axis=3)
    cache_all = jnp.concatenate([cache_block, swap_core(cache_block, seq)], axis=3)
    output_proj = Weight(output_weight, chips, rows, row_at, order, dep=token)
    grad_group = [
        lax.all_gather(tie(g.astype(BF16), output_proj.token), "seq", axis=0, tiled=True)
        for g in grad_out
    ]
    per = chips // KV

    def to_slots(value):
        value = jnp.repeat(value, per, axis=2) if per > 1 else value
        value = jnp.concatenate([value, value], axis=2)
        return lax.dynamic_slice_in_dim(value, place, chips, axis=2)

    def from_slots(value):
        value = jnp.concatenate([value, value], axis=2)
        value = lax.dynamic_slice_in_dim(value, (chips - place) % chips, chips, axis=2)
        if per > 1:
            shape = value.shape
            value = value.reshape(*shape[:2], KV, per, *shape[3:]).astype(F32).sum(axis=3)
        return value.astype(BF16)

    def to_heads(halves):
        value = jnp.stack([h.reshape(rows_here, seg_len, chips, -1, HEAD) for h in halves])
        value = value.transpose(1, 3, 0, 4, 2, 5)
        return value.reshape(rows_here, chips, -1, HEAD)

    def from_heads(value):
        value = value.reshape(rows_here, chips, 2, -1, seg_len, HEAD).transpose(2, 0, 4, 1, 3, 5)
        value = value.reshape(2, rows_here * seg_len, -1)
        return [value[0], value[1]]

    def heads_dot(spec, left, right):
        return jnp.einsum(spec, left, right, preferred_element_type=F32)

    key_pos = (starts[:, None] + jnp.arange(seg_len, dtype=jnp.int32)).reshape(-1)
    limit = jnp.minimum(query_pos[None], lengths[:, None] - 1)
    limit = jnp.tile(limit, (1, HEADS // chips))
    valid = (key_pos[None, None] <= limit[:, :, None])[:, None]
    scale = HEAD ** (-0.5)

    inputs = tokens.astype(F32).reshape(rows_here * seg_len, width)
    inverse_one = lax.rsqrt(jnp.mean(inputs * inputs, axis=-1, keepdims=True) + EPS)
    normed_one = (inputs * inverse_one * gain_one).astype(BF16)
    query = query_proj.features(normed_one)
    cache_slot = to_slots(cache_all)
    keys, values = cache_slot[0], cache_slot[1]
    query_heads = to_heads(query)
    scores = heads_dot("rjqd,rjkd->rjqk", query_heads, keys) * scale
    scores = jnp.where(valid, scores, NEG)
    best = jnp.max(scores, axis=-1, keepdims=True)
    weights = jnp.exp(scores - best)
    total = jnp.sum(weights, axis=-1, keepdims=True)
    mixed_heads = heads_dot("rjqk,rjkd->rjqd", weights.astype(BF16), values) / total
    lse = best + jnp.log(total)
    mixed = from_heads(mixed_heads.astype(BF16))
    mixed, grad_group[0] = lax.optimization_barrier((mixed, grad_group[0]))
    middle_all = inputs + output_proj.back(mixed)
    inverse_all = lax.rsqrt(jnp.mean(middle_all * middle_all, axis=-1, keepdims=True) + EPS)
    normed_all = (middle_all * inverse_all * gain_two).astype(BF16)
    normed_all, grad_group[1:] = lax.optimization_barrier((normed_all, grad_group[1:]))

    def split(value):
        return [value[r * seg_len : (r + 1) * seg_len] for r in range(rows_here)]

    middle, inverse_two, normed_two = split(middle_all), split(inverse_all), split(normed_all)
    normed_group = [lax.all_gather(n, "seq", axis=0, tiled=True) for n in normed_two]

    main, fill = Lane(), Lane()
    units = down_weight.shape[0]
    hidden, grad_gate_up, grad_part, ffn_part = [], [], [], []
    for r in range(rows_here):
        kept = dot(beside(normed_group[r], main), gate_up_weight, ((1,), (1,)))
        gate, upper = kept[:, :units], kept[:, units:]
        sigma = jax.nn.sigmoid(gate)
        grad_hidden = dot(beside(grad_group[r], main), down_weight, ((1,), (1,)))
        hidden.append((gate * sigma * upper).astype(BF16))
        grad_gate = grad_hidden * upper * sigma * (1.0 + gate * (1.0 - sigma))
        grad_up = grad_hidden * gate * sigma
        grad_gate_up.append(jnp.concatenate([grad_gate, grad_up], axis=1).astype(BF16))
        part = dot(beside(grad_gate_up[r], main), gate_up_weight, ((1,), (0,))).astype(BF16)
        grad_part.append(part)
        ffn_part.append(dot(hidden[r], down_weight, ((1,), (0,))).astype(BF16))
        main.add(("grad", r), scatter_tokens(part, chips, place, core))

    def over_tokens(left, right, start, size):
        total = 0.0
        for r in range(rows_here):
            part = left[r][:, start : start + size]
            total += dot(part, right[r], ((0,), (0,)))
        return total.astype(BF16)

    gate_part = over_tokens(grad_gate_up, normed_group, 0, units)
    up_part = over_tokens(grad_gate_up, normed_group, units, units)
    down_part = over_tokens(hidden, grad_group, 0, units)
    for r in range(rows_here):
        fill.add(("ffn", r), scatter_tokens(ffn_part[r], chips, place, core))
    parts = (gate_part, up_part, down_part)
    summed = lax.psum(parts, "rows")

    grad_middle, gain_two_grad = [], 0.0
    for r in range(rows_here):
        grad_normed_two = main.result(("grad", r))
        if r:
            grad_normed_two, parts = lax.optimization_barrier((grad_normed_two, parts))
        scaled_two = middle[r] * inverse_two[r]
        gain_two_grad += jnp.sum(grad_normed_two * scaled_two, axis=0)
        grad_middle.append(
            grad_out[r] + norm_back(grad_normed_two, scaled_two, inverse_two[r], gain_two)
        )
    grad_middle = jnp.concatenate(grad_middle, axis=0)
    grad_branch = grad_middle.astype(BF16)
    output_part = [dot(half, grad_branch, ((0,), (0,))).astype(BF16) for half in mixed]

    def scatter_rows(parts):
        def take(value, j):
            return block_of(value, j, chips)

        return scatter_halves(lambda j: take(parts[0], j), parts[1], take, chips)

    main.add("output", scatter_rows(output_part))
    grad_heads = to_heads(output_proj.features(grad_branch))
    delta = jnp.sum(grad_heads.astype(F32) * mixed_heads, axis=-1, keepdims=True)
    scores = heads_dot("rjqd,rjkd->rjqk", query_heads, keys) * scale
    probs = jnp.where(valid, jnp.exp(scores - lse), 0.0)
    grad_probs = heads_dot("rjqd,rjkd->rjqk", grad_heads, values)
    grad_scores = (probs * (grad_probs - delta)).astype(BF16)
    query_term = from_heads(
        (heads_dot("rjqk,rjkd->rjqd", grad_scores, keys) * scale).astype(BF16)
    )
    grad_keys = heads_dot("rjqk,rjqd->rjkd", grad_scores, query_heads) * scale
    grad_values = heads_dot("rjqk,rjqd->rjkd", probs.astype(BF16), grad_heads)
    cache_part = from_slots(jnp.stack([grad_keys.astype(BF16), grad_values.astype(BF16)]))
    half_len = cache_part.shape[3] // 2

    def positions_of(value, j):
        return value[:, :, :, j * seg_len : (j + 1) * seg_len]

    fill.add(
        "cache",
        scatter_halves(
            lambda j: positions_of(cache_part, j), cache_part[:, :, :, half_len:], positions_of, chips
        ),
    )
    query_part = [dot(half, normed_one, ((0,), (0,))).astype(BF16) for half in query_term]
    main.add("query", scatter_rows(query_part))

    grad_normed_one = query_proj.back(query_term)
    scaled_one = inputs * inverse_one
    gain_one_grad = jnp.sum(grad_normed_one * scaled_one, axis=0)
    input_grad = grad_middle + norm_back(grad_normed_one, scaled_one, inverse_one, gain_one)
    gain_grad = sum_all(jnp.stack([gain_one_grad, gain_two_grad]), rows, seq)

    layer_out = [
        (live[r] * (middle[r] + fill.result(("ffn", r)))).astype(BF16) for r in range(rows_here)
    ]
    cache_grad = fill.result("cache")
    cache_grad = cache_grad.transpose(1, 3, 0, 2, 4).reshape(rows_here, seg_len, 2, KV * HEAD)
    summed, output_sum, query_sum = lax.optimization_barrier(
        (summed, main.result("output").astype(BF16), main.result("query").astype(BF16))
    )
    gate_grad, up_grad, down_grad = summed
    output_grad, query_grad = sum_rows(output_sum, rows), sum_rows(query_sum, rows)
    in_grad = jnp.concatenate([gate_grad, up_grad], axis=1)
    in_grad = lax.optimization_barrier(in_grad.reshape(units, 2, width))
    return (
        jnp.stack(layer_out),
        input_grad.reshape(rows_here, seg_len, width),
        cache_grad,
        gain_grad,
        query_grad,
        output_grad,
        in_grad.astype(F32),
        down_grad.astype(F32),
    )


def solution(mesh):
    in_specs = (
        P("rows", "seq", None),
        P("rows", "seq", None, None),
        P("rows"),
        P(),
        P("seq", None),
        P("seq", None),
        P("seq", None, None),
        P("seq", None),
        P("rows", "seq", None),
    )
    out_specs = (
        P("rows", "seq", None),
        P("rows", "seq", None),
        P("rows", "seq", None, None),
        P(),
        P("seq", None),
        P("seq", None),
        P("seq", None, None),
        P("seq", None),
    )
    return jax.shard_map(local, mesh=mesh, in_specs=in_specs, out_specs=out_specs, check_vma=False)
```

```python
import jax
import jax.numpy as jnp
from jax import lax
from jax.sharding import PartitionSpec as P

HEADS = 16
HEAD = 128
KV = 4
GROUP = 4
EPS = 1e-05
NEG = -1e30
F32 = jnp.float32
BF16 = jnp.bfloat16


def dot(left, right, dims):
    return lax.dot_general(left, right, (dims, ((), ())), preferred_element_type=F32)


def tie(value, dep):
    if dep is None:
        return value
    return lax.optimization_barrier((value, dep))[0]


def norm_back(grad_normed, scaled, inverse, gain):
    inner = grad_normed * gain
    return inverse * (inner - scaled * jnp.mean(inner * scaled, axis=-1, keepdims=True))


def swap_core(value, seq):
    return lax.ppermute(value, "seq", [(s, s ^ 1) for s in range(seq)])


def ring(value, chips):
    pairs = [(2 * z + c, 2 * ((z + 1) % chips) + c) for z in range(chips) for c in range(2)]
    return lax.ppermute(value, "seq", pairs)


def swap_row(value, rows, mask):
    return lax.ppermute(value, "rows", [(r, r ^ mask) for r in range(rows)])


def ring_gather(own, chips, dep=None):
    got = [tie(own, dep)]
    for _ in range(1, chips):
        got.append(ring(got[-1], chips))
    return [own] + got[:0:-1], got[-2]


def ring_scatter(parts, chips):
    sent = parts[chips - 1]
    for j in range(chips - 2, -1, -1):
        yield sent
        total = ring(sent, chips).astype(F32) + parts[j].astype(F32)
        sent = total.astype(BF16)
    return total


class Lane:
    def __init__(self):
        self.waiting, self.results, self.sent = [], {}, None

    def add(self, name, steps):
        self.waiting.append((name, steps))

    def step(self):
        if self.waiting:
            name, steps = self.waiting[0]
            try:
                sent = next(steps)
                self.sent = sent
                return sent
            except StopIteration as end:
                self.results[name] = end.value
                self.waiting.pop(0)
                return self.step()
        return None

    def result(self, name):
        while name not in self.results:
            self.step()
        return self.results[name]


def beside(value, *lanes):
    for lane in lanes:
        value = tie(value, lane.step())
    return value


def xor_order(value, at):
    shape = value.shape
    value = value.reshape(2, 2, *shape[1:])
    value = jnp.where(at % 2 == 1, value[:, ::-1], value)
    return jnp.where(at // 2 == 1, value[::-1], value).reshape(shape)


def own_order(value, chips, place, core):
    count = value.shape[0]
    value = value.reshape(count, chips, 2, -1)
    value = jnp.where(core == 0, value, value[:, :, ::-1])
    value = jnp.concatenate([value, value], axis=1)
    value = lax.dynamic_slice_in_dim(value, place, chips, axis=1)
    return value.transpose(0, 2, 1, 3).reshape(count, -1)


def index_order(value, chips, place, core):
    count = value.shape[0]
    value = value.reshape(count, 2, chips, -1).transpose(0, 2, 1, 3)
    value = jnp.concatenate([value, value], axis=1)
    value = lax.dynamic_slice_in_dim(value, (chips - place) % chips, chips, axis=1)
    value = jnp.where(core == 0, value, value[:, :, ::-1])
    return value.reshape(count, -1)


class Weight:
    def __init__(self, chips, row_at, order, near=None, far=None, whole=None):
        self.chips, self.row_at, self.order = chips, row_at, order
        self.near, self.far, self.whole = near, far, whole
        self.split = whole is None

    def features(self, value):
        if not self.split:
            out = own_order(dot(value, self.whole, ((1,), (1,))), *self.order)
            half = out.shape[1] // 2
            return [out[:, :half].astype(BF16), out[:, half:].astype(BF16)]
        count = value.shape[0]
        blocks = value.reshape(count, 4, -1).transpose(1, 0, 2)
        blocks = xor_order(blocks, self.row_at)
        out = []
        for near, far in zip(self.near, self.far, strict=True):
            term = jnp.einsum("ktc,kfc->ktf", blocks, far, preferred_element_type=F32)
            term = jnp.sum(term, axis=0).astype(BF16)
            out.append(jnp.concatenate([dot(value, near, ((1,), (1,))).astype(BF16), term], axis=1))
        return out

    def back(self, halves):
        if not self.split:
            value = jnp.concatenate(halves, axis=1)
            return dot(index_order(value, *self.order), self.whole, ((1,), (0,)))
        count = halves[0].shape[0]
        near_sum = far_sum = 0.0
        for part, near, far in zip(halves, self.near, self.far, strict=True):
            depth = near.shape[0]
            near_sum += dot(part[:, :depth], near, ((1,), (0,)))
            far_sum += jnp.einsum("tf,kfc->ktc", part[:, depth:], far, preferred_element_type=F32)
        far_sum = xor_order(far_sum, self.row_at).transpose(1, 0, 2).reshape(count, -1)
        return near_sum + far_sum


def gather_weights(shards, chips, rows, row_at, order):
    seq = 2 * chips
    depth, width = shards[0].shape
    if rows != 4 or depth % 32 or width % 512:
        whole = [lax.all_gather(w, "seq", axis=0, tiled=True) for w in shards]
        return [Weight(chips, row_at, order, whole=w) for w in whole], None
    part = width // rows
    mine = jnp.stack([lax.dynamic_slice_in_dim(w, row_at * part, part, axis=1) for w in shards])
    slots, token = ring_gather(mine, chips)
    first, second = (jnp.stack([v[n] for v in slots[1:]]) for n in range(2))
    first_x = swap_row(first, rows, 1)
    second_y = swap_row(second, rows, 2)
    first_pair = swap_row(jnp.stack([first, first_x]), rows, 2)
    second_pair = swap_row(jnp.stack([second, second_y]), rows, 1)
    pieces = [
        jnp.stack([first, first_x, first_pair[0], first_pair[1]]),
        jnp.stack([second, second_pair[0], second_y, second_pair[1]]),
    ]
    out = []
    for shard, piece in zip(shards, pieces, strict=True):
        far = piece.reshape(rows, (chips - 1) * depth, part)
        far, near = [far, swap_core(far, seq)], [shard, swap_core(shard, seq)]
        out.append(Weight(chips, row_at, order, near=near, far=far))
    return out, token


def scatter_halves(own, sib, got_at, chips):
    got = swap_core(sib, 2 * chips)
    parts = [own(j).astype(F32) + got_at(got, j).astype(F32) for j in range(chips)]
    return (yield from ring_scatter([p.astype(BF16) for p in parts], chips))


def block_of(value, j, chips):
    size = value.shape[0] // chips
    return value[j * size : (j + 1) * size]


def scatter_tokens(part, chips, place, core):
    size = part.shape[0] // (2 * chips)

    def block(j, at):
        start = (2 * ((place + j) % chips) + at) * size
        return lax.dynamic_slice_in_dim(part, start, size, axis=0)

    sib = jnp.concatenate([block(j, 1 - core) for j in range(chips)], axis=0)
    return scatter_halves(
        lambda j: block(j, core), sib, lambda got, j: block_of(got, j, chips), chips
    )


def sum_rows(values, rows, other):
    if rows != 4:
        return [lax.psum(v.astype(BF16), "rows").astype(F32) for v in values], other

    def pair(item, mask):
        return item.astype(F32) + swap_row(item, rows, mask).astype(F32)

    halves = []
    for value in values:
        half = value.shape[0] // 2
        halves.append(pair(value[:half].astype(BF16), 1).astype(BF16))
        halves.append(pair(value[half:].astype(BF16), 2).astype(BF16))
    halves, other = lax.optimization_barrier((halves, other))
    masks = [2, 1] * len(values)
    sums = [pair(h, m) for h, m in zip(halves, masks, strict=True)]
    return [jnp.concatenate(sums[2 * n : 2 * n + 2], axis=0) for n in range(len(values))], other


def sum_all(value, rows, seq):
    mask = 1
    while mask < seq:
        value = value + lax.ppermute(value, "seq", [(s, s ^ mask) for s in range(seq)])
        mask *= 2
    mask = 1
    while mask < rows:
        value = value + swap_row(value, rows, mask)
        mask *= 2
    return value


def local(
    tokens,
    kv_cache,
    lengths,
    norm_gains,
    query_weight,
    output_weight,
    ffn_in_weight,
    down_weight,
    cotangent,
):
    rows_here, seg_len, width = tokens.shape
    seq = lax.axis_size("seq")
    rows = lax.axis_size("rows")
    chips = seq // 2
    seq_at = lax.axis_index("seq")
    row_at = lax.axis_index("rows")
    place, core = seq_at // 2, seq_at % 2
    order = (chips, place, core)
    gain_one, gain_two = norm_gains[0], norm_gains[1]
    query_pos = seq_at * seg_len + jnp.arange(seg_len, dtype=jnp.int32)
    chip_range = jnp.arange(chips, dtype=jnp.int32)
    ring_at = (place + chip_range) % chips
    starts = jnp.concatenate([2 * ring_at + core, 2 * ring_at + 1 - core]) * seg_len

    live = [
        (query_pos < lengths[r]).astype(F32).reshape(seg_len, 1) for r in range(rows_here)
    ]
    grad_out = [cotangent[r].astype(F32) * live[r] for r in range(rows_here)]
    gate_up_weight = jnp.concatenate([ffn_in_weight[:, 0], ffn_in_weight[:, 1]], axis=0)
    (query_proj, output_proj), token = gather_weights(
        (query_weight, output_weight), chips, rows, row_at, order
    )
    cache_own = kv_cache.reshape(rows_here, seg_len, 2, KV, HEAD).transpose(2, 0, 3, 1, 4)
    cache_slots, token = ring_gather(cache_own, chips, dep=token)
    cache_block = jnp.concatenate(cache_slots, axis=3)
    cache_all = jnp.concatenate([cache_block, swap_core(cache_block, seq)], axis=3)
    grad_group = [
        lax.all_gather(tie(g.astype(BF16), token), "seq", axis=0, tiled=True)
        for g in grad_out
    ]
    per = chips // KV

    def to_slots(value):
        value = jnp.repeat(value, per, axis=2) if per > 1 else value
        value = jnp.concatenate([value, value], axis=2)
        return lax.dynamic_slice_in_dim(value, place, chips, axis=2)

    def from_slots(value):
        value = jnp.concatenate([value, value], axis=2)
        value = lax.dynamic_slice_in_dim(value, (chips - place) % chips, chips, axis=2)
        if per > 1:
            shape = value.shape
            value = value.reshape(*shape[:2], KV, per, *shape[3:]).astype(F32).sum(axis=3)
        return value.astype(BF16)

    def to_heads(halves):
        value = jnp.stack([h.reshape(rows_here, seg_len, chips, -1, HEAD) for h in halves])
        value = value.transpose(1, 3, 0, 4, 2, 5)
        return value.reshape(rows_here, chips, -1, HEAD)

    def from_heads(value):
        value = value.reshape(rows_here, chips, 2, -1, seg_len, HEAD).transpose(2, 0, 4, 1, 3, 5)
        value = value.reshape(2, rows_here * seg_len, -1)
        return [value[0], value[1]]

    def heads_dot(spec, left, right):
        return jnp.einsum(spec, left, right, preferred_element_type=F32)

    key_pos = (starts[:, None] + jnp.arange(seg_len, dtype=jnp.int32)).reshape(-1)
    limit = jnp.minimum(query_pos[None], lengths[:, None] - 1)
    limit = jnp.tile(limit, (1, HEADS // chips))
    valid = (key_pos[None, None] <= limit[:, :, None])[:, None]
    scale = HEAD ** (-0.5)

    inputs = tokens.astype(F32).reshape(rows_here * seg_len, width)
    inverse_one = lax.rsqrt(jnp.mean(inputs * inputs, axis=-1, keepdims=True) + EPS)
    normed_one = (inputs * inverse_one * gain_one).astype(BF16)
    query = query_proj.features(normed_one)
    cache_slot = to_slots(cache_all)
    keys, values = cache_slot[0], cache_slot[1]
    query_heads = to_heads(query)
    scores = heads_dot("rjqd,rjkd->rjqk", query_heads, keys) * scale
    scores = jnp.where(valid, scores, NEG)
    best = jnp.max(scores, axis=-1, keepdims=True)
    weights = jnp.exp(scores - best)
    total = jnp.sum(weights, axis=-1, keepdims=True)
    mixed_heads = heads_dot("rjqk,rjkd->rjqd", weights.astype(BF16), values) / total
    lse = best + jnp.log(total)
    mixed = from_heads(mixed_heads.astype(BF16))
    mixed, grad_group[0] = lax.optimization_barrier((mixed, grad_group[0]))
    middle_all = inputs + output_proj.back(mixed)
    inverse_all = lax.rsqrt(jnp.mean(middle_all * middle_all, axis=-1, keepdims=True) + EPS)
    normed_all = (middle_all * inverse_all * gain_two).astype(BF16)
    normed_all, grad_group[1:] = lax.optimization_barrier((normed_all, grad_group[1:]))

    def split(value):
        return [value[r * seg_len : (r + 1) * seg_len] for r in range(rows_here)]

    middle, inverse_two, normed_two = split(middle_all), split(inverse_all), split(normed_all)
    normed_group = [lax.all_gather(n, "seq", axis=0, tiled=True) for n in normed_two]

    main, fill = Lane(), Lane()
    units = down_weight.shape[0]
    hidden, grad_gate_up, ffn_part = [], [], []
    for r in range(rows_here):
        kept = dot(beside(normed_group[r], main), gate_up_weight, ((1,), (1,)))
        gate, upper = kept[:, :units], kept[:, units:]
        sigma = jax.nn.sigmoid(gate)
        grad_hidden = dot(beside(grad_group[r], main), down_weight, ((1,), (1,)))
        hidden.append((gate * sigma * upper).astype(BF16))
        grad_gate = grad_hidden * upper * sigma * (1.0 + gate * (1.0 - sigma))
        grad_up = grad_hidden * gate * sigma
        grad_gate_up.append(jnp.concatenate([grad_gate, grad_up], axis=1).astype(BF16))
        part = dot(beside(grad_gate_up[r], main), gate_up_weight, ((1,), (0,))).astype(BF16)
        ffn_part.append(dot(hidden[r], down_weight, ((1,), (0,))).astype(BF16))
        main.add(("grad", r), scatter_tokens(part, chips, place, core))
        if r == 0:
            fill.add(("ffn", 0), scatter_tokens(ffn_part[0], chips, place, core))

    def over_tokens(left, right, start, size):
        total = 0.0
        for r in range(rows_here):
            part = left[r][:, start : start + size]
            total += dot(part, right[r], ((0,), (0,)))
        return total.astype(BF16)

    gate_part = over_tokens(grad_gate_up, normed_group, 0, units)
    up_part = over_tokens(grad_gate_up, normed_group, units, units)
    down_part = over_tokens(hidden, grad_group, 0, units)
    parts = (gate_part, up_part, down_part)
    summed = lax.psum(parts, "rows")

    grad_middle, gain_two_grad = [], 0.0
    for r in range(rows_here):
        grad_normed_two = main.result(("grad", r))
        if r:
            grad_normed_two, parts = lax.optimization_barrier((grad_normed_two, parts))
        scaled_two = middle[r] * inverse_two[r]
        gain_two_grad += jnp.sum(grad_normed_two * scaled_two, axis=0)
        grad_middle.append(
            grad_out[r] + norm_back(grad_normed_two, scaled_two, inverse_two[r], gain_two)
        )
    for r in range(1, rows_here):
        part = tie(ffn_part[r], grad_middle[-1])
        fill.add(("ffn", r), scatter_tokens(part, chips, place, core))
    grad_middle = jnp.concatenate(grad_middle, axis=0)
    grad_branch = grad_middle.astype(BF16)
    output_part = [dot(half, grad_branch, ((0,), (0,))).astype(BF16) for half in mixed]

    def scatter_rows(parts):
        def take(value, j):
            return block_of(value, j, chips)

        return scatter_halves(lambda j: take(parts[0], j), parts[1], take, chips)

    main.add("output", scatter_rows(output_part))
    grad_heads = to_heads(output_proj.features(tie(grad_branch, output_part[1])))
    grad_heads = beside(grad_heads, main)
    delta = jnp.sum(grad_heads.astype(F32) * mixed_heads, axis=-1, keepdims=True)
    scores = heads_dot("rjqd,rjkd->rjqk", query_heads, keys) * scale
    probs = jnp.where(valid, jnp.exp(scores - lse), 0.0)
    grad_probs = heads_dot("rjqd,rjkd->rjqk", grad_heads, values)
    grad_scores = beside((probs * (grad_probs - delta)).astype(BF16), main)
    query_term = from_heads(
        (heads_dot("rjqk,rjkd->rjqd", grad_scores, keys) * scale).astype(BF16)
    )
    query_term[0] = beside(query_term[0], main)
    grad_keys = heads_dot("rjqk,rjqd->rjkd", grad_scores, query_heads) * scale
    grad_values = heads_dot("rjqk,rjqd->rjkd", probs.astype(BF16), grad_heads)
    cache_part = from_slots(jnp.stack([grad_keys.astype(BF16), grad_values.astype(BF16)]))
    half_len = cache_part.shape[3] // 2

    def positions_of(value, j):
        return value[:, :, :, j * seg_len : (j + 1) * seg_len]

    fill.add(
        "cache",
        scatter_halves(
            lambda j: positions_of(cache_part, j), cache_part[:, :, :, half_len:], positions_of, chips
        ),
    )
    query_part = [dot(half, normed_one, ((0,), (0,))).astype(BF16) for half in query_term]
    main.add("query", scatter_rows(query_part))

    grad_normed_one = query_proj.back(query_term)
    scaled_one = inputs * inverse_one
    gain_one_grad = jnp.sum(grad_normed_one * scaled_one, axis=0)
    input_grad = grad_middle + norm_back(grad_normed_one, scaled_one, inverse_one, gain_one)
    gain_grad = sum_all(jnp.stack([gain_one_grad, gain_two_grad]), rows, seq)

    layer_out = [
        (live[r] * (middle[r] + fill.result(("ffn", r)))).astype(BF16) for r in range(rows_here)
    ]
    cache_grad = fill.result("cache")
    cache_grad = cache_grad.transpose(1, 3, 0, 2, 4).reshape(rows_here, seg_len, 2, KV * HEAD)
    summed, output_sum, query_sum = lax.optimization_barrier(
        (summed, main.result("output").astype(BF16), main.result("query").astype(BF16))
    )
    gate_grad, up_grad, down_grad = summed
    in_grad = jnp.concatenate([gate_grad, up_grad], axis=1)
    (output_grad, query_grad), in_grad = sum_rows([output_sum, query_sum], rows, in_grad)
    in_grad = lax.optimization_barrier(in_grad.reshape(units, 2, width))
    return (
        jnp.stack(layer_out),
        input_grad.reshape(rows_here, seg_len, width),
        cache_grad,
        gain_grad,
        query_grad,
        output_grad,
        in_grad.astype(F32),
        down_grad.astype(F32),
    )


def solution(mesh):
    in_specs = (
        P("rows", "seq", None),
        P("rows", "seq", None, None),
        P("rows"),
        P(),
        P("seq", None),
        P("seq", None),
        P("seq", None, None),
        P("seq", None),
        P("rows", "seq", None),
    )
    out_specs = (
        P("rows", "seq", None),
        P("rows", "seq", None),
        P("rows", "seq", None, None),
        P(),
        P("seq", None),
        P("seq", None),
        P("seq", None, None),
        P("seq", None),
    )
    return jax.shard_map(local, mesh=mesh, in_specs=in_specs, out_specs=out_specs, check_vma=False)
```

```python
import jax
import jax.numpy as jnp
from jax import lax
from jax.sharding import PartitionSpec as P

HEADS = 16
HEAD = 128
KV = 4
GROUP = 4
EPS = 1e-05
NEG = -1e30
F32 = jnp.float32
BF16 = jnp.bfloat16


def dot(left, right, dims):
    return lax.dot_general(left, right, (dims, ((), ())), preferred_element_type=F32)


def tie(value, dep):
    if dep is None:
        return value
    return lax.optimization_barrier((value, dep))[0]


def norm_back(grad_normed, scaled, inverse, gain):
    inner = grad_normed * gain
    return inverse * (inner - scaled * jnp.mean(inner * scaled, axis=-1, keepdims=True))


def swap_core(value, seq):
    return lax.ppermute(value, "seq", [(s, s ^ 1) for s in range(seq)])


def ring(value, chips):
    pairs = [(2 * z + c, 2 * ((z + 1) % chips) + c) for z in range(chips) for c in range(2)]
    return lax.ppermute(value, "seq", pairs)


def swap_row(value, rows, mask):
    return lax.ppermute(value, "rows", [(r, r ^ mask) for r in range(rows)])


def ring_gather(own, chips, dep=None):
    got = [tie(own, dep)]
    for _ in range(1, chips):
        got.append(ring(got[-1], chips))
    return [own] + got[:0:-1], got[-1]


def ring_scatter(parts, chips):
    sent = parts[chips - 1]
    for j in range(chips - 2, -1, -1):
        yield sent
        total = ring(sent, chips).astype(F32) + parts[j].astype(F32)
        sent = total.astype(BF16)
    return total


class Lane:
    def __init__(self):
        self.waiting, self.results, self.sent = [], {}, None

    def add(self, name, steps):
        self.waiting.append((name, steps))

    def step(self):
        if self.waiting:
            name, steps = self.waiting[0]
            try:
                sent = next(steps)
                self.sent = sent
                return sent
            except StopIteration as end:
                self.results[name] = end.value
                self.waiting.pop(0)
                return self.step()
        return None

    def result(self, name):
        while name not in self.results:
            self.step()
        return self.results[name]


def beside(value, *lanes):
    for lane in lanes:
        value = tie(value, lane.step())
    return value


def xor_order(value, at):
    shape = value.shape
    value = value.reshape(2, 2, *shape[1:])
    value = jnp.where(at % 2 == 1, value[:, ::-1], value)
    return jnp.where(at // 2 == 1, value[::-1], value).reshape(shape)


def own_order(value, chips, place, core):
    count = value.shape[0]
    value = value.reshape(count, chips, 2, -1)
    value = jnp.where(core == 0, value, value[:, :, ::-1])
    value = jnp.concatenate([value, value], axis=1)
    value = lax.dynamic_slice_in_dim(value, place, chips, axis=1)
    return value.transpose(0, 2, 1, 3).reshape(count, -1)


def index_order(value, chips, place, core):
    count = value.shape[0]
    value = value.reshape(count, 2, chips, -1).transpose(0, 2, 1, 3)
    value = jnp.concatenate([value, value], axis=1)
    value = lax.dynamic_slice_in_dim(value, (chips - place) % chips, chips, axis=1)
    value = jnp.where(core == 0, value, value[:, :, ::-1])
    return value.reshape(count, -1)


class Weight:
    def __init__(self, shard, chips, rows, row_at, order, dep=None):
        seq = 2 * chips
        self.chips, self.row_at, self.order = chips, row_at, order
        depth, width = shard.shape
        self.depth = depth
        self.split = rows == 4 and depth % 32 == 0 and width % 512 == 0
        if not self.split:
            self.whole = lax.all_gather(shard, "seq", axis=0, tiled=True)
            self.token = dep
            self.steps = [None, None]
            return
        part = width // rows
        half = depth // 2
        mine = lax.dynamic_slice_in_dim(shard, row_at * part, part, axis=1)
        slots, self.token = ring_gather(mine, chips, dep=dep)
        first = jnp.stack([v[:half] for v in slots[1:]])
        second = jnp.stack([v[half:] for v in slots[1:]])
        first_x = swap_row(first, rows, 1)
        second_y = swap_row(second, rows, 2)
        first_pair = swap_row(jnp.stack([first, first_x]), rows, 2)
        second_pair = swap_row(jnp.stack([second, second_y]), rows, 1)
        parts = [first, second, first_x, second_pair[0]]
        parts += [first_pair[0], second_y, first_pair[1], second_pair[1]]
        parts = jnp.concatenate(parts, axis=0).reshape(rows, (chips - 1) * depth, part)
        self.steps = [(first_x, second_y), (first_pair, second_pair)]
        self.far = [parts, swap_core(parts, seq)]
        self.near = [shard, swap_core(shard, seq)]

    def features(self, value, lane=None):
        if not self.split:
            out = own_order(dot(value, self.whole, ((1,), (1,))), *self.order)
            half = out.shape[1] // 2
            return [out[:, :half].astype(BF16), out[:, half:].astype(BF16)]
        count = value.shape[0]
        out = []
        for near, far in zip(self.near, self.far, strict=True):
            if out and lane is not None:
                value = beside(value, lane)
            blocks = value.reshape(count, 4, -1).transpose(1, 0, 2)
            blocks = xor_order(blocks, self.row_at)
            term = jnp.einsum("ktc,kfc->ktf", blocks, far, preferred_element_type=F32)
            term = jnp.sum(term, axis=0).astype(BF16)
            term = term.reshape(count, 2, self.chips - 1, -1).transpose(0, 2, 1, 3)
            term = term.reshape(count, -1)
            out.append(jnp.concatenate([dot(value, near, ((1,), (1,))).astype(BF16), term], axis=1))
        return out

    def back(self, halves):
        if not self.split:
            value = jnp.concatenate(halves, axis=1)
            return dot(index_order(value, *self.order), self.whole, ((1,), (0,)))
        count = halves[0].shape[0]
        near_sum = far_sum = 0.0
        for part, near, far in zip(halves, self.near, self.far, strict=True):
            near_sum += dot(part[:, : self.depth], near, ((1,), (0,)))
            rest = part[:, self.depth :].reshape(count, self.chips - 1, 2, -1)
            rest = rest.transpose(0, 2, 1, 3).reshape(count, -1)
            far_sum += jnp.einsum("tf,kfc->ktc", rest, far, preferred_element_type=F32)
        far_sum = xor_order(far_sum, self.row_at).transpose(1, 0, 2).reshape(count, -1)
        return near_sum + far_sum


def scatter_halves(own, sib, got_at, chips):
    got = swap_core(sib, 2 * chips)
    parts = [own(j).astype(F32) + got_at(got, j).astype(F32) for j in range(chips)]
    return (yield from ring_scatter([p.astype(BF16) for p in parts], chips))


def block_of(value, j, chips):
    size = value.shape[0] // chips
    return value[j * size : (j + 1) * size]


def scatter_tokens(part, chips, place, core):
    size = part.shape[0] // (2 * chips)

    def block(j, at):
        start = (2 * ((place + j) % chips) + at) * size
        return lax.dynamic_slice_in_dim(part, start, size, axis=0)

    sib = jnp.concatenate([block(j, 1 - core) for j in range(chips)], axis=0)
    return scatter_halves(
        lambda j: block(j, core), sib, lambda got, j: block_of(got, j, chips), chips
    )


def sum_rows(values, rows, other):
    if rows != 4:
        return [lax.psum(v.astype(BF16), "rows").astype(F32) for v in values], other

    def pair(item, mask):
        return item.astype(F32) + swap_row(item, rows, mask).astype(F32)

    halves = []
    for value in values:
        half = value.shape[0] // 2
        halves.append(pair(value[:half].astype(BF16), 1).astype(BF16))
        halves.append(pair(value[half:].astype(BF16), 2).astype(BF16))
    halves, other = lax.optimization_barrier((halves, other))
    masks = [2, 1] * len(values)
    sums = [pair(h, m) for h, m in zip(halves, masks, strict=True)]
    return [jnp.concatenate(sums[2 * n : 2 * n + 2], axis=0) for n in range(len(values))], other


def sum_all(value, rows, seq):
    mask = 1
    while mask < seq:
        value = value + lax.ppermute(value, "seq", [(s, s ^ mask) for s in range(seq)])
        mask *= 2
    mask = 1
    while mask < rows:
        value = value + swap_row(value, rows, mask)
        mask *= 2
    return value


def local(
    tokens,
    kv_cache,
    lengths,
    norm_gains,
    query_weight,
    output_weight,
    ffn_in_weight,
    down_weight,
    cotangent,
):
    rows_here, seg_len, width = tokens.shape
    seq = lax.axis_size("seq")
    rows = lax.axis_size("rows")
    chips = seq // 2
    seq_at = lax.axis_index("seq")
    row_at = lax.axis_index("rows")
    place, core = seq_at // 2, seq_at % 2
    order = (chips, place, core)
    gain_one, gain_two = norm_gains[0], norm_gains[1]
    query_pos = seq_at * seg_len + jnp.arange(seg_len, dtype=jnp.int32)
    chip_range = jnp.arange(chips, dtype=jnp.int32)
    ring_at = (place + chip_range) % chips
    starts = jnp.concatenate([2 * ring_at + core, 2 * ring_at + 1 - core]) * seg_len

    live = [
        (query_pos < lengths[r]).astype(F32).reshape(seg_len, 1) for r in range(rows_here)
    ]
    grad_out = [cotangent[r].astype(F32) * live[r] for r in range(rows_here)]
    gate_up_weight = jnp.concatenate([ffn_in_weight[:, 0], ffn_in_weight[:, 1]], axis=0)
    query_proj = Weight(query_weight, chips, rows, row_at, order)
    cache_own = kv_cache.reshape(rows_here, seg_len, 2, KV, HEAD).transpose(2, 0, 3, 1, 4)
    output_proj = Weight(output_weight, chips, rows, row_at, order, dep=query_proj.token)
    cache_slots, token = ring_gather(cache_own, chips, dep=output_proj.token)
    cache_block = jnp.concatenate(cache_slots, axis=3)
    cache_block = tie(cache_block, output_proj.steps[0])
    cache_all = jnp.concatenate([cache_block, swap_core(cache_block, seq)], axis=3)
    grad_group = [
        lax.all_gather(tie(g.astype(BF16), token), "seq", axis=0, tiled=True) for g in grad_out
    ]
    per = chips // KV

    def to_slots(value):
        value = jnp.repeat(value, per, axis=2) if per > 1 else value
        value = jnp.concatenate([value, value], axis=2)
        return lax.dynamic_slice_in_dim(value, place, chips, axis=2)

    def from_slots(value):
        value = jnp.concatenate([value, value], axis=2)
        value = lax.dynamic_slice_in_dim(value, (chips - place) % chips, chips, axis=2)
        if per > 1:
            shape = value.shape
            value = value.reshape(*shape[:2], KV, per, *shape[3:]).astype(F32).sum(axis=3)
        return value.astype(BF16)

    def to_heads(halves):
        value = jnp.stack([h.reshape(rows_here, seg_len, chips, -1, HEAD) for h in halves])
        value = value.transpose(1, 3, 0, 4, 2, 5)
        return value.reshape(rows_here, chips, -1, HEAD)

    def from_heads(value):
        value = value.reshape(rows_here, chips, 2, -1, seg_len, HEAD).transpose(2, 0, 4, 1, 3, 5)
        value = value.reshape(2, rows_here * seg_len, -1)
        return [value[0], value[1]]

    def heads_dot(spec, left, right):
        return jnp.einsum(spec, left, right, preferred_element_type=F32)

    key_pos = (starts[:, None] + jnp.arange(seg_len, dtype=jnp.int32)).reshape(-1)
    limit = jnp.minimum(query_pos[None], lengths[:, None] - 1)
    limit = jnp.tile(limit, (1, HEADS // chips))
    valid = (key_pos[None, None] <= limit[:, :, None])[:, None]
    scale = HEAD ** (-0.5)

    inputs = tokens.astype(F32).reshape(rows_here * seg_len, width)
    inverse_one = lax.rsqrt(jnp.mean(inputs * inputs, axis=-1, keepdims=True) + EPS)
    normed_one = (inputs * inverse_one * gain_one).astype(BF16)
    query = tie(query_proj.features(normed_one), output_proj.steps[1])
    cache_slot = to_slots(cache_all)
    keys, values = cache_slot[0], cache_slot[1]
    query_heads = to_heads(query)
    scores = heads_dot("rjqd,rjkd->rjqk", query_heads, keys) * scale
    scores = jnp.where(valid, scores, NEG)
    best = jnp.max(scores, axis=-1, keepdims=True)
    weights = jnp.exp(scores - best)
    total = jnp.sum(weights, axis=-1, keepdims=True)
    mixed_heads = heads_dot("rjqk,rjkd->rjqd", weights.astype(BF16), values) / total
    lse = best + jnp.log(total)
    mixed = from_heads(mixed_heads.astype(BF16))
    mixed, grad_group[0] = lax.optimization_barrier((mixed, grad_group[0]))
    middle_all = inputs + output_proj.back(mixed)
    inverse_all = lax.rsqrt(jnp.mean(middle_all * middle_all, axis=-1, keepdims=True) + EPS)
    normed_all = (middle_all * inverse_all * gain_two).astype(BF16)
    normed_all, grad_group[1:] = lax.optimization_barrier((normed_all, grad_group[1:]))

    def split(value):
        return [value[r * seg_len : (r + 1) * seg_len] for r in range(rows_here)]

    middle, inverse_two, normed_two = split(middle_all), split(inverse_all), split(normed_all)
    normed_group = [lax.all_gather(n, "seq", axis=0, tiled=True) for n in normed_two]

    main, fill = Lane(), Lane()
    units = down_weight.shape[0]
    hidden, grad_gate_up, grad_part, ffn_part = [], [], [], []
    for r in range(rows_here):
        kept = dot(normed_group[r], gate_up_weight, ((1,), (1,)))
        gate, upper = kept[:, :units], kept[:, units:]
        sigma = jax.nn.sigmoid(gate)
        grad_hidden = dot(beside(grad_group[r], fill), down_weight, ((1,), (1,)))
        hidden.append((gate * sigma * upper).astype(BF16))
        grad_gate = grad_hidden * upper * sigma * (1.0 + gate * (1.0 - sigma))
        grad_up = grad_hidden * gate * sigma
        grad_gate_up.append(jnp.concatenate([grad_gate, grad_up], axis=1).astype(BF16))
        part = dot(beside(grad_gate_up[r], fill), gate_up_weight, ((1,), (0,))).astype(BF16)
        grad_part.append(lax.psum_scatter(part, "seq", scatter_dimension=0, tiled=True))
        ffn_part.append(dot(hidden[r], down_weight, ((1,), (0,))).astype(BF16))
        if r == 0:
            fill.add(("ffn", 0), scatter_tokens(ffn_part[0], chips, place, core))

    def over_tokens(left, right, start, size):
        total = 0.0
        for r in range(rows_here):
            part = left[r][:, start : start + size]
            total += dot(part, right[r], ((0,), (0,)))
        return total.astype(BF16)

    gate_part = over_tokens(grad_gate_up, normed_group, 0, units)
    up_part = over_tokens(grad_gate_up, normed_group, units, units)
    down_part = over_tokens(hidden, grad_group, 0, units)
    parts = (gate_part, up_part, down_part)
    summed = lax.psum(parts, "rows")

    grad_middle, gain_two_grad = [], 0.0
    for r in range(rows_here):
        grad_normed_two = grad_part[r].astype(F32)
        if r:
            grad_normed_two, parts = lax.optimization_barrier((grad_normed_two, parts))
        scaled_two = middle[r] * inverse_two[r]
        gain_two_grad += jnp.sum(grad_normed_two * scaled_two, axis=0)
        grad_middle.append(
            grad_out[r] + norm_back(grad_normed_two, scaled_two, inverse_two[r], gain_two)
        )
    for r in range(1, rows_here):
        part = tie(ffn_part[r], grad_middle[-1])
        fill.add(("ffn", r), scatter_tokens(part, chips, place, core))
    grad_middle = jnp.concatenate(grad_middle, axis=0)
    grad_branch = grad_middle.astype(BF16)
    output_part = [dot(half, grad_branch, ((0,), (0,))).astype(BF16) for half in mixed]

    def scatter_rows(parts):
        def take(value, j):
            return block_of(value, j, chips)

        return scatter_halves(lambda j: take(parts[0], j), parts[1], take, chips)

    main.add("output", scatter_rows(output_part))
    grad_heads = to_heads(output_proj.features(tie(grad_branch, output_part[1]), main))
    delta = jnp.sum(grad_heads.astype(F32) * mixed_heads, axis=-1, keepdims=True)
    scores = heads_dot("rjqd,rjkd->rjqk", query_heads, keys) * scale
    probs = jnp.where(valid, jnp.exp(scores - lse), 0.0)
    grad_probs = heads_dot("rjqd,rjkd->rjqk", grad_heads, values)
    grad_scores = beside((probs * (grad_probs - delta)).astype(BF16), main)
    query_term = from_heads(
        (heads_dot("rjqk,rjkd->rjqd", grad_scores, keys) * scale).astype(BF16)
    )
    query_term[0] = beside(query_term[0], main)
    grad_keys = heads_dot("rjqk,rjqd->rjkd", grad_scores, query_heads) * scale
    grad_values = heads_dot("rjqk,rjqd->rjkd", probs.astype(BF16), grad_heads)
    cache_part = from_slots(jnp.stack([grad_keys.astype(BF16), grad_values.astype(BF16)]))
    half_len = cache_part.shape[3] // 2

    def positions_of(value, j):
        return value[:, :, :, j * seg_len : (j + 1) * seg_len]

    fill.add(
        "cache",
        scatter_halves(
            lambda j: positions_of(cache_part, j), cache_part[:, :, :, half_len:], positions_of, chips
        ),
    )
    query_part = [dot(half, normed_one, ((0,), (0,))).astype(BF16) for half in query_term]
    main.add("query", scatter_rows(query_part))

    grad_normed_one = query_proj.back(query_term)
    scaled_one = inputs * inverse_one
    gain_one_grad = jnp.sum(grad_normed_one * scaled_one, axis=0)
    input_grad = grad_middle + norm_back(grad_normed_one, scaled_one, inverse_one, gain_one)
    gain_grad = jnp.stack([gain_one_grad, gain_two_grad])

    layer_out = [
        (live[r] * (middle[r] + fill.result(("ffn", r)))).astype(BF16) for r in range(rows_here)
    ]
    cache_grad = fill.result("cache")
    cache_grad = cache_grad.transpose(1, 3, 0, 2, 4).reshape(rows_here, seg_len, 2, KV * HEAD)
    sums = (main.result("output").astype(BF16), main.result("query").astype(BF16))
    summed, sums, gain_grad = lax.optimization_barrier((summed, sums, gain_grad))
    gain_grad = sum_all(gain_grad, rows, seq)
    gate_grad, up_grad, down_grad = summed
    in_grad = jnp.concatenate([gate_grad, up_grad], axis=1)
    (output_grad, query_grad), in_grad = sum_rows(sums, rows, in_grad)
    in_grad = lax.optimization_barrier(in_grad.reshape(units, 2, width))
    return (
        jnp.stack(layer_out),
        input_grad.reshape(rows_here, seg_len, width),
        cache_grad,
        gain_grad,
        query_grad,
        output_grad,
        in_grad.astype(F32),
        down_grad.astype(F32),
    )


def solution(mesh):
    in_specs = (
        P("rows", "seq", None),
        P("rows", "seq", None, None),
        P("rows"),
        P(),
        P("seq", None),
        P("seq", None),
        P("seq", None, None),
        P("seq", None),
        P("rows", "seq", None),
    )
    out_specs = (
        P("rows", "seq", None),
        P("rows", "seq", None),
        P("rows", "seq", None, None),
        P(),
        P("seq", None),
        P("seq", None),
        P("seq", None, None),
        P("seq", None),
    )
    return jax.shard_map(local, mesh=mesh, in_specs=in_specs, out_specs=out_specs, check_vma=False)
```

```python
import jax
import jax.numpy as jnp
from jax import lax
from jax.sharding import PartitionSpec as P

HEADS = 16
HEAD = 128
KV = 4
GROUP = 4
EPS = 1e-05
NEG = -1e30
F32 = jnp.float32
BF16 = jnp.bfloat16


def dot(left, right, dims):
    return lax.dot_general(left, right, (dims, ((), ())), preferred_element_type=F32)


def tie(value, dep):
    if dep is None:
        return value
    return lax.optimization_barrier((value, dep))[0]


def norm_back(grad_normed, scaled, inverse, gain):
    inner = grad_normed * gain
    return inverse * (inner - scaled * jnp.mean(inner * scaled, axis=-1, keepdims=True))


def swap_core(value, seq):
    return lax.ppermute(value, "seq", [(s, s ^ 1) for s in range(seq)])


def ring(value, chips):
    pairs = [(2 * z + c, 2 * ((z + 1) % chips) + c) for z in range(chips) for c in range(2)]
    return lax.ppermute(value, "seq", pairs)


def swap_row(value, rows, mask):
    return lax.ppermute(value, "rows", [(r, r ^ mask) for r in range(rows)])


def ring_gather(own, chips, dep=None):
    got = [tie(own, dep)]
    for _ in range(1, chips):
        got.append(ring(got[-1], chips))
    return [own] + got[:0:-1], got[-1]


def ring_scatter(parts, chips):
    sent = parts[chips - 1]
    for j in range(chips - 2, -1, -1):
        yield sent
        total = ring(sent, chips).astype(F32) + parts[j].astype(F32)
        sent = total.astype(BF16)
    return total


class Lane:
    def __init__(self):
        self.waiting, self.results, self.sent = [], {}, None

    def add(self, name, steps):
        self.waiting.append((name, steps))

    def step(self):
        if self.waiting:
            name, steps = self.waiting[0]
            try:
                sent = next(steps)
                self.sent = sent
                return sent
            except StopIteration as end:
                self.results[name] = end.value
                self.waiting.pop(0)
                return self.step()
        return None

    def result(self, name):
        while name not in self.results:
            self.step()
        return self.results[name]


def beside(value, *lanes):
    for lane in lanes:
        value = tie(value, lane.step())
    return value


def xor_order(value, at):
    shape = value.shape
    value = value.reshape(2, 2, *shape[1:])
    value = jnp.where(at % 2 == 1, value[:, ::-1], value)
    return jnp.where(at // 2 == 1, value[::-1], value).reshape(shape)


def own_order(value, chips, place, core):
    count = value.shape[0]
    value = value.reshape(count, chips, 2, -1)
    value = jnp.where(core == 0, value, value[:, :, ::-1])
    value = jnp.concatenate([value, value], axis=1)
    value = lax.dynamic_slice_in_dim(value, place, chips, axis=1)
    return value.transpose(0, 2, 1, 3).reshape(count, -1)


def index_order(value, chips, place, core):
    count = value.shape[0]
    value = value.reshape(count, 2, chips, -1).transpose(0, 2, 1, 3)
    value = jnp.concatenate([value, value], axis=1)
    value = lax.dynamic_slice_in_dim(value, (chips - place) % chips, chips, axis=1)
    value = jnp.where(core == 0, value, value[:, :, ::-1])
    return value.reshape(count, -1)


class Weight:
    def __init__(self, shard, chips, rows, row_at, order, dep=None):
        seq = 2 * chips
        self.chips, self.row_at, self.order = chips, row_at, order
        depth, width = shard.shape
        self.depth = depth
        self.split = rows == 4 and depth % 32 == 0 and width % 512 == 0
        if not self.split:
            self.whole = lax.all_gather(shard, "seq", axis=0, tiled=True)
            self.token = dep
            self.steps = [None, None]
            return
        part = width // rows
        half = part // 2
        mine = lax.dynamic_slice_in_dim(shard, row_at * part, part, axis=1)
        slots, self.token = ring_gather(mine, chips, dep=dep)
        first = jnp.stack([v[:, :half] for v in slots[1:]])
        second = jnp.stack([v[:, half:] for v in slots[1:]])
        first_x = swap_row(first, rows, 1)
        second_y = swap_row(second, rows, 2)
        first_pair = swap_row(jnp.stack([first, first_x]), rows, 2)
        second_pair = swap_row(jnp.stack([second, second_y]), rows, 1)
        parts = [first, second, first_x, second_pair[0]]
        parts += [first_pair[0], second_y, first_pair[1], second_pair[1]]
        parts = jnp.concatenate(parts, axis=0).reshape(rows * 2, (chips - 1) * depth, half)
        self.steps = [(first_x, second_y), (first_pair, second_pair)]
        self.far = [parts, swap_core(parts, seq)]
        self.near = [shard, swap_core(shard, seq)]

    def features(self, value, lane=None):
        if not self.split:
            out = own_order(dot(value, self.whole, ((1,), (1,))), *self.order)
            half = out.shape[1] // 2
            return [out[:, :half].astype(BF16), out[:, half:].astype(BF16)]
        count = value.shape[0]
        out = []
        for near, far in zip(self.near, self.far, strict=True):
            if out and lane is not None:
                value = beside(value, lane)
            blocks = value.reshape(count, 4, 2, -1).transpose(1, 2, 0, 3)
            blocks = xor_order(blocks, self.row_at).reshape(8, count, -1)
            term = jnp.einsum("ktc,kfc->ktf", blocks, far, preferred_element_type=F32)
            term = jnp.sum(term, axis=0).astype(BF16)
            out.append(jnp.concatenate([dot(value, near, ((1,), (1,))).astype(BF16), term], axis=1))
        return out

    def back(self, halves):
        if not self.split:
            value = jnp.concatenate(halves, axis=1)
            return dot(index_order(value, *self.order), self.whole, ((1,), (0,)))
        count = halves[0].shape[0]
        near_sum = far_sum = 0.0
        for part, near, far in zip(halves, self.near, self.far, strict=True):
            near_sum += dot(part[:, : self.depth], near, ((1,), (0,)))
            far_sum += jnp.einsum(
                "tf,kfc->ktc", part[:, self.depth :], far, preferred_element_type=F32
            )
        far_sum = far_sum.reshape(4, 2, count, -1)
        far_sum = xor_order(far_sum, self.row_at).transpose(2, 0, 1, 3).reshape(count, -1)
        return near_sum + far_sum


def scatter_halves(own, sib, got_at, chips):
    got = swap_core(sib, 2 * chips)
    parts = [own(j).astype(F32) + got_at(got, j).astype(F32) for j in range(chips)]
    return (yield from ring_scatter([p.astype(BF16) for p in parts], chips))


def block_of(value, j, chips):
    size = value.shape[0] // chips
    return value[j * size : (j + 1) * size]


def scatter_tokens(part, chips, place, core):
    size = part.shape[0] // (2 * chips)

    def block(j, at):
        start = (2 * ((place + j) % chips) + at) * size
        return lax.dynamic_slice_in_dim(part, start, size, axis=0)

    sib = jnp.concatenate([block(j, 1 - core) for j in range(chips)], axis=0)
    return scatter_halves(
        lambda j: block(j, core), sib, lambda got, j: block_of(got, j, chips), chips
    )


def sum_rows(values, rows, other):
    if rows != 4:
        return [lax.psum(v.astype(BF16), "rows").astype(F32) for v in values], other

    def pair(item, mask):
        return item.astype(F32) + swap_row(item, rows, mask).astype(F32)

    halves = []
    for value in values:
        half = value.shape[0] // 2
        halves.append(pair(value[:half].astype(BF16), 1).astype(BF16))
        halves.append(pair(value[half:].astype(BF16), 2).astype(BF16))
    halves, other = lax.optimization_barrier((halves, other))
    masks = [2, 1] * len(values)
    sums = [pair(h, m) for h, m in zip(halves, masks, strict=True)]
    return [jnp.concatenate(sums[2 * n : 2 * n + 2], axis=0) for n in range(len(values))], other


def sum_all(value, rows, seq):
    mask = 1
    while mask < seq:
        value = value + lax.ppermute(value, "seq", [(s, s ^ mask) for s in range(seq)])
        mask *= 2
    mask = 1
    while mask < rows:
        value = value + swap_row(value, rows, mask)
        mask *= 2
    return value


def local(
    tokens,
    kv_cache,
    lengths,
    norm_gains,
    query_weight,
    output_weight,
    ffn_in_weight,
    down_weight,
    cotangent,
):
    rows_here, seg_len, width = tokens.shape
    seq = lax.axis_size("seq")
    rows = lax.axis_size("rows")
    chips = seq // 2
    seq_at = lax.axis_index("seq")
    row_at = lax.axis_index("rows")
    place, core = seq_at // 2, seq_at % 2
    order = (chips, place, core)
    gain_one, gain_two = norm_gains[0], norm_gains[1]
    query_pos = seq_at * seg_len + jnp.arange(seg_len, dtype=jnp.int32)
    chip_range = jnp.arange(chips, dtype=jnp.int32)
    ring_at = (place + chip_range) % chips
    starts = jnp.concatenate([2 * ring_at + core, 2 * ring_at + 1 - core]) * seg_len

    live = [
        (query_pos < lengths[r]).astype(F32).reshape(seg_len, 1) for r in range(rows_here)
    ]
    grad_out = [cotangent[r].astype(F32) * live[r] for r in range(rows_here)]
    gate_up_weight = jnp.concatenate([ffn_in_weight[:, 0], ffn_in_weight[:, 1]], axis=0)
    query_proj = Weight(query_weight, chips, rows, row_at, order)
    cache_own = kv_cache.reshape(rows_here, seg_len, 2, KV, HEAD).transpose(2, 0, 3, 1, 4)
    output_proj = Weight(output_weight, chips, rows, row_at, order, dep=query_proj.token)
    cache_slots, token = ring_gather(cache_own, chips, dep=output_proj.token)
    cache_block = jnp.concatenate(cache_slots, axis=3)
    cache_block = tie(cache_block, output_proj.steps[0])
    cache_all = jnp.concatenate([cache_block, swap_core(cache_block, seq)], axis=3)
    grad_group = [
        lax.all_gather(tie(g.astype(BF16), token), "seq", axis=0, tiled=True) for g in grad_out
    ]
    per = chips // KV

    def to_slots(value):
        value = jnp.repeat(value, per, axis=2) if per > 1 else value
        value = jnp.concatenate([value, value], axis=2)
        return lax.dynamic_slice_in_dim(value, place, chips, axis=2)

    def from_slots(value):
        value = jnp.concatenate([value, value], axis=2)
        value = lax.dynamic_slice_in_dim(value, (chips - place) % chips, chips, axis=2)
        if per > 1:
            shape = value.shape
            value = value.reshape(*shape[:2], KV, per, *shape[3:]).astype(F32).sum(axis=3)
        return value.astype(BF16)

    def to_heads(halves):
        value = jnp.stack([h.reshape(rows_here, seg_len, chips, -1, HEAD) for h in halves])
        value = value.transpose(1, 3, 0, 4, 2, 5)
        return value.reshape(rows_here, chips, -1, HEAD)

    def from_heads(value):
        value = value.reshape(rows_here, chips, 2, -1, seg_len, HEAD).transpose(2, 0, 4, 1, 3, 5)
        value = value.reshape(2, rows_here * seg_len, -1)
        return [value[0], value[1]]

    def heads_dot(spec, left, right):
        return jnp.einsum(spec, left, right, preferred_element_type=F32)

    key_pos = (starts[:, None] + jnp.arange(seg_len, dtype=jnp.int32)).reshape(-1)
    limit = jnp.minimum(query_pos[None], lengths[:, None] - 1)
    limit = jnp.tile(limit, (1, HEADS // chips))
    valid = (key_pos[None, None] <= limit[:, :, None])[:, None]
    scale = HEAD ** (-0.5)

    inputs = tokens.astype(F32).reshape(rows_here * seg_len, width)
    inverse_one = lax.rsqrt(jnp.mean(inputs * inputs, axis=-1, keepdims=True) + EPS)
    normed_one = (inputs * inverse_one * gain_one).astype(BF16)
    query = tie(query_proj.features(normed_one), output_proj.steps[1])
    cache_slot = to_slots(cache_all)
    keys, values = cache_slot[0], cache_slot[1]
    query_heads = to_heads(query)
    scores = heads_dot("rjqd,rjkd->rjqk", query_heads, keys) * scale
    scores = jnp.where(valid, scores, NEG)
    best = jnp.max(scores, axis=-1, keepdims=True)
    weights = jnp.exp(scores - best)
    total = jnp.sum(weights, axis=-1, keepdims=True)
    mixed_heads = heads_dot("rjqk,rjkd->rjqd", weights.astype(BF16), values) / total
    lse = best + jnp.log(total)
    mixed = from_heads(mixed_heads.astype(BF16))
    mixed, grad_group[0] = lax.optimization_barrier((mixed, grad_group[0]))
    middle_all = inputs + output_proj.back(mixed)
    inverse_all = lax.rsqrt(jnp.mean(middle_all * middle_all, axis=-1, keepdims=True) + EPS)
    normed_all = (middle_all * inverse_all * gain_two).astype(BF16)
    normed_all, grad_group[1:] = lax.optimization_barrier((normed_all, grad_group[1:]))

    def split(value):
        return [value[r * seg_len : (r + 1) * seg_len] for r in range(rows_here)]

    middle, inverse_two, normed_two = split(middle_all), split(inverse_all), split(normed_all)
    normed_group = [lax.all_gather(n, "seq", axis=0, tiled=True) for n in normed_two]

    main, fill = Lane(), Lane()
    units = down_weight.shape[0]
    hidden, grad_gate_up, grad_part, ffn_part = [], [], [], []
    for r in range(rows_here):
        kept = dot(normed_group[r], gate_up_weight, ((1,), (1,)))
        gate, upper = kept[:, :units], kept[:, units:]
        sigma = jax.nn.sigmoid(gate)
        grad_hidden = dot(beside(grad_group[r], fill), down_weight, ((1,), (1,)))
        hidden.append((gate * sigma * upper).astype(BF16))
        grad_gate = grad_hidden * upper * sigma * (1.0 + gate * (1.0 - sigma))
        grad_up = grad_hidden * gate * sigma
        grad_gate_up.append(jnp.concatenate([grad_gate, grad_up], axis=1).astype(BF16))
        part = dot(beside(grad_gate_up[r], fill), gate_up_weight, ((1,), (0,))).astype(BF16)
        if r + 1 < rows_here:
            part, normed_group[r + 1] = lax.optimization_barrier((part, normed_group[r + 1]))
        grad_part.append(lax.psum_scatter(part, "seq", scatter_dimension=0, tiled=True))
        ffn_part.append(dot(hidden[r], down_weight, ((1,), (0,))).astype(BF16))
        if r == 0:
            fill.add(("ffn", 0), scatter_tokens(ffn_part[0], chips, place, core))

    def over_tokens(left, right):
        terms = [dot(a, b, ((0,), (0,))) for a, b in zip(left, right, strict=True)]
        return sum(terms).astype(BF16)

    for r in range(rows_here - 1):
        grad_part[r], grad_gate_up[-1], hidden[-1] = lax.optimization_barrier(
            (grad_part[r], grad_gate_up[-1], hidden[-1])
        )
    in_part = over_tokens(grad_gate_up, normed_group)
    down_part = over_tokens(hidden, grad_group)
    parts = (in_part, down_part)
    summed = lax.psum(parts, "rows")

    grad_middle, gain_two_grad = [], 0.0
    for r in range(rows_here):
        grad_normed_two = grad_part[r].astype(F32)
        if r:
            grad_normed_two, parts = lax.optimization_barrier((grad_normed_two, parts))
        scaled_two = middle[r] * inverse_two[r]
        gain_two_grad += jnp.sum(grad_normed_two * scaled_two, axis=0)
        grad_middle.append(
            grad_out[r] + norm_back(grad_normed_two, scaled_two, inverse_two[r], gain_two)
        )
    grad_middle = jnp.concatenate(grad_middle, axis=0)
    grad_branch = grad_middle.astype(BF16)
    output_part = [dot(half, grad_branch, ((0,), (0,))).astype(BF16) for half in mixed]

    def scatter_rows(parts):
        def take(value, j):
            return block_of(value, j, chips)

        return scatter_halves(lambda j: take(parts[0], j), parts[1], take, chips)

    main.add("output", scatter_rows(output_part))
    grad_heads = to_heads(output_proj.features(tie(grad_branch, output_part[1]), main))
    delta = jnp.sum(grad_heads.astype(F32) * mixed_heads, axis=-1, keepdims=True)
    scores = heads_dot("rjqd,rjkd->rjqk", query_heads, keys) * scale
    probs = jnp.where(valid, jnp.exp(scores - lse), 0.0)
    grad_probs = heads_dot("rjqd,rjkd->rjqk", grad_heads, values)
    grad_scores = beside((probs * (grad_probs - delta)).astype(BF16), main)
    for r in range(1, rows_here):
        part, grad_scores = lax.optimization_barrier((ffn_part[r], grad_scores))
        fill.add(("ffn", r), scatter_tokens(part, chips, place, core))
    query_term = from_heads(
        (heads_dot("rjqk,rjkd->rjqd", grad_scores, keys) * scale).astype(BF16)
    )
    query_term[0] = beside(query_term[0], main)
    grad_keys = heads_dot("rjqk,rjqd->rjkd", grad_scores, query_heads) * scale
    grad_values = heads_dot("rjqk,rjqd->rjkd", probs.astype(BF16), grad_heads)
    cache_part = from_slots(jnp.stack([grad_keys.astype(BF16), grad_values.astype(BF16)]))
    half_len = cache_part.shape[3] // 2

    def positions_of(value, j):
        return value[:, :, :, j * seg_len : (j + 1) * seg_len]

    fill.add(
        "cache",
        scatter_halves(
            lambda j: positions_of(cache_part, j), cache_part[:, :, :, half_len:], positions_of, chips
        ),
    )
    query_part = [dot(half, normed_one, ((0,), (0,))).astype(BF16) for half in query_term]
    main.add("query", scatter_rows(query_part))

    grad_normed_one = query_proj.back(query_term)
    scaled_one = inputs * inverse_one
    gain_one_grad = jnp.sum(grad_normed_one * scaled_one, axis=0)
    input_grad = grad_middle + norm_back(grad_normed_one, scaled_one, inverse_one, gain_one)
    gain_grad = jnp.stack([gain_one_grad, gain_two_grad])

    layer_out = [
        (live[r] * (middle[r] + fill.result(("ffn", r)))).astype(BF16) for r in range(rows_here)
    ]
    cache_grad = fill.result("cache")
    cache_grad = cache_grad.transpose(1, 3, 0, 2, 4).reshape(rows_here, seg_len, 2, KV * HEAD)
    summed, output_sum = lax.optimization_barrier((summed, main.result("output").astype(BF16)))
    in_grad, down_grad = summed
    (output_grad,), in_grad = sum_rows([output_sum], rows, in_grad)
    in_grad = in_grad.reshape(2, units, width).transpose(1, 0, 2)
    in_grad = lax.optimization_barrier(in_grad)
    query_sum, gain_grad = lax.optimization_barrier(
        (main.result("query").astype(BF16), gain_grad)
    )
    gain_grad = sum_all(gain_grad, rows, seq)
    (query_grad,), _ = sum_rows([query_sum], rows, ())
    return (
        jnp.stack(layer_out),
        input_grad.reshape(rows_here, seg_len, width),
        cache_grad,
        gain_grad,
        query_grad,
        output_grad,
        in_grad.astype(F32),
        down_grad.astype(F32),
    )


def solution(mesh):
    in_specs = (
        P("rows", "seq", None),
        P("rows", "seq", None, None),
        P("rows"),
        P(),
        P("seq", None),
        P("seq", None),
        P("seq", None, None),
        P("seq", None),
        P("rows", "seq", None),
    )
    out_specs = (
        P("rows", "seq", None),
        P("rows", "seq", None),
        P("rows", "seq", None, None),
        P(),
        P("seq", None),
        P("seq", None),
        P("seq", None, None),
        P("seq", None),
    )
    return jax.shard_map(local, mesh=mesh, in_specs=in_specs, out_specs=out_specs, check_vma=False)
```

```python
import jax
import jax.numpy as jnp
from jax import lax
from jax.sharding import PartitionSpec as P

HEADS = 16
HEAD = 128
KV = 4
GROUP = 4
EPS = 1e-05
NEG = -1e30
F32 = jnp.float32
BF16 = jnp.bfloat16


def dot(left, right, dims):
    return lax.dot_general(left, right, (dims, ((), ())), preferred_element_type=F32)


def tie(value, dep):
    if dep is None:
        return value
    return lax.optimization_barrier((value, dep))[0]


def norm_back(grad_normed, scaled, inverse, gain):
    inner = grad_normed * gain
    return inverse * (inner - scaled * jnp.mean(inner * scaled, axis=-1, keepdims=True))


def swap_core(value, seq):
    return lax.ppermute(value, "seq", [(s, s ^ 1) for s in range(seq)])


def ring(value, chips):
    pairs = [(2 * z + c, 2 * ((z + 1) % chips) + c) for z in range(chips) for c in range(2)]
    return lax.ppermute(value, "seq", pairs)


def swap_row(value, rows, mask):
    return lax.ppermute(value, "rows", [(r, r ^ mask) for r in range(rows)])


def ring_gather(own, chips, dep=None):
    got = [tie(own, dep)]
    for _ in range(1, chips):
        got.append(ring(got[-1], chips))
    return [own] + got[:0:-1], got[-1]


def ring_scatter(parts, chips):
    sent = parts[chips - 1]
    for j in range(chips - 2, -1, -1):
        yield sent
        total = ring(sent, chips).astype(F32) + parts[j].astype(F32)
        sent = total.astype(BF16)
    return total


class Lane:
    def __init__(self):
        self.waiting, self.results, self.sent = [], {}, None

    def add(self, name, steps):
        self.waiting.append((name, steps))

    def step(self):
        if self.waiting:
            name, steps = self.waiting[0]
            try:
                sent = next(steps)
                self.sent = sent
                return sent
            except StopIteration as end:
                self.results[name] = end.value
                self.waiting.pop(0)
                return self.step()
        return None

    def result(self, name):
        while name not in self.results:
            self.step()
        return self.results[name]


def beside(value, *lanes):
    for lane in lanes:
        value = tie(value, lane.step())
    return value


def xor_order(value, at):
    shape = value.shape
    value = value.reshape(2, 2, *shape[1:])
    value = jnp.where(at % 2 == 1, value[:, ::-1], value)
    return jnp.where(at // 2 == 1, value[::-1], value).reshape(shape)


def own_order(value, chips, place, core):
    count = value.shape[0]
    value = value.reshape(count, chips, 2, -1)
    value = jnp.where(core == 0, value, value[:, :, ::-1])
    value = jnp.concatenate([value, value], axis=1)
    value = lax.dynamic_slice_in_dim(value, place, chips, axis=1)
    return value.transpose(0, 2, 1, 3).reshape(count, -1)


def index_order(value, chips, place, core):
    count = value.shape[0]
    value = value.reshape(count, 2, chips, -1).transpose(0, 2, 1, 3)
    value = jnp.concatenate([value, value], axis=1)
    value = lax.dynamic_slice_in_dim(value, (chips - place) % chips, chips, axis=1)
    value = jnp.where(core == 0, value, value[:, :, ::-1])
    return value.reshape(count, -1)


class Weight:
    def __init__(self, shard, chips, rows, row_at, order, dep=None):
        seq = 2 * chips
        self.chips, self.row_at, self.order = chips, row_at, order
        depth, width = shard.shape
        self.depth = depth
        self.split = rows == 4 and depth % 32 == 0 and width % 512 == 0
        if not self.split:
            self.whole = lax.all_gather(shard, "seq", axis=0, tiled=True)
            self.token = dep
            self.steps = [None, None]
            return
        part = width // rows
        half = part // 2
        mine = lax.dynamic_slice_in_dim(shard, row_at * part, part, axis=1)
        slots, self.token = ring_gather(mine, chips, dep=dep)
        first = jnp.stack([v[:, :half] for v in slots[1:]])
        second = jnp.stack([v[:, half:] for v in slots[1:]])
        first_x = swap_row(first, rows, 1)
        second_y = swap_row(second, rows, 2)
        first_pair = swap_row(jnp.stack([first, first_x]), rows, 2)
        second_pair = swap_row(jnp.stack([second, second_y]), rows, 1)
        parts = [first, second, first_x, second_pair[0]]
        parts += [first_pair[0], second_y, first_pair[1], second_pair[1]]
        parts = jnp.concatenate(parts, axis=0).reshape(rows * 2, (chips - 1) * depth, half)
        self.steps = [(first_x, second_y), (first_pair, second_pair)]
        self.far = [parts, swap_core(parts, seq)]
        self.near = [shard, swap_core(shard, seq)]

    def features(self, value, lane=None):
        if not self.split:
            out = own_order(dot(value, self.whole, ((1,), (1,))), *self.order)
            half = out.shape[1] // 2
            return [out[:, :half].astype(BF16), out[:, half:].astype(BF16)]
        count = value.shape[0]
        out = []
        for near, far in zip(self.near, self.far, strict=True):
            if out and lane is not None:
                value = beside(value, lane)
            blocks = value.reshape(count, 4, 2, -1).transpose(1, 2, 0, 3)
            blocks = xor_order(blocks, self.row_at).reshape(8, count, -1)
            term = jnp.einsum("ktc,kfc->ktf", blocks, far, preferred_element_type=F32)
            term = jnp.sum(term, axis=0).astype(BF16)
            out.append(jnp.concatenate([dot(value, near, ((1,), (1,))).astype(BF16), term], axis=1))
        return out

    def back(self, halves):
        if not self.split:
            value = jnp.concatenate(halves, axis=1)
            return dot(index_order(value, *self.order), self.whole, ((1,), (0,)))
        count = halves[0].shape[0]
        near_sum = far_sum = 0.0
        for part, near, far in zip(halves, self.near, self.far, strict=True):
            near_sum += dot(part[:, : self.depth], near, ((1,), (0,)))
            far_sum += jnp.einsum(
                "tf,kfc->ktc", part[:, self.depth :], far, preferred_element_type=F32
            )
        far_sum = xor_order(far_sum.reshape(4, 2, count, -1), self.row_at)
        far_sum = jnp.concatenate([far_sum[k, h] for k in range(4) for h in range(2)], axis=1)
        return near_sum + far_sum


def scatter_halves(own, sib, got_at, chips):
    got = swap_core(sib, 2 * chips)
    parts = [own(j).astype(F32) + got_at(got, j).astype(F32) for j in range(chips)]
    return (yield from ring_scatter([p.astype(BF16) for p in parts], chips))


def block_of(value, j, chips):
    size = value.shape[0] // chips
    return value[j * size : (j + 1) * size]


def scatter_tokens(part, chips, place, core):
    size = part.shape[0] // (2 * chips)

    def block(j, at):
        start = (2 * ((place + j) % chips) + at) * size
        return lax.dynamic_slice_in_dim(part, start, size, axis=0)

    sib = jnp.concatenate([block(j, 1 - core) for j in range(chips)], axis=0)
    return scatter_halves(
        lambda j: block(j, core), sib, lambda got, j: block_of(got, j, chips), chips
    )


def sum_rows(values, rows, other):
    if rows != 4:
        return [lax.psum(v.astype(BF16), "rows").astype(F32) for v in values], other

    def pair(item, mask):
        return item.astype(F32) + swap_row(item, rows, mask).astype(F32)

    halves = []
    for value in values:
        half = value.shape[0] // 2
        halves.append(pair(value[:half].astype(BF16), 1).astype(BF16))
        halves.append(pair(value[half:].astype(BF16), 2).astype(BF16))
    halves, other = lax.optimization_barrier((halves, other))
    masks = [2, 1] * len(values)
    sums = [pair(h, m) for h, m in zip(halves, masks, strict=True)]
    return [jnp.concatenate(sums[2 * n : 2 * n + 2], axis=0) for n in range(len(values))], other


def sum_all(value, rows, seq):
    mask = 1
    while mask < seq:
        value = value + lax.ppermute(value, "seq", [(s, s ^ mask) for s in range(seq)])
        mask *= 2
    mask = 1
    while mask < rows:
        value = value + swap_row(value, rows, mask)
        mask *= 2
    return value


def local(
    tokens,
    kv_cache,
    lengths,
    norm_gains,
    query_weight,
    output_weight,
    ffn_in_weight,
    down_weight,
    cotangent,
):
    rows_here, seg_len, width = tokens.shape
    seq = lax.axis_size("seq")
    rows = lax.axis_size("rows")
    chips = seq // 2
    seq_at = lax.axis_index("seq")
    row_at = lax.axis_index("rows")
    place, core = seq_at // 2, seq_at % 2
    order = (chips, place, core)
    gain_one, gain_two = norm_gains[0], norm_gains[1]
    query_pos = seq_at * seg_len + jnp.arange(seg_len, dtype=jnp.int32)
    chip_range = jnp.arange(chips, dtype=jnp.int32)
    ring_at = (place + chip_range) % chips
    starts = jnp.concatenate([2 * ring_at + core, 2 * ring_at + 1 - core]) * seg_len

    live = [
        (query_pos < lengths[r]).astype(F32).reshape(seg_len, 1) for r in range(rows_here)
    ]
    grad_out = [cotangent[r].astype(F32) * live[r] for r in range(rows_here)]
    gate_up_weight = jnp.concatenate([ffn_in_weight[:, 0], ffn_in_weight[:, 1]], axis=0)
    query_proj = Weight(query_weight, chips, rows, row_at, order)
    cache_own = kv_cache.reshape(rows_here, seg_len, 2, KV, HEAD).transpose(2, 0, 3, 1, 4)
    output_proj = Weight(output_weight, chips, rows, row_at, order, dep=query_proj.token)
    cache_slots, token = ring_gather(cache_own, chips, dep=output_proj.token)
    cache_block = jnp.concatenate(cache_slots, axis=3)
    cache_block = tie(cache_block, output_proj.steps[0])
    cache_all = jnp.concatenate([cache_block, swap_core(cache_block, seq)], axis=3)
    grad_group = [
        lax.all_gather(tie(g.astype(BF16), token), "seq", axis=0, tiled=True) for g in grad_out
    ]
    per = chips // KV

    def to_slots(value):
        value = jnp.repeat(value, per, axis=2) if per > 1 else value
        value = jnp.concatenate([value, value], axis=2)
        return lax.dynamic_slice_in_dim(value, place, chips, axis=2)

    def from_slots(value):
        value = jnp.concatenate([value, value], axis=2)
        value = lax.dynamic_slice_in_dim(value, (chips - place) % chips, chips, axis=2)
        if per > 1:
            shape = value.shape
            value = value.reshape(*shape[:2], KV, per, *shape[3:]).astype(F32).sum(axis=3)
        return value.astype(BF16)

    def to_heads(halves):
        value = jnp.stack([h.reshape(rows_here, seg_len, chips, -1, HEAD) for h in halves])
        value = value.transpose(1, 3, 0, 4, 2, 5)
        return value.reshape(rows_here, chips, -1, HEAD)

    def from_heads(value):
        value = value.reshape(rows_here, chips, 2, -1, seg_len, HEAD).transpose(2, 0, 4, 1, 3, 5)
        value = value.reshape(2, rows_here * seg_len, -1)
        return [value[0], value[1]]

    def heads_dot(spec, left, right):
        return jnp.einsum(spec, left, right, preferred_element_type=F32)

    key_pos = (starts[:, None] + jnp.arange(seg_len, dtype=jnp.int32)).reshape(-1)
    limit = jnp.minimum(query_pos[None], lengths[:, None] - 1)
    limit = jnp.tile(limit, (1, HEADS // chips))
    valid = (key_pos[None, None] <= limit[:, :, None])[:, None]
    scale = HEAD ** (-0.5)

    inputs = tokens.astype(F32).reshape(rows_here * seg_len, width)
    inverse_one = lax.rsqrt(jnp.mean(inputs * inputs, axis=-1, keepdims=True) + EPS)
    normed_one = (inputs * inverse_one * gain_one).astype(BF16)
    query = query_proj.features(normed_one)
    cache_slot = to_slots(cache_all)
    keys, values = cache_slot[0], cache_slot[1]
    query_heads = to_heads(query)
    scores = heads_dot("rjqd,rjkd->rjqk", query_heads, keys) * scale
    scores = jnp.where(valid, scores, NEG)
    best = tie(jnp.max(scores, axis=-1, keepdims=True), output_proj.steps[1])
    weights = jnp.exp(scores - best)
    total = jnp.sum(weights, axis=-1, keepdims=True)
    mixed_heads = heads_dot("rjqk,rjkd->rjqd", weights.astype(BF16), values) / total
    lse = best + jnp.log(total)
    mixed = from_heads(mixed_heads.astype(BF16))
    mixed, grad_group[0] = lax.optimization_barrier((mixed, grad_group[0]))
    middle_all = inputs + output_proj.back(mixed)
    inverse_all = lax.rsqrt(jnp.mean(middle_all * middle_all, axis=-1, keepdims=True) + EPS)
    normed_all = (middle_all * inverse_all * gain_two).astype(BF16)
    normed_all, grad_group[1:] = lax.optimization_barrier((normed_all, grad_group[1:]))

    def split(value):
        return [value[r * seg_len : (r + 1) * seg_len] for r in range(rows_here)]

    middle, inverse_two, normed_two = split(middle_all), split(inverse_all), split(normed_all)
    normed_group = [lax.all_gather(n, "seq", axis=0, tiled=True) for n in normed_two]

    main, fill = Lane(), Lane()
    units = down_weight.shape[0]
    hidden, grad_gate_up, grad_part, ffn_part = [], [], [], []
    for r in range(rows_here):
        kept = dot(normed_group[r], gate_up_weight, ((1,), (1,)))
        gate, upper = kept[:, :units], kept[:, units:]
        sigma = jax.nn.sigmoid(gate)
        grad_hidden = dot(beside(grad_group[r], fill), down_weight, ((1,), (1,)))
        hidden.append((gate * sigma * upper).astype(BF16))
        grad_gate = grad_hidden * upper * sigma * (1.0 + gate * (1.0 - sigma))
        grad_up = grad_hidden * gate * sigma
        grad_gate_up.append(jnp.concatenate([grad_gate, grad_up], axis=1).astype(BF16))
        part = dot(beside(grad_gate_up[r], fill), gate_up_weight, ((1,), (0,))).astype(BF16)
        if r + 1 < rows_here:
            part, normed_group[r + 1] = lax.optimization_barrier((part, normed_group[r + 1]))
        grad_part.append(lax.psum_scatter(part, "seq", scatter_dimension=0, tiled=True))
        ffn_part.append(dot(hidden[r], down_weight, ((1,), (0,))).astype(BF16))

    def over_tokens(left, right):
        terms = [dot(a, b, ((0,), (0,))) for a, b in zip(left, right, strict=True)]
        return sum(terms).astype(BF16)

    for r in range(rows_here - 1):
        grad_part[r], grad_gate_up[-1], hidden[-1] = lax.optimization_barrier(
            (grad_part[r], grad_gate_up[-1], hidden[-1])
        )
    in_part = over_tokens(grad_gate_up, normed_group)
    down_part = over_tokens(hidden, grad_group)
    in_part, ffn_part[0] = lax.optimization_barrier((in_part, ffn_part[0]))
    fill.add(("ffn", 0), scatter_tokens(ffn_part[0], chips, place, core))
    parts = (in_part, down_part)
    summed = lax.psum(parts, "rows")

    grad_middle, gain_two_grad = [], 0.0
    for r in range(rows_here):
        grad_normed_two = grad_part[r].astype(F32)
        if r:
            grad_normed_two, parts = lax.optimization_barrier((grad_normed_two, parts))
        scaled_two = middle[r] * inverse_two[r]
        gain_two_grad += jnp.sum(grad_normed_two * scaled_two, axis=0)
        grad_middle.append(
            grad_out[r] + norm_back(grad_normed_two, scaled_two, inverse_two[r], gain_two)
        )
    for r in range(1, rows_here):
        part = tie(ffn_part[r], grad_middle[-1])
        fill.add(("ffn", r), scatter_tokens(part, chips, place, core))
    grad_middle = jnp.concatenate(grad_middle, axis=0)
    grad_branch = grad_middle.astype(BF16)
    output_part = [dot(half, grad_branch, ((0,), (0,))).astype(BF16) for half in mixed]

    def scatter_rows(parts):
        def take(value, j):
            return block_of(value, j, chips)

        return scatter_halves(lambda j: take(parts[0], j), parts[1], take, chips)

    main.add("output", scatter_rows(output_part))
    grad_heads = to_heads(output_proj.features(tie(grad_branch, output_part[1]), main))
    grad_heads = beside(grad_heads, main, fill)
    delta = jnp.sum(grad_heads.astype(F32) * mixed_heads, axis=-1, keepdims=True)
    scores = heads_dot("rjqd,rjkd->rjqk", query_heads, keys) * scale
    probs = jnp.where(valid, jnp.exp(scores - lse), 0.0)
    grad_probs = heads_dot("rjqd,rjkd->rjqk", grad_heads, values)
    grad_scores = beside((probs * (grad_probs - delta)).astype(BF16), main, fill)
    query_term = from_heads(
        (heads_dot("rjqk,rjkd->rjqd", grad_scores, keys) * scale).astype(BF16)
    )
    grad_keys = heads_dot("rjqk,rjqd->rjkd", grad_scores, query_heads) * scale
    grad_values = heads_dot("rjqk,rjqd->rjkd", probs.astype(BF16), grad_heads)
    cache_part = from_slots(jnp.stack([grad_keys.astype(BF16), grad_values.astype(BF16)]))
    half_len = cache_part.shape[3] // 2

    def positions_of(value, j):
        return value[:, :, :, j * seg_len : (j + 1) * seg_len]

    fill.add(
        "cache",
        scatter_halves(
            lambda j: positions_of(cache_part, j), cache_part[:, :, :, half_len:], positions_of, chips
        ),
    )
    query_part = [dot(half, normed_one, ((0,), (0,))).astype(BF16) for half in query_term]
    main.add("query", scatter_rows(query_part))

    grad_normed_one = query_proj.back(query_term)
    scaled_one = inputs * inverse_one
    gain_one_grad = jnp.sum(grad_normed_one * scaled_one, axis=0)
    input_grad = grad_middle + norm_back(grad_normed_one, scaled_one, inverse_one, gain_one)
    gain_grad = jnp.stack([gain_one_grad, gain_two_grad])

    layer_out = [
        (live[r] * (middle[r] + fill.result(("ffn", r)))).astype(BF16) for r in range(rows_here)
    ]
    cache_grad = fill.result("cache")
    cache_grad = cache_grad.transpose(1, 3, 0, 2, 4).reshape(rows_here, seg_len, 2, KV * HEAD)
    sums = (main.result("output").astype(BF16), main.result("query").astype(BF16))
    summed, sums, gain_grad = lax.optimization_barrier((summed, sums, gain_grad))
    gain_grad = sum_all(gain_grad, rows, seq)
    in_grad, down_grad = summed
    (output_grad, query_grad), in_grad = sum_rows(sums, rows, in_grad)
    in_grad = in_grad.reshape(2, units, width).transpose(1, 0, 2)
    in_grad = lax.optimization_barrier(in_grad)
    return (
        jnp.stack(layer_out),
        input_grad.reshape(rows_here, seg_len, width),
        cache_grad,
        gain_grad,
        query_grad,
        output_grad,
        in_grad.astype(F32),
        down_grad.astype(F32),
    )


def solution(mesh):
    in_specs = (
        P("rows", "seq", None),
        P("rows", "seq", None, None),
        P("rows"),
        P(),
        P("seq", None),
        P("seq", None),
        P("seq", None, None),
        P("seq", None),
        P("rows", "seq", None),
    )
    out_specs = (
        P("rows", "seq", None),
        P("rows", "seq", None),
        P("rows", "seq", None, None),
        P(),
        P("seq", None),
        P("seq", None),
        P("seq", None, None),
        P("seq", None),
    )
    return jax.shard_map(local, mesh=mesh, in_specs=in_specs, out_specs=out_specs, check_vma=False)
```

```python
import jax
import jax.numpy as jnp
from jax import lax
from jax.sharding import PartitionSpec as P

HEADS = 16
HEAD = 128
KV = 4
GROUP = 4
EPS = 1e-05
NEG = -1e30
F32 = jnp.float32
BF16 = jnp.bfloat16


def dot(left, right, dims):
    return lax.dot_general(left, right, (dims, ((), ())), preferred_element_type=F32)


def tie(value, dep):
    if dep is None:
        return value
    return lax.optimization_barrier((value, dep))[0]


def norm_back(grad_normed, scaled, inverse, gain):
    inner = grad_normed * gain
    return inverse * (inner - scaled * jnp.mean(inner * scaled, axis=-1, keepdims=True))


def swap_core(value, seq):
    return lax.ppermute(value, "seq", [(s, s ^ 1) for s in range(seq)])


def ring(value, chips):
    pairs = [(2 * z + c, 2 * ((z + 1) % chips) + c) for z in range(chips) for c in range(2)]
    return lax.ppermute(value, "seq", pairs)


def swap_row(value, rows, mask):
    return lax.ppermute(value, "rows", [(r, r ^ mask) for r in range(rows)])


def ring_gather(own, chips, dep=None):
    got = [tie(own, dep)]
    for _ in range(1, chips):
        got.append(ring(got[-1], chips))
    return [own] + got[:0:-1], got[-1]


def ring_scatter(parts, chips):
    sent = parts[chips - 1]
    for j in range(chips - 2, -1, -1):
        yield sent
        total = ring(sent, chips).astype(F32) + parts[j].astype(F32)
        sent = total.astype(BF16)
    return total


class Lane:
    def __init__(self):
        self.waiting, self.results, self.sent = [], {}, None

    def add(self, name, steps):
        self.waiting.append((name, steps))

    def step(self):
        if self.waiting:
            name, steps = self.waiting[0]
            try:
                sent = next(steps)
                self.sent = sent
                return sent
            except StopIteration as end:
                self.results[name] = end.value
                self.waiting.pop(0)
                return self.step()
        return None

    def result(self, name):
        while name not in self.results:
            self.step()
        return self.results[name]


def beside(value, *lanes):
    for lane in lanes:
        value = tie(value, lane.step())
    return value


def xor_order(value, at):
    shape = value.shape
    value = value.reshape(2, 2, *shape[1:])
    value = jnp.where(at % 2 == 1, value[:, ::-1], value)
    return jnp.where(at // 2 == 1, value[::-1], value).reshape(shape)


def own_order(value, chips, place, core):
    count = value.shape[0]
    value = value.reshape(count, chips, 2, -1)
    value = jnp.where(core == 0, value, value[:, :, ::-1])
    value = jnp.concatenate([value, value], axis=1)
    value = lax.dynamic_slice_in_dim(value, place, chips, axis=1)
    return value.transpose(0, 2, 1, 3).reshape(count, -1)


def index_order(value, chips, place, core):
    count = value.shape[0]
    value = value.reshape(count, 2, chips, -1).transpose(0, 2, 1, 3)
    value = jnp.concatenate([value, value], axis=1)
    value = lax.dynamic_slice_in_dim(value, (chips - place) % chips, chips, axis=1)
    value = jnp.where(core == 0, value, value[:, :, ::-1])
    return value.reshape(count, -1)


class Weight:
    def __init__(self, shard, chips, rows, row_at, order, dep=None):
        seq = 2 * chips
        self.chips, self.row_at, self.order = chips, row_at, order
        depth, width = shard.shape
        self.depth = depth
        self.split = rows == 4 and depth % 32 == 0 and width % 512 == 0
        if not self.split:
            self.whole = lax.all_gather(shard, "seq", axis=0, tiled=True)
            self.token = dep
            self.steps = [None, None]
            return
        part = width // rows
        half = part // 2
        mine = lax.dynamic_slice_in_dim(shard, row_at * part, part, axis=1)
        slots, self.token = ring_gather(mine, chips, dep=dep)
        first = jnp.stack([v[:, :half] for v in slots[1:]])
        second = jnp.stack([v[:, half:] for v in slots[1:]])
        first_x = swap_row(first, rows, 1)
        second_y = swap_row(second, rows, 2)
        first_pair = swap_row(jnp.stack([first, first_x]), rows, 2)
        second_pair = swap_row(jnp.stack([second, second_y]), rows, 1)
        parts = [first, second, first_x, second_pair[0]]
        parts += [first_pair[0], second_y, first_pair[1], second_pair[1]]
        parts = jnp.concatenate(parts, axis=0).reshape(rows * 2, (chips - 1) * depth, half)
        self.steps = [(first_x, second_y), (first_pair, second_pair)]
        self.far = [parts, swap_core(parts, seq)]
        self.near = [shard, swap_core(shard, seq)]

    def features(self, value, lanes=()):
        if not self.split:
            out = own_order(dot(value, self.whole, ((1,), (1,))), *self.order)
            half = out.shape[1] // 2
            return [out[:, :half].astype(BF16), out[:, half:].astype(BF16)]
        count = value.shape[0]
        out = []
        for near, far in zip(self.near, self.far, strict=True):
            if out:
                value = beside(value, *lanes)
            blocks = value.reshape(count, 4, 2, -1).transpose(1, 2, 0, 3)
            blocks = xor_order(blocks, self.row_at).reshape(8, count, -1)
            term = jnp.einsum("ktc,kfc->ktf", blocks, far, preferred_element_type=F32)
            term = jnp.sum(term, axis=0).astype(BF16)
            out.append(jnp.concatenate([dot(value, near, ((1,), (1,))).astype(BF16), term], axis=1))
        return out

    def back(self, halves):
        if not self.split:
            value = jnp.concatenate(halves, axis=1)
            return dot(index_order(value, *self.order), self.whole, ((1,), (0,)))
        count = halves[0].shape[0]
        near_sum = far_sum = 0.0
        for part, near, far in zip(halves, self.near, self.far, strict=True):
            near_sum += dot(part[:, : self.depth], near, ((1,), (0,)))
            far_sum += jnp.einsum(
                "tf,kfc->ktc", part[:, self.depth :], far, preferred_element_type=F32
            )
        far_sum = xor_order(far_sum.reshape(4, 2, count, -1), self.row_at)
        far_sum = jnp.concatenate([far_sum[k, h] for k in range(4) for h in range(2)], axis=1)
        return near_sum + far_sum


def scatter_halves(own, sib, got_at, chips):
    got = swap_core(sib, 2 * chips)
    parts = [own(j).astype(F32) + got_at(got, j).astype(F32) for j in range(chips)]
    return (yield from ring_scatter([p.astype(BF16) for p in parts], chips))


def block_of(value, j, chips):
    size = value.shape[0] // chips
    return value[j * size : (j + 1) * size]


def scatter_tokens(part, chips, place, core):
    size = part.shape[0] // (2 * chips)

    def block(j, at):
        start = (2 * ((place + j) % chips) + at) * size
        return lax.dynamic_slice_in_dim(part, start, size, axis=0)

    sib = jnp.concatenate([block(j, 1 - core) for j in range(chips)], axis=0)
    return scatter_halves(
        lambda j: block(j, core), sib, lambda got, j: block_of(got, j, chips), chips
    )


def sum_rows(values, rows):
    if rows != 4:
        return [lax.psum(v.astype(BF16), "rows").astype(F32) for v in values]

    def pair(item, mask):
        return item.astype(F32) + swap_row(item, rows, mask).astype(F32)

    out = []
    for value in values:
        half = value.shape[0] // 2
        first, second = value[:half].astype(BF16), value[half:].astype(BF16)
        first, second = pair(first, 1).astype(BF16), pair(second, 2).astype(BF16)
        out.append(jnp.concatenate([pair(first, 2), pair(second, 1)], axis=0))
    return out


def sum_all(value, rows, seq):
    mask = 1
    while mask < seq:
        value = value + lax.ppermute(value, "seq", [(s, s ^ mask) for s in range(seq)])
        mask *= 2
    mask = 1
    while mask < rows:
        value = value + swap_row(value, rows, mask)
        mask *= 2
    return value


def local(
    tokens,
    kv_cache,
    lengths,
    norm_gains,
    query_weight,
    output_weight,
    ffn_in_weight,
    down_weight,
    cotangent,
):
    rows_here, seg_len, width = tokens.shape
    seq = lax.axis_size("seq")
    rows = lax.axis_size("rows")
    chips = seq // 2
    seq_at = lax.axis_index("seq")
    row_at = lax.axis_index("rows")
    place, core = seq_at // 2, seq_at % 2
    order = (chips, place, core)
    gain_one, gain_two = norm_gains[0], norm_gains[1]
    query_pos = seq_at * seg_len + jnp.arange(seg_len, dtype=jnp.int32)
    chip_range = jnp.arange(chips, dtype=jnp.int32)
    ring_at = (place + chip_range) % chips
    starts = jnp.concatenate([2 * ring_at + core, 2 * ring_at + 1 - core]) * seg_len

    live = [
        (query_pos < lengths[r]).astype(F32).reshape(seg_len, 1) for r in range(rows_here)
    ]
    grad_out = [cotangent[r].astype(F32) * live[r] for r in range(rows_here)]
    gate_up_weight = jnp.concatenate([ffn_in_weight[:, 0], ffn_in_weight[:, 1]], axis=0)
    query_proj = Weight(query_weight, chips, rows, row_at, order)
    cache_own = kv_cache.reshape(rows_here, seg_len, 2, KV, HEAD).transpose(2, 0, 3, 1, 4)
    output_proj = Weight(output_weight, chips, rows, row_at, order, dep=query_proj.token)
    cache_slots, token = ring_gather(cache_own, chips, dep=output_proj.token)
    cache_block = jnp.concatenate(cache_slots, axis=3)
    cache_block = tie(cache_block, output_proj.steps[0])
    cache_all = jnp.concatenate([cache_block, swap_core(cache_block, seq)], axis=3)
    grad_group = [
        lax.all_gather(tie(g.astype(BF16), token), "seq", axis=0, tiled=True) for g in grad_out
    ]
    per = chips // KV

    def to_slots(value):
        value = jnp.repeat(value, per, axis=2) if per > 1 else value
        value = jnp.concatenate([value, value], axis=2)
        return lax.dynamic_slice_in_dim(value, place, chips, axis=2)

    def from_slots(value):
        value = jnp.concatenate([value, value], axis=2)
        value = lax.dynamic_slice_in_dim(value, (chips - place) % chips, chips, axis=2)
        if per > 1:
            shape = value.shape
            value = value.reshape(*shape[:2], KV, per, *shape[3:]).astype(F32).sum(axis=3)
        return value.astype(BF16)

    def to_heads(halves):
        value = jnp.stack([h.reshape(rows_here, seg_len, chips, -1, HEAD) for h in halves])
        value = value.transpose(1, 3, 0, 4, 2, 5)
        return value.reshape(rows_here, chips, -1, HEAD)

    def from_heads(value):
        value = value.reshape(rows_here, chips, 2, -1, seg_len, HEAD).transpose(2, 0, 4, 1, 3, 5)
        value = value.reshape(2, rows_here * seg_len, -1)
        return [value[0], value[1]]

    def heads_dot(spec, left, right):
        return jnp.einsum(spec, left, right, preferred_element_type=F32)

    key_pos = (starts[:, None] + jnp.arange(seg_len, dtype=jnp.int32)).reshape(-1)
    limit = jnp.minimum(query_pos[None], lengths[:, None] - 1)
    limit = jnp.tile(limit, (1, HEADS // chips))
    valid = (key_pos[None, None] <= limit[:, :, None])[:, None]
    scale = HEAD ** (-0.5)

    inputs = tokens.astype(F32).reshape(rows_here * seg_len, width)
    inverse_one = lax.rsqrt(jnp.mean(inputs * inputs, axis=-1, keepdims=True) + EPS)
    normed_one = (inputs * inverse_one * gain_one).astype(BF16)
    query = query_proj.features(normed_one)
    cache_slot = to_slots(cache_all)
    keys, values = cache_slot[0], cache_slot[1]
    query_heads = to_heads(query)
    scores = heads_dot("rjqd,rjkd->rjqk", query_heads, keys) * scale
    scores = jnp.where(valid, scores, NEG)
    best = tie(jnp.max(scores, axis=-1, keepdims=True), output_proj.steps[1])
    weights = jnp.exp(scores - best)
    total = jnp.sum(weights, axis=-1, keepdims=True)
    mixed_heads = heads_dot("rjqk,rjkd->rjqd", weights.astype(BF16), values) / total
    lse = best + jnp.log(total)
    mixed = from_heads(mixed_heads.astype(BF16))
    mixed, grad_group[0] = lax.optimization_barrier((mixed, grad_group[0]))
    middle_all = inputs + output_proj.back(mixed)
    inverse_all = lax.rsqrt(jnp.mean(middle_all * middle_all, axis=-1, keepdims=True) + EPS)
    normed_all = (middle_all * inverse_all * gain_two).astype(BF16)
    normed_all, grad_group[1:] = lax.optimization_barrier((normed_all, grad_group[1:]))

    def split(value):
        return [value[r * seg_len : (r + 1) * seg_len] for r in range(rows_here)]

    middle, inverse_two, normed_two = split(middle_all), split(inverse_all), split(normed_all)
    normed_group = [lax.all_gather(n, "seq", axis=0, tiled=True) for n in normed_two]

    main, fill = Lane(), Lane()
    units = down_weight.shape[0]
    hidden, grad_gate_up, grad_part, ffn_part = [], [], [], []
    for r in range(rows_here):
        kept = dot(normed_group[r], gate_up_weight, ((1,), (1,)))
        gate, upper = kept[:, :units], kept[:, units:]
        sigma = jax.nn.sigmoid(gate)
        grad_hidden = dot(beside(grad_group[r], fill), down_weight, ((1,), (1,)))
        hidden.append((gate * sigma * upper).astype(BF16))
        grad_gate = grad_hidden * upper * sigma * (1.0 + gate * (1.0 - sigma))
        grad_up = grad_hidden * gate * sigma
        grad_gate_up.append(jnp.concatenate([grad_gate, grad_up], axis=1).astype(BF16))
        part = dot(beside(grad_gate_up[r], fill), gate_up_weight, ((1,), (0,))).astype(BF16)
        if r + 1 < rows_here:
            part, normed_group[r + 1] = lax.optimization_barrier((part, normed_group[r + 1]))
        grad_part.append(lax.psum_scatter(part, "seq", scatter_dimension=0, tiled=True))
        ffn_part.append(dot(hidden[r], down_weight, ((1,), (0,))).astype(BF16))

    def over_tokens(left, right):
        terms = [dot(a, b, ((0,), (0,))) for a, b in zip(left, right, strict=True)]
        return sum(terms).astype(BF16)

    for r in range(rows_here - 1):
        grad_part[r], grad_gate_up[-1], hidden[-1] = lax.optimization_barrier(
            (grad_part[r], grad_gate_up[-1], hidden[-1])
        )
    in_part = over_tokens(grad_gate_up, normed_group)
    down_part = over_tokens(hidden, grad_group)
    parts = (in_part, down_part)
    summed = lax.psum(parts, "rows")

    grad_middle, gain_two_grad = [], 0.0
    for r in range(rows_here):
        grad_normed_two = grad_part[r].astype(F32)
        if r:
            grad_normed_two, parts = lax.optimization_barrier((grad_normed_two, parts))
        scaled_two = middle[r] * inverse_two[r]
        gain_two_grad += jnp.sum(grad_normed_two * scaled_two, axis=0)
        grad_middle.append(
            grad_out[r] + norm_back(grad_normed_two, scaled_two, inverse_two[r], gain_two)
        )
    part = tie(ffn_part[0], grad_middle[-1])
    fill.add(("ffn", 0), scatter_tokens(part, chips, place, core))
    grad_middle = jnp.concatenate(grad_middle, axis=0)
    grad_branch = grad_middle.astype(BF16)
    output_part = [dot(half, grad_branch, ((0,), (0,))).astype(BF16) for half in mixed]

    def scatter_rows(parts):
        def take(value, j):
            return block_of(value, j, chips)

        return scatter_halves(lambda j: take(parts[0], j), parts[1], take, chips)

    main.add("output", scatter_rows(output_part))
    grad_heads = to_heads(output_proj.features(tie(grad_branch, output_part[1]), (main, fill)))
    grad_heads = beside(grad_heads, main, fill)
    delta = jnp.sum(grad_heads.astype(F32) * mixed_heads, axis=-1, keepdims=True)
    scores = heads_dot("rjqd,rjkd->rjqk", query_heads, keys) * scale
    probs = jnp.where(valid, jnp.exp(scores - lse), 0.0)
    grad_probs = heads_dot("rjqd,rjkd->rjqk", grad_heads, values)
    grad_scores = beside((probs * (grad_probs - delta)).astype(BF16), main, fill)
    for r in range(1, rows_here):
        part, grad_scores = lax.optimization_barrier((ffn_part[r], grad_scores))
        fill.add(("ffn", r), scatter_tokens(part, chips, place, core))
    query_term = from_heads(
        (heads_dot("rjqk,rjkd->rjqd", grad_scores, keys) * scale).astype(BF16)
    )
    grad_keys = heads_dot("rjqk,rjqd->rjkd", grad_scores, query_heads) * scale
    grad_values = heads_dot("rjqk,rjqd->rjkd", probs.astype(BF16), grad_heads)
    cache_part = from_slots(jnp.stack([grad_keys.astype(BF16), grad_values.astype(BF16)]))
    half_len = cache_part.shape[3] // 2

    def positions_of(value, j):
        return value[:, :, :, j * seg_len : (j + 1) * seg_len]

    fill.add(
        "cache",
        scatter_halves(
            lambda j: positions_of(cache_part, j), cache_part[:, :, :, half_len:], positions_of, chips
        ),
    )
    query_part = [dot(half, normed_one, ((0,), (0,))).astype(BF16) for half in query_term]
    main.add("query", scatter_rows(query_part))

    grad_normed_one = query_proj.back(query_term)
    scaled_one = inputs * inverse_one
    gain_one_grad = jnp.sum(grad_normed_one * scaled_one, axis=0)
    input_grad = grad_middle + norm_back(grad_normed_one, scaled_one, inverse_one, gain_one)
    gain_grad = jnp.stack([gain_one_grad, gain_two_grad])

    layer_out = [
        (live[r] * (middle[r] + fill.result(("ffn", r)))).astype(BF16) for r in range(rows_here)
    ]
    cache_grad = fill.result("cache")
    cache_grad = cache_grad.transpose(1, 3, 0, 2, 4).reshape(rows_here, seg_len, 2, KV * HEAD)
    output_sum = main.result("output")
    for _ in range(chips - 1):
        sent = main.step()
    summed, output_sum = lax.optimization_barrier((summed, output_sum.astype(BF16)))
    in_grad, down_grad = tie(summed, sent)
    in_grad = in_grad.reshape(2, units, width).transpose(1, 0, 2)
    in_grad = lax.optimization_barrier(in_grad)
    query_sum, gain_grad = lax.optimization_barrier((main.result("query"), gain_grad))
    gain_grad = sum_all(gain_grad, rows, seq)
    output_grad, query_grad = sum_rows((output_sum, query_sum), rows)
    return (
        jnp.stack(layer_out),
        input_grad.reshape(rows_here, seg_len, width),
        cache_grad,
        gain_grad,
        query_grad,
        output_grad,
        in_grad.astype(F32),
        down_grad.astype(F32),
    )


def solution(mesh):
    in_specs = (
        P("rows", "seq", None),
        P("rows", "seq", None, None),
        P("rows"),
        P(),
        P("seq", None),
        P("seq", None),
        P("seq", None, None),
        P("seq", None),
        P("rows", "seq", None),
    )
    out_specs = (
        P("rows", "seq", None),
        P("rows", "seq", None),
        P("rows", "seq", None, None),
        P(),
        P("seq", None),
        P("seq", None),
        P("seq", None, None),
        P("seq", None),
    )
    return jax.shard_map(local, mesh=mesh, in_specs=in_specs, out_specs=out_specs, check_vma=False)
```

```python
import jax
import jax.numpy as jnp
from jax import lax
from jax.sharding import PartitionSpec as P

HEADS = 16
HEAD = 128
KV = 4
GROUP = 4
EPS = 1e-05
NEG = -1e30
F32 = jnp.float32
BF16 = jnp.bfloat16


def dot(left, right, dims):
    return lax.dot_general(left, right, (dims, ((), ())), preferred_element_type=F32)


def tie(value, dep):
    if dep is None:
        return value
    return lax.optimization_barrier((value, dep))[0]


def norm_back(grad_normed, scaled, inverse, gain):
    inner = grad_normed * gain
    return inverse * (inner - scaled * jnp.mean(inner * scaled, axis=-1, keepdims=True))


def swap_core(value, seq):
    return lax.ppermute(value, "seq", [(s, s ^ 1) for s in range(seq)])


def ring(value, chips):
    pairs = [(2 * z + c, 2 * ((z + 1) % chips) + c) for z in range(chips) for c in range(2)]
    return lax.ppermute(value, "seq", pairs)


def swap_row(value, rows, mask):
    return lax.ppermute(value, "rows", [(r, r ^ mask) for r in range(rows)])


def ring_gather(own, chips, dep=None):
    got = [tie(own, dep)]
    for _ in range(1, chips):
        got.append(ring(got[-1], chips))
    return [own] + got[:0:-1], got[-1]


def ring_scatter(parts, chips):
    sent = parts[chips - 1]
    for j in range(chips - 2, -1, -1):
        after = yield sent
        total = ring(sent, chips).astype(F32) + tie(parts[j], after).astype(F32)
        sent = total.astype(BF16)
    return total


class Lane:
    def __init__(self):
        self.waiting, self.results, self.begun, self.sent = [], {}, set(), None

    def add(self, name, steps):
        self.waiting.append((name, steps))

    def step(self, after=None):
        if self.waiting:
            name, steps = self.waiting[0]
            try:
                self.sent = next(steps) if name not in self.begun else steps.send(after)
                self.begun.add(name)
                return self.sent
            except StopIteration as end:
                self.results[name] = end.value
                self.waiting.pop(0)
                return self.step(after)
        return None

    def result(self, name):
        while name not in self.results:
            self.step()
        return self.results[name]


def beside(value, *lanes):
    for lane in lanes:
        value = tie(value, lane.step(value))
    return value


def xor_order(value, at):
    shape = value.shape
    value = value.reshape(2, 2, *shape[1:])
    value = jnp.where(at % 2 == 1, value[:, ::-1], value)
    return jnp.where(at // 2 == 1, value[::-1], value).reshape(shape)


def own_order(value, chips, place, core):
    count = value.shape[0]
    value = value.reshape(count, chips, 2, -1)
    value = jnp.where(core == 0, value, value[:, :, ::-1])
    value = jnp.concatenate([value, value], axis=1)
    value = lax.dynamic_slice_in_dim(value, place, chips, axis=1)
    return value.transpose(0, 2, 1, 3).reshape(count, -1)


def index_order(value, chips, place, core):
    count = value.shape[0]
    value = value.reshape(count, 2, chips, -1).transpose(0, 2, 1, 3)
    value = jnp.concatenate([value, value], axis=1)
    value = lax.dynamic_slice_in_dim(value, (chips - place) % chips, chips, axis=1)
    value = jnp.where(core == 0, value, value[:, :, ::-1])
    return value.reshape(count, -1)


class Weight:
    def __init__(self, shard, chips, rows, row_at, order, dep=None):
        seq = 2 * chips
        self.chips, self.row_at, self.order = chips, row_at, order
        depth, width = shard.shape
        self.depth = depth
        self.split = rows == 4 and depth % 32 == 0 and width % 512 == 0
        if not self.split:
            self.whole = lax.all_gather(shard, "seq", axis=0, tiled=True)
            self.token = dep
            self.steps = [None, None]
            return
        part = width // rows
        half = part // 2
        mine = lax.dynamic_slice_in_dim(shard, row_at * part, part, axis=1)
        slots, self.token = ring_gather(mine, chips, dep=dep)
        first = jnp.stack([v[:, :half] for v in slots[1:]])
        second = jnp.stack([v[:, half:] for v in slots[1:]])
        first_x = swap_row(first, rows, 1)
        second_y = swap_row(second, rows, 2)
        first_pair = swap_row(jnp.stack([first, first_x]), rows, 2)
        second_pair = swap_row(jnp.stack([second, second_y]), rows, 1)
        parts = [first, second, first_x, second_pair[0]]
        parts += [first_pair[0], second_y, first_pair[1], second_pair[1]]
        parts = jnp.concatenate(parts, axis=0).reshape(rows * 2, (chips - 1) * depth, half)
        self.steps = [(first_x, second_y), (first_pair, second_pair)]
        self.far = [parts, swap_core(parts, seq)]
        self.near = [shard, swap_core(shard, seq)]

    def features(self, value, lanes=()):
        if not self.split:
            out = own_order(dot(value, self.whole, ((1,), (1,))), *self.order)
            half = out.shape[1] // 2
            return [out[:, :half].astype(BF16), out[:, half:].astype(BF16)]
        count = value.shape[0]
        out = []
        for near, far in zip(self.near, self.far, strict=True):
            if out:
                value = beside(value, *lanes)
            blocks = value.reshape(count, 4, 2, -1).transpose(1, 2, 0, 3)
            blocks = xor_order(blocks, self.row_at).reshape(8, count, -1)
            term = jnp.einsum("ktc,kfc->ktf", blocks, far, preferred_element_type=F32)
            term = jnp.sum(term, axis=0).astype(BF16)
            out.append(jnp.concatenate([dot(value, near, ((1,), (1,))).astype(BF16), term], axis=1))
        return out

    def back(self, halves):
        if not self.split:
            value = jnp.concatenate(halves, axis=1)
            return dot(index_order(value, *self.order), self.whole, ((1,), (0,)))
        count = halves[0].shape[0]
        near_sum = far_sum = 0.0
        for part, near, far in zip(halves, self.near, self.far, strict=True):
            near_sum += dot(part[:, : self.depth], near, ((1,), (0,)))
            far_sum += jnp.einsum(
                "tf,kfc->ktc", part[:, self.depth :], far, preferred_element_type=F32
            )
        far_sum = xor_order(far_sum.reshape(4, 2, count, -1), self.row_at)
        far_sum = jnp.concatenate([far_sum[k, h] for k in range(4) for h in range(2)], axis=1)
        return near_sum + far_sum


def scatter_halves(own, sib, got_at, chips):
    got = swap_core(sib, 2 * chips)
    parts = [own(j).astype(F32) + got_at(got, j).astype(F32) for j in range(chips)]
    return (yield from ring_scatter([p.astype(BF16) for p in parts], chips))


def block_of(value, j, chips):
    size = value.shape[0] // chips
    return value[j * size : (j + 1) * size]


def scatter_tokens(part, chips, place, core):
    size = part.shape[0] // (2 * chips)

    def block(j, at):
        start = (2 * ((place + j) % chips) + at) * size
        return lax.dynamic_slice_in_dim(part, start, size, axis=0)

    sib = jnp.concatenate([block(j, 1 - core) for j in range(chips)], axis=0)
    return scatter_halves(
        lambda j: block(j, core), sib, lambda got, j: block_of(got, j, chips), chips
    )


def sum_rows(values, rows):
    if rows != 4:
        return [lax.psum(v.astype(BF16), "rows").astype(F32) for v in values]

    def pair(item, mask):
        return item.astype(F32) + swap_row(item, rows, mask).astype(F32)

    out = []
    for value in values:
        half = value.shape[0] // 2
        first, second = value[:half].astype(BF16), value[half:].astype(BF16)
        first, second = pair(first, 1).astype(BF16), pair(second, 2).astype(BF16)
        out.append(jnp.concatenate([pair(first, 2), pair(second, 1)], axis=0))
    return out


def sum_all(value, rows, seq):
    mask = 1
    while mask < seq:
        value = value + lax.ppermute(value, "seq", [(s, s ^ mask) for s in range(seq)])
        mask *= 2
    mask = 1
    while mask < rows:
        value = value + swap_row(value, rows, mask)
        mask *= 2
    return value


def local(
    tokens,
    kv_cache,
    lengths,
    norm_gains,
    query_weight,
    output_weight,
    ffn_in_weight,
    down_weight,
    cotangent,
):
    rows_here, seg_len, width = tokens.shape
    seq = lax.axis_size("seq")
    rows = lax.axis_size("rows")
    chips = seq // 2
    seq_at = lax.axis_index("seq")
    row_at = lax.axis_index("rows")
    place, core = seq_at // 2, seq_at % 2
    order = (chips, place, core)
    gain_one, gain_two = norm_gains[0], norm_gains[1]
    query_pos = seq_at * seg_len + jnp.arange(seg_len, dtype=jnp.int32)
    chip_range = jnp.arange(chips, dtype=jnp.int32)
    ring_at = (place + chip_range) % chips
    starts = jnp.concatenate([2 * ring_at + core, 2 * ring_at + 1 - core]) * seg_len

    live = [
        (query_pos < lengths[r]).astype(F32).reshape(seg_len, 1) for r in range(rows_here)
    ]
    grad_out = [cotangent[r].astype(F32) * live[r] for r in range(rows_here)]
    gate_up_weight = jnp.concatenate([ffn_in_weight[:, 0], ffn_in_weight[:, 1]], axis=0)
    query_proj = Weight(query_weight, chips, rows, row_at, order)
    cache_own = kv_cache.reshape(rows_here, seg_len, 2, KV, HEAD).transpose(2, 0, 3, 1, 4)
    output_proj = Weight(output_weight, chips, rows, row_at, order, dep=query_proj.token)
    cache_slots, token = ring_gather(cache_own, chips, dep=output_proj.token)
    cache_block = jnp.concatenate(cache_slots, axis=3)
    cache_block = tie(cache_block, output_proj.steps[0])
    cache_all = jnp.concatenate([cache_block, swap_core(cache_block, seq)], axis=3)
    grad_group = [
        lax.all_gather(tie(g.astype(BF16), token), "seq", axis=0, tiled=True) for g in grad_out
    ]
    per = chips // KV

    def to_slots(value):
        value = jnp.repeat(value, per, axis=2) if per > 1 else value
        value = jnp.concatenate([value, value], axis=2)
        return lax.dynamic_slice_in_dim(value, place, chips, axis=2)

    def from_slots(value):
        value = jnp.concatenate([value, value], axis=2)
        value = lax.dynamic_slice_in_dim(value, (chips - place) % chips, chips, axis=2)
        if per > 1:
            shape = value.shape
            value = value.reshape(*shape[:2], KV, per, *shape[3:]).astype(F32).sum(axis=3)
        return value.astype(BF16)

    def to_heads(halves):
        value = jnp.stack([h.reshape(rows_here, seg_len, chips, -1, HEAD) for h in halves])
        value = value.transpose(1, 3, 0, 4, 2, 5)
        return value.reshape(rows_here, chips, -1, HEAD)

    def from_heads(value):
        value = value.reshape(rows_here, chips, 2, -1, seg_len, HEAD).transpose(2, 0, 4, 1, 3, 5)
        value = value.reshape(2, rows_here * seg_len, -1)
        return [value[0], value[1]]

    def heads_dot(spec, left, right):
        return jnp.einsum(spec, left, right, preferred_element_type=F32)

    key_pos = (starts[:, None] + jnp.arange(seg_len, dtype=jnp.int32)).reshape(-1)
    limit = jnp.minimum(query_pos[None], lengths[:, None] - 1)
    limit = jnp.tile(limit, (1, HEADS // chips))
    valid = (key_pos[None, None] <= limit[:, :, None])[:, None]
    scale = HEAD ** (-0.5)

    inputs = tokens.astype(F32).reshape(rows_here * seg_len, width)
    inverse_one = lax.rsqrt(jnp.mean(inputs * inputs, axis=-1, keepdims=True) + EPS)
    normed_one = (inputs * inverse_one * gain_one).astype(BF16)
    query = query_proj.features(normed_one)
    cache_slot = to_slots(cache_all)
    keys, values = cache_slot[0], cache_slot[1]
    query_heads = to_heads(query)
    scores = heads_dot("rjqd,rjkd->rjqk", query_heads, keys) * scale
    scores = jnp.where(valid, scores, NEG)
    best = tie(jnp.max(scores, axis=-1, keepdims=True), output_proj.steps[1])
    weights = jnp.exp(scores - best)
    total = jnp.sum(weights, axis=-1, keepdims=True)
    mixed_heads = heads_dot("rjqk,rjkd->rjqd", weights.astype(BF16), values) / total
    lse = best + jnp.log(total)
    mixed = from_heads(mixed_heads.astype(BF16))
    mixed, grad_group[0] = lax.optimization_barrier((mixed, grad_group[0]))
    middle_all = inputs + output_proj.back(mixed)
    inverse_all = lax.rsqrt(jnp.mean(middle_all * middle_all, axis=-1, keepdims=True) + EPS)
    normed_all = (middle_all * inverse_all * gain_two).astype(BF16)
    normed_all, grad_group[1:] = lax.optimization_barrier((normed_all, grad_group[1:]))

    def split(value):
        return [value[r * seg_len : (r + 1) * seg_len] for r in range(rows_here)]

    middle, inverse_two, normed_two = split(middle_all), split(inverse_all), split(normed_all)
    normed_group = [lax.all_gather(n, "seq", axis=0, tiled=True) for n in normed_two]

    main, fill = Lane(), Lane()
    units = down_weight.shape[0]
    hidden, grad_gate_up, grad_part, ffn_part = [], [], [], []
    for r in range(rows_here):
        kept = dot(normed_group[r], gate_up_weight, ((1,), (1,)))
        gate, upper = kept[:, :units], kept[:, units:]
        sigma = jax.nn.sigmoid(gate)
        grad_hidden = dot(beside(grad_group[r], fill), down_weight, ((1,), (1,)))
        hidden.append((gate * sigma * upper).astype(BF16))
        grad_gate = grad_hidden * upper * sigma * (1.0 + gate * (1.0 - sigma))
        grad_up = grad_hidden * gate * sigma
        grad_gate_up.append(jnp.concatenate([grad_gate, grad_up], axis=1).astype(BF16))
        part = dot(beside(grad_gate_up[r], fill), gate_up_weight, ((1,), (0,))).astype(BF16)
        if r + 1 < rows_here:
            part, normed_group[r + 1] = lax.optimization_barrier((part, normed_group[r + 1]))
        grad_part.append(lax.psum_scatter(part, "seq", scatter_dimension=0, tiled=True))
        ffn_part.append(dot(hidden[r], down_weight, ((1,), (0,))).astype(BF16))

    def over_tokens(left, right):
        terms = [dot(a, b, ((0,), (0,))) for a, b in zip(left, right, strict=True)]
        return sum(terms).astype(BF16)

    for r in range(rows_here - 1):
        grad_part[r], grad_gate_up[-1], hidden[-1] = lax.optimization_barrier(
            (grad_part[r], grad_gate_up[-1], hidden[-1])
        )
    in_part = over_tokens(grad_gate_up, normed_group)
    down_part = over_tokens(hidden, grad_group)
    parts = (in_part, down_part)
    summed = lax.psum(parts, "rows")

    grad_middle, gain_two_grad = [], 0.0
    for r in range(rows_here):
        grad_normed_two = grad_part[r].astype(F32)
        if r:
            grad_normed_two, parts = lax.optimization_barrier((grad_normed_two, parts))
        scaled_two = middle[r] * inverse_two[r]
        gain_two_grad += jnp.sum(grad_normed_two * scaled_two, axis=0)
        grad_middle.append(
            grad_out[r] + norm_back(grad_normed_two, scaled_two, inverse_two[r], gain_two)
        )
    part = tie(ffn_part[0], grad_middle[-1])
    fill.add(("ffn", 0), scatter_tokens(part, chips, place, core))
    grad_middle = jnp.concatenate(grad_middle, axis=0)
    grad_branch = grad_middle.astype(BF16)
    output_part = [dot(half, grad_branch, ((0,), (0,))).astype(BF16) for half in mixed]

    def scatter_rows(parts):
        def take(value, j):
            return block_of(value, j, chips)

        return scatter_halves(lambda j: take(parts[0], j), parts[1], take, chips)

    main.add("output", scatter_rows(output_part))
    grad_heads = to_heads(output_proj.features(tie(grad_branch, output_part[1]), (main, fill)))
    grad_heads = beside(grad_heads, main, fill)
    delta = jnp.sum(grad_heads.astype(F32) * mixed_heads, axis=-1, keepdims=True)
    scores = heads_dot("rjqd,rjkd->rjqk", query_heads, keys) * scale
    probs = jnp.where(valid, jnp.exp(scores - lse), 0.0)
    grad_probs = heads_dot("rjqd,rjkd->rjqk", grad_heads, values)
    grad_scores = beside((probs * (grad_probs - delta)).astype(BF16), main, fill)
    query_term = from_heads(
        (heads_dot("rjqk,rjkd->rjqd", grad_scores, keys) * scale).astype(BF16)
    )
    query_part = [dot(half, normed_one, ((0,), (0,))).astype(BF16) for half in query_term]
    query_part, grad_scores = lax.optimization_barrier((query_part, grad_scores))
    output_sum = main.result("output")
    main.add("query", scatter_rows(query_part))
    main.step()
    sent = main.step()
    grad_keys = heads_dot("rjqk,rjqd->rjkd", grad_scores, query_heads) * scale
    grad_values = heads_dot("rjqk,rjqd->rjkd", probs.astype(BF16), grad_heads)
    cache_part = from_slots(jnp.stack([grad_keys.astype(BF16), grad_values.astype(BF16)]))
    cache_part = tie(cache_part, sent)
    half_len = cache_part.shape[3] // 2

    def positions_of(value, j):
        return value[:, :, :, j * seg_len : (j + 1) * seg_len]

    fill.add(
        "cache",
        scatter_halves(
            lambda j: positions_of(cache_part, j), cache_part[:, :, :, half_len:], positions_of, chips
        ),
    )
    fill.result(("ffn", 0))
    for r in range(1, rows_here):
        fill.add(("ffn", r), scatter_tokens(tie(ffn_part[r], sent), chips, place, core))

    grad_normed_one = query_proj.back(query_term)
    scaled_one = inputs * inverse_one
    gain_one_grad = jnp.sum(grad_normed_one * scaled_one, axis=0)
    input_grad = grad_middle + norm_back(grad_normed_one, scaled_one, inverse_one, gain_one)
    gain_grad = jnp.stack([gain_one_grad, gain_two_grad])

    layer_out = [
        (live[r] * (middle[r] + fill.result(("ffn", r)))).astype(BF16) for r in range(rows_here)
    ]
    cache_grad = fill.result("cache")
    cache_grad = cache_grad.transpose(1, 3, 0, 2, 4).reshape(rows_here, seg_len, 2, KV * HEAD)
    summed, query_sum = lax.optimization_barrier((summed, main.result("query").astype(BF16)))
    summed, gain_grad = lax.optimization_barrier((summed, gain_grad))
    in_grad, down_grad = summed
    in_grad = in_grad.reshape(2, units, width).transpose(1, 0, 2)
    in_grad = lax.optimization_barrier(in_grad)
    gain_grad = sum_all(gain_grad, rows, seq)
    output_grad, query_grad = sum_rows((output_sum, query_sum), rows)
    return (
        jnp.stack(layer_out),
        input_grad.reshape(rows_here, seg_len, width),
        cache_grad,
        gain_grad,
        query_grad,
        output_grad,
        in_grad.astype(F32),
        down_grad.astype(F32),
    )


def solution(mesh):
    in_specs = (
        P("rows", "seq", None),
        P("rows", "seq", None, None),
        P("rows"),
        P(),
        P("seq", None),
        P("seq", None),
        P("seq", None, None),
        P("seq", None),
        P("rows", "seq", None),
    )
    out_specs = (
        P("rows", "seq", None),
        P("rows", "seq", None),
        P("rows", "seq", None, None),
        P(),
        P("seq", None),
        P("seq", None),
        P("seq", None, None),
        P("seq", None),
    )
    return jax.shard_map(local, mesh=mesh, in_specs=in_specs, out_specs=out_specs, check_vma=False)
```

```python
import jax
import jax.numpy as jnp
from jax import lax
from jax.sharding import PartitionSpec as P

HEADS = 16
HEAD = 128
KV = 4
GROUP = 4
EPS = 1e-05
NEG = -1e30
F32 = jnp.float32
BF16 = jnp.bfloat16


def dot(left, right, dims):
    return lax.dot_general(left, right, (dims, ((), ())), preferred_element_type=F32)


def tie(value, dep):
    if dep is None:
        return value
    return lax.optimization_barrier((value, dep))[0]


def norm_back(grad_normed, scaled, inverse, gain):
    inner = grad_normed * gain
    return inverse * (inner - scaled * jnp.mean(inner * scaled, axis=-1, keepdims=True))


def swap_core(value, seq):
    return lax.ppermute(value, "seq", [(s, s ^ 1) for s in range(seq)])


def ring(value, chips):
    pairs = [(2 * z + c, 2 * ((z + 1) % chips) + c) for z in range(chips) for c in range(2)]
    return lax.ppermute(value, "seq", pairs)


def swap_row(value, rows, mask):
    return lax.ppermute(value, "rows", [(r, r ^ mask) for r in range(rows)])


def ring_gather(own, chips, dep=None):
    got = [tie(own, dep)]
    for _ in range(1, chips):
        got.append(ring(got[-1], chips))
    return [own] + got[:0:-1], got[-1]


def ring_scatter(parts, chips):
    sent = parts[chips - 1]
    for j in range(chips - 2, -1, -1):
        after = yield sent
        total = ring(sent, chips).astype(F32) + tie(parts[j], after).astype(F32)
        sent = total.astype(BF16)
    return total


class Lane:
    def __init__(self):
        self.waiting, self.results, self.begun, self.sent = [], {}, set(), None

    def add(self, name, steps):
        self.waiting.append((name, steps))

    def step(self, after=None):
        if self.waiting:
            name, steps = self.waiting[0]
            try:
                self.sent = next(steps) if name not in self.begun else steps.send(after)
                self.begun.add(name)
                return self.sent
            except StopIteration as end:
                self.results[name] = end.value
                self.waiting.pop(0)
                return self.step(after)
        return None

    def result(self, name):
        while name not in self.results:
            self.step()
        return self.results[name]


def beside(value, *lanes):
    for lane in lanes:
        value = tie(value, lane.step(value))
    return value


def xor_order(value, at):
    shape = value.shape
    value = value.reshape(2, 2, *shape[1:])
    value = jnp.where(at % 2 == 1, value[:, ::-1], value)
    return jnp.where(at // 2 == 1, value[::-1], value).reshape(shape)


def own_order(value, chips, place, core):
    count = value.shape[0]
    value = value.reshape(count, chips, 2, -1)
    value = jnp.where(core == 0, value, value[:, :, ::-1])
    value = jnp.concatenate([value, value], axis=1)
    value = lax.dynamic_slice_in_dim(value, place, chips, axis=1)
    return value.transpose(0, 2, 1, 3).reshape(count, -1)


def index_order(value, chips, place, core):
    count = value.shape[0]
    value = value.reshape(count, 2, chips, -1).transpose(0, 2, 1, 3)
    value = jnp.concatenate([value, value], axis=1)
    value = lax.dynamic_slice_in_dim(value, (chips - place) % chips, chips, axis=1)
    value = jnp.where(core == 0, value, value[:, :, ::-1])
    return value.reshape(count, -1)


class Weight:
    def __init__(self, shard, chips, rows, row_at, order, dep=None):
        seq = 2 * chips
        self.chips, self.row_at, self.order = chips, row_at, order
        depth, width = shard.shape
        self.depth = depth
        self.split = rows == 4 and depth % 32 == 0 and width % 512 == 0
        if not self.split:
            self.whole = lax.all_gather(shard, "seq", axis=0, tiled=True)
            self.token = dep
            self.steps = [None, None]
            return
        part = width // rows
        half = part // 2
        mine = lax.dynamic_slice_in_dim(shard, row_at * part, part, axis=1)
        slots, self.token = ring_gather(mine, chips, dep=dep)
        first = jnp.stack([v[:, :half] for v in slots[1:]])
        second = jnp.stack([v[:, half:] for v in slots[1:]])
        first_x = swap_row(first, rows, 1)
        second_y = swap_row(second, rows, 2)
        first_pair = swap_row(jnp.stack([first, first_x]), rows, 2)
        second_pair = swap_row(jnp.stack([second, second_y]), rows, 1)
        parts = [first, second, first_x, second_pair[0]]
        parts += [first_pair[0], second_y, first_pair[1], second_pair[1]]
        parts = jnp.concatenate(parts, axis=0).reshape(rows * 2, (chips - 1) * depth, half)
        self.steps = [(first_x, second_y), (first_pair, second_pair)]
        self.far = [parts, swap_core(parts, seq)]
        self.near = [shard, swap_core(shard, seq)]

    def features(self, value, lanes=()):
        if not self.split:
            out = own_order(dot(value, self.whole, ((1,), (1,))), *self.order)
            half = out.shape[1] // 2
            return [out[:, :half].astype(BF16), out[:, half:].astype(BF16)]
        count = value.shape[0]
        out = []
        for near, far in zip(self.near, self.far, strict=True):
            if out:
                value = beside(value, *lanes)
            blocks = value.reshape(count, 4, 2, -1).transpose(1, 2, 0, 3)
            blocks = xor_order(blocks, self.row_at).reshape(8, count, -1)
            term = jnp.einsum("ktc,kfc->ktf", blocks, far, preferred_element_type=F32)
            term = jnp.sum(term, axis=0).astype(BF16)
            out.append(jnp.concatenate([dot(value, near, ((1,), (1,))).astype(BF16), term], axis=1))
        return out

    def back(self, halves):
        if not self.split:
            value = jnp.concatenate(halves, axis=1)
            return dot(index_order(value, *self.order), self.whole, ((1,), (0,)))
        count = halves[0].shape[0]
        near_sum = far_sum = 0.0
        for part, near, far in zip(halves, self.near, self.far, strict=True):
            near_sum += dot(part[:, : self.depth], near, ((1,), (0,)))
            far_sum += jnp.einsum(
                "tf,kfc->ktc", part[:, self.depth :], far, preferred_element_type=F32
            )
        far_sum = xor_order(far_sum.reshape(4, 2, count, -1), self.row_at)
        far_sum = jnp.concatenate([far_sum[k, h] for k in range(4) for h in range(2)], axis=1)
        return near_sum + far_sum


def scatter_halves(own, sib, got_at, chips):
    got = swap_core(sib, 2 * chips)
    parts = [own(j).astype(F32) + got_at(got, j).astype(F32) for j in range(chips)]
    return (yield from ring_scatter([p.astype(BF16) for p in parts], chips))


def block_of(value, j, chips):
    size = value.shape[0] // chips
    return value[j * size : (j + 1) * size]


def scatter_tokens(part, chips, place, core):
    size = part.shape[0] // (2 * chips)

    def block(j, at):
        start = (2 * ((place + j) % chips) + at) * size
        return lax.dynamic_slice_in_dim(part, start, size, axis=0)

    sib = jnp.concatenate([block(j, 1 - core) for j in range(chips)], axis=0)
    return scatter_halves(
        lambda j: block(j, core), sib, lambda got, j: block_of(got, j, chips), chips
    )


def sum_rows(values, rows):
    if rows != 4:
        return [lax.psum(v.astype(BF16), "rows").astype(F32) for v in values]

    def pair(item, mask):
        return item.astype(F32) + swap_row(item, rows, mask).astype(F32)

    out = []
    for value in values:
        half = value.shape[0] // 2
        first, second = value[:half].astype(BF16), value[half:].astype(BF16)
        first, second = pair(first, 1).astype(BF16), pair(second, 2).astype(BF16)
        out.append(jnp.concatenate([pair(first, 2), pair(second, 1)], axis=0))
    return out


def sum_all(value, rows, seq):
    mask = 1
    while mask < seq:
        value = value + lax.ppermute(value, "seq", [(s, s ^ mask) for s in range(seq)])
        mask *= 2
    mask = 1
    while mask < rows:
        value = value + swap_row(value, rows, mask)
        mask *= 2
    return value


def local(
    tokens,
    kv_cache,
    lengths,
    norm_gains,
    query_weight,
    output_weight,
    ffn_in_weight,
    down_weight,
    cotangent,
):
    rows_here, seg_len, width = tokens.shape
    seq = lax.axis_size("seq")
    rows = lax.axis_size("rows")
    chips = seq // 2
    seq_at = lax.axis_index("seq")
    row_at = lax.axis_index("rows")
    place, core = seq_at // 2, seq_at % 2
    order = (chips, place, core)
    gain_one, gain_two = norm_gains[0], norm_gains[1]
    query_pos = seq_at * seg_len + jnp.arange(seg_len, dtype=jnp.int32)
    chip_range = jnp.arange(chips, dtype=jnp.int32)
    ring_at = (place + chip_range) % chips
    starts = jnp.concatenate([2 * ring_at + core, 2 * ring_at + 1 - core]) * seg_len

    live = [
        (query_pos < lengths[r]).astype(F32).reshape(seg_len, 1) for r in range(rows_here)
    ]
    grad_out = [cotangent[r].astype(F32) * live[r] for r in range(rows_here)]
    gate_up_weight = jnp.concatenate([ffn_in_weight[:, 0], ffn_in_weight[:, 1]], axis=0)
    query_proj = Weight(query_weight, chips, rows, row_at, order)
    cache_own = kv_cache.reshape(rows_here, seg_len, 2, KV, HEAD).transpose(2, 0, 3, 1, 4)
    output_proj = Weight(output_weight, chips, rows, row_at, order, dep=query_proj.token)
    cache_slots, token = ring_gather(cache_own, chips, dep=output_proj.token)
    cache_block = jnp.concatenate(cache_slots, axis=3)
    cache_block = tie(cache_block, output_proj.steps[0])
    cache_all = jnp.concatenate([cache_block, swap_core(cache_block, seq)], axis=3)
    grad_group = [
        lax.all_gather(tie(g.astype(BF16), token), "seq", axis=0, tiled=True) for g in grad_out
    ]
    per = chips // KV

    def to_slots(value):
        value = jnp.repeat(value, per, axis=2) if per > 1 else value
        value = jnp.concatenate([value, value], axis=2)
        return lax.dynamic_slice_in_dim(value, place, chips, axis=2)

    def from_slots(value):
        value = jnp.concatenate([value, value], axis=2)
        value = lax.dynamic_slice_in_dim(value, (chips - place) % chips, chips, axis=2)
        if per > 1:
            shape = value.shape
            value = value.reshape(*shape[:2], KV, per, *shape[3:]).astype(F32).sum(axis=3)
        return value.astype(BF16)

    def to_heads(halves):
        value = jnp.stack([h.reshape(rows_here, seg_len, chips, -1, HEAD) for h in halves])
        value = value.transpose(1, 3, 0, 4, 2, 5)
        return value.reshape(rows_here, chips, -1, HEAD)

    def from_heads(value):
        value = value.reshape(rows_here, chips, 2, -1, seg_len, HEAD).transpose(2, 0, 4, 1, 3, 5)
        value = value.reshape(2, rows_here * seg_len, -1)
        return [value[0], value[1]]

    def heads_dot(spec, left, right):
        return jnp.einsum(spec, left, right, preferred_element_type=F32)

    key_pos = (starts[:, None] + jnp.arange(seg_len, dtype=jnp.int32)).reshape(-1)
    limit = jnp.minimum(query_pos[None], lengths[:, None] - 1)
    limit = jnp.tile(limit, (1, HEADS // chips))
    valid = (key_pos[None, None] <= limit[:, :, None])[:, None]
    scale = HEAD ** (-0.5)

    inputs = tokens.astype(F32).reshape(rows_here * seg_len, width)
    inverse_one = lax.rsqrt(jnp.mean(inputs * inputs, axis=-1, keepdims=True) + EPS)
    normed_one = (inputs * inverse_one * gain_one).astype(BF16)
    query = query_proj.features(normed_one)
    cache_slot = to_slots(cache_all)
    keys, values = cache_slot[0], cache_slot[1]
    query_heads = to_heads(query)
    scores = heads_dot("rjqd,rjkd->rjqk", query_heads, keys) * scale
    scores = jnp.where(valid, scores, NEG)
    best = tie(jnp.max(scores, axis=-1, keepdims=True), output_proj.steps[1])
    weights = jnp.exp(scores - best)
    total = jnp.sum(weights, axis=-1, keepdims=True)
    mixed_heads = heads_dot("rjqk,rjkd->rjqd", weights.astype(BF16), values) / total
    lse = best + jnp.log(total)
    mixed = from_heads(mixed_heads.astype(BF16))
    mixed, grad_group[0] = lax.optimization_barrier((mixed, grad_group[0]))
    middle_all = inputs + output_proj.back(mixed)
    inverse_all = lax.rsqrt(jnp.mean(middle_all * middle_all, axis=-1, keepdims=True) + EPS)
    normed_all = (middle_all * inverse_all * gain_two).astype(BF16)
    normed_all, grad_group[1:] = lax.optimization_barrier((normed_all, grad_group[1:]))

    def split(value):
        return [value[r * seg_len : (r + 1) * seg_len] for r in range(rows_here)]

    middle, inverse_two, normed_two = split(middle_all), split(inverse_all), split(normed_all)
    normed_group = [lax.all_gather(n, "seq", axis=0, tiled=True) for n in normed_two]

    main, fill = Lane(), Lane()
    units = down_weight.shape[0]
    hidden, grad_gate_up, grad_part, ffn_part = [], [], [], []
    for r in range(rows_here):
        kept = dot(normed_group[r], gate_up_weight, ((1,), (1,)))
        gate, upper = kept[:, :units], kept[:, units:]
        sigma = jax.nn.sigmoid(gate)
        grad_hidden = dot(beside(grad_group[r], fill), down_weight, ((1,), (1,)))
        hidden.append((gate * sigma * upper).astype(BF16))
        grad_gate = grad_hidden * upper * sigma * (1.0 + gate * (1.0 - sigma))
        grad_up = grad_hidden * gate * sigma
        grad_gate_up.append(jnp.concatenate([grad_gate, grad_up], axis=1).astype(BF16))
        part = dot(beside(grad_gate_up[r], fill), gate_up_weight, ((1,), (0,))).astype(BF16)
        if r + 1 < rows_here:
            part, normed_group[r + 1] = lax.optimization_barrier((part, normed_group[r + 1]))
        grad_part.append(lax.psum_scatter(part, "seq", scatter_dimension=0, tiled=True))
        ffn_part.append(dot(hidden[r], down_weight, ((1,), (0,))).astype(BF16))

    def over_tokens(left, right):
        terms = [dot(a, b, ((0,), (0,))) for a, b in zip(left, right, strict=True)]
        return sum(terms).astype(BF16)

    for r in range(rows_here - 1):
        grad_part[r], grad_gate_up[-1], hidden[-1] = lax.optimization_barrier(
            (grad_part[r], grad_gate_up[-1], hidden[-1])
        )
    in_part = over_tokens(grad_gate_up, normed_group)
    down_part = over_tokens(hidden, grad_group)
    parts = (in_part, down_part)
    summed = lax.psum(parts, "rows")

    grad_middle, gain_two_grad = [], 0.0
    for r in range(rows_here):
        grad_normed_two = grad_part[r].astype(F32)
        if r:
            grad_normed_two, parts = lax.optimization_barrier((grad_normed_two, parts))
        scaled_two = middle[r] * inverse_two[r]
        gain_two_grad += jnp.sum(grad_normed_two * scaled_two, axis=0)
        grad_middle.append(
            grad_out[r] + norm_back(grad_normed_two, scaled_two, inverse_two[r], gain_two)
        )
    part = tie(ffn_part[0], grad_middle[-1])
    fill.add(("ffn", 0), scatter_tokens(part, chips, place, core))
    grad_middle = jnp.concatenate(grad_middle, axis=0)
    grad_branch = grad_middle.astype(BF16)
    output_part = [dot(half, grad_branch, ((0,), (0,))).astype(BF16) for half in mixed]

    def scatter_rows(parts):
        def take(value, j):
            return block_of(value, j, chips)

        return scatter_halves(lambda j: take(parts[0], j), parts[1], take, chips)

    main.add("output", scatter_rows(output_part))
    grad_heads = to_heads(output_proj.features(tie(grad_branch, output_part[1]), (main, fill)))
    grad_heads = beside(grad_heads, main, fill)
    delta = jnp.sum(grad_heads.astype(F32) * mixed_heads, axis=-1, keepdims=True)
    scores = heads_dot("rjqd,rjkd->rjqk", query_heads, keys) * scale
    probs = jnp.where(valid, jnp.exp(scores - lse), 0.0)
    grad_probs = heads_dot("rjqd,rjkd->rjqk", grad_heads, values)
    grad_scores = beside((probs * (grad_probs - delta)).astype(BF16), main, fill)
    query_term = from_heads(
        (heads_dot("rjqk,rjkd->rjqd", grad_scores, keys) * scale).astype(BF16)
    )
    query_part = [dot(half, normed_one, ((0,), (0,))).astype(BF16) for half in query_term]
    query_part, grad_scores = lax.optimization_barrier((query_part, grad_scores))
    output_sum = main.result("output")
    main.add("query", scatter_rows(query_part))
    sent = main.step()
    grad_keys = heads_dot("rjqk,rjqd->rjkd", grad_scores, query_heads) * scale
    grad_values = heads_dot("rjqk,rjqd->rjkd", probs.astype(BF16), grad_heads)
    cache_part = from_slots(jnp.stack([grad_keys.astype(BF16), grad_values.astype(BF16)]))
    cache_part = tie(cache_part, sent)
    half_len = cache_part.shape[3] // 2

    def positions_of(value, j):
        return value[:, :, :, j * seg_len : (j + 1) * seg_len]

    cache_lane, last_lane = Lane(), Lane()
    cache_lane.add(
        "cache",
        scatter_halves(
            lambda j: positions_of(cache_part, j), cache_part[:, :, :, half_len:], positions_of, chips
        ),
    )
    fill.result(("ffn", 0))
    for r in range(1, rows_here):
        last_lane.add(("ffn", r), scatter_tokens(tie(ffn_part[r], sent), chips, place, core))
    last_sent = [[lane.step() for _ in range(chips - 1)] for lane in (cache_lane, last_lane)]

    grad_normed_one = query_proj.back(query_term)
    scaled_one = inputs * inverse_one
    gain_one_grad = jnp.sum(grad_normed_one * scaled_one, axis=0)
    input_grad = grad_middle + norm_back(grad_normed_one, scaled_one, inverse_one, gain_one)
    gain_grad = jnp.stack([gain_one_grad, gain_two_grad])

    ffn_out = [fill.result(("ffn", 0))]
    ffn_out += [last_lane.result(("ffn", r)) for r in range(1, rows_here)]
    layer_out = [(live[r] * (middle[r] + ffn_out[r])).astype(BF16) for r in range(rows_here)]
    cache_grad = cache_lane.result("cache")
    cache_grad = cache_grad.transpose(1, 3, 0, 2, 4).reshape(rows_here, seg_len, 2, KV * HEAD)
    summed = tie(summed, [sent[-1] for sent in last_sent])
    summed, gain_grad = lax.optimization_barrier((summed, gain_grad))
    in_grad, down_grad = summed
    in_grad = in_grad.reshape(2, units, width).transpose(1, 0, 2)
    in_grad = lax.optimization_barrier(in_grad)
    gain_grad = sum_all(gain_grad, rows, seq)
    output_grad, query_grad = sum_rows((output_sum, main.result("query")), rows)
    return (
        jnp.stack(layer_out),
        input_grad.reshape(rows_here, seg_len, width),
        cache_grad,
        gain_grad,
        query_grad,
        output_grad,
        in_grad.astype(F32),
        down_grad.astype(F32),
    )


def solution(mesh):
    in_specs = (
        P("rows", "seq", None),
        P("rows", "seq", None, None),
        P("rows"),
        P(),
        P("seq", None),
        P("seq", None),
        P("seq", None, None),
        P("seq", None),
        P("rows", "seq", None),
    )
    out_specs = (
        P("rows", "seq", None),
        P("rows", "seq", None),
        P("rows", "seq", None, None),
        P(),
        P("seq", None),
        P("seq", None),
        P("seq", None, None),
        P("seq", None),
    )
    return jax.shard_map(local, mesh=mesh, in_specs=in_specs, out_specs=out_specs, check_vma=False)
```

```python
import jax
import jax.numpy as jnp
from jax import lax
from jax.sharding import PartitionSpec as P

HEADS = 16
HEAD = 128
KV = 4
GROUP = 4
EPS = 1e-05
NEG = -1e30
F32 = jnp.float32
BF16 = jnp.bfloat16


def dot(left, right, dims):
    return lax.dot_general(left, right, (dims, ((), ())), preferred_element_type=F32)


def tie(value, dep):
    if dep is None:
        return value
    return lax.optimization_barrier((value, dep))[0]


def norm_back(grad_normed, scaled, inverse, gain):
    inner = grad_normed * gain
    return inverse * (inner - scaled * jnp.mean(inner * scaled, axis=-1, keepdims=True))


def swap_core(value, seq):
    return lax.ppermute(value, "seq", [(s, s ^ 1) for s in range(seq)])


def ring(value, chips):
    pairs = [(2 * z + c, 2 * ((z + 1) % chips) + c) for z in range(chips) for c in range(2)]
    return lax.ppermute(value, "seq", pairs)


def swap_row(value, rows, mask):
    return lax.ppermute(value, "rows", [(r, r ^ mask) for r in range(rows)])


def ring_gather(own, chips, dep=None):
    got = [tie(own, dep)]
    for _ in range(1, chips):
        got.append(ring(got[-1], chips))
    return [own] + got[:0:-1], got[-1]


def ring_scatter(parts, chips):
    sent = parts[chips - 1]
    for j in range(chips - 2, -1, -1):
        after = yield sent
        total = ring(sent, chips).astype(F32) + tie(parts[j], after).astype(F32)
        sent = total.astype(BF16)
    return total


class Lane:
    def __init__(self):
        self.waiting, self.results, self.begun, self.sent = [], {}, set(), None

    def add(self, name, steps):
        self.waiting.append((name, steps))

    def step(self, after=None):
        if self.waiting:
            name, steps = self.waiting[0]
            try:
                self.sent = next(steps) if name not in self.begun else steps.send(after)
                self.begun.add(name)
                return self.sent
            except StopIteration as end:
                self.results[name] = end.value
                self.waiting.pop(0)
                return self.step(after)
        return None

    def result(self, name):
        while name not in self.results:
            self.step()
        return self.results[name]


def beside(value, *lanes):
    for lane in lanes:
        value = tie(value, lane.step(value))
    return value


def xor_order(value, at):
    shape = value.shape
    value = value.reshape(2, 2, *shape[1:])
    value = jnp.where(at % 2 == 1, value[:, ::-1], value)
    return jnp.where(at // 2 == 1, value[::-1], value).reshape(shape)


def own_order(value, chips, place, core):
    count = value.shape[0]
    value = value.reshape(count, chips, 2, -1)
    value = jnp.where(core == 0, value, value[:, :, ::-1])
    value = jnp.concatenate([value, value], axis=1)
    value = lax.dynamic_slice_in_dim(value, place, chips, axis=1)
    return value.transpose(0, 2, 1, 3).reshape(count, -1)


def index_order(value, chips, place, core):
    count = value.shape[0]
    value = value.reshape(count, 2, chips, -1).transpose(0, 2, 1, 3)
    value = jnp.concatenate([value, value], axis=1)
    value = lax.dynamic_slice_in_dim(value, (chips - place) % chips, chips, axis=1)
    value = jnp.where(core == 0, value, value[:, :, ::-1])
    return value.reshape(count, -1)


class Weight:
    def __init__(self, shard, chips, rows, row_at, order, dep=None):
        seq = 2 * chips
        self.chips, self.row_at, self.order = chips, row_at, order
        depth, width = shard.shape
        self.depth = depth
        self.split = rows == 4 and depth % 32 == 0 and width % 512 == 0
        if not self.split:
            self.whole = lax.all_gather(shard, "seq", axis=0, tiled=True)
            self.token = dep
            self.steps = [None, None]
            return
        part = width // rows
        half = part // 2
        mine = lax.dynamic_slice_in_dim(shard, row_at * part, part, axis=1)
        slots, self.token = ring_gather(mine, chips, dep=dep)
        first = jnp.stack([v[:, :half] for v in slots[1:]])
        second = jnp.stack([v[:, half:] for v in slots[1:]])
        first_x = swap_row(first, rows, 1)
        second_y = swap_row(second, rows, 2)
        first_pair = swap_row(jnp.stack([first, first_x]), rows, 2)
        second_pair = swap_row(jnp.stack([second, second_y]), rows, 1)
        parts = [first, second, first_x, second_pair[0]]
        parts += [first_pair[0], second_y, first_pair[1], second_pair[1]]
        parts = jnp.concatenate(parts, axis=0).reshape(rows * 2, (chips - 1) * depth, half)
        self.steps = [(first_x, second_y), (first_pair, second_pair)]
        self.far = [parts, swap_core(parts, seq)]
        self.near = [shard, swap_core(shard, seq)]

    def features(self, value, lanes=()):
        if not self.split:
            out = own_order(dot(value, self.whole, ((1,), (1,))), *self.order)
            half = out.shape[1] // 2
            return [out[:, :half].astype(BF16), out[:, half:].astype(BF16)]
        count = value.shape[0]
        out = []
        for near, far in zip(self.near, self.far, strict=True):
            if out:
                value = beside(value, *lanes)
            blocks = value.reshape(count, 4, 2, -1).transpose(1, 2, 0, 3)
            blocks = xor_order(blocks, self.row_at).reshape(8, count, -1)
            term = jnp.einsum("ktc,kfc->ktf", blocks, far, preferred_element_type=F32)
            term = jnp.sum(term, axis=0).astype(BF16)
            out.append(jnp.concatenate([dot(value, near, ((1,), (1,))).astype(BF16), term], axis=1))
        return out

    def back(self, halves):
        if not self.split:
            value = jnp.concatenate(halves, axis=1)
            return dot(index_order(value, *self.order), self.whole, ((1,), (0,)))
        count = halves[0].shape[0]
        near_sum = far_sum = 0.0
        for part, near, far in zip(halves, self.near, self.far, strict=True):
            near_sum += dot(part[:, : self.depth], near, ((1,), (0,)))
            far_sum += jnp.einsum(
                "tf,kfc->ktc", part[:, self.depth :], far, preferred_element_type=F32
            )
        far_sum = xor_order(far_sum.reshape(4, 2, count, -1), self.row_at)
        far_sum = jnp.concatenate([far_sum[k, h] for k in range(4) for h in range(2)], axis=1)
        return near_sum + far_sum


def scatter_halves(own, sib, got_at, chips):
    got = swap_core(sib, 2 * chips)
    parts = [own(j).astype(F32) + got_at(got, j).astype(F32) for j in range(chips)]
    return (yield from ring_scatter([p.astype(BF16) for p in parts], chips))


def block_of(value, j, chips):
    size = value.shape[0] // chips
    return value[j * size : (j + 1) * size]


def scatter_tokens(part, chips, place, core):
    size = part.shape[0] // (2 * chips)

    def block(j, at):
        start = (2 * ((place + j) % chips) + at) * size
        return lax.dynamic_slice_in_dim(part, start, size, axis=0)

    sib = jnp.concatenate([block(j, 1 - core) for j in range(chips)], axis=0)
    return scatter_halves(
        lambda j: block(j, core), sib, lambda got, j: block_of(got, j, chips), chips
    )


def sum_rows(values, rows):
    if rows != 4:
        return [lax.psum(v.astype(BF16), "rows").astype(F32) for v in values]

    def pair(item, mask):
        return item.astype(F32) + swap_row(item, rows, mask).astype(F32)

    out = []
    for value in values:
        half = value.shape[0] // 2
        first, second = value[:half].astype(BF16), value[half:].astype(BF16)
        first, second = pair(first, 1).astype(BF16), pair(second, 2).astype(BF16)
        out.append(jnp.concatenate([pair(first, 2), pair(second, 1)], axis=0))
    return out


def sum_all(value, rows, seq):
    mask = 1
    while mask < seq:
        value = value + lax.ppermute(value, "seq", [(s, s ^ mask) for s in range(seq)])
        mask *= 2
    mask = 1
    while mask < rows:
        value = value + swap_row(value, rows, mask)
        mask *= 2
    return value


def local(
    tokens,
    kv_cache,
    lengths,
    norm_gains,
    query_weight,
    output_weight,
    ffn_in_weight,
    down_weight,
    cotangent,
):
    rows_here, seg_len, width = tokens.shape
    seq = lax.axis_size("seq")
    rows = lax.axis_size("rows")
    chips = seq // 2
    seq_at = lax.axis_index("seq")
    row_at = lax.axis_index("rows")
    place, core = seq_at // 2, seq_at % 2
    order = (chips, place, core)
    gain_one, gain_two = norm_gains[0], norm_gains[1]
    query_pos = seq_at * seg_len + jnp.arange(seg_len, dtype=jnp.int32)
    chip_range = jnp.arange(chips, dtype=jnp.int32)
    ring_at = (place + chip_range) % chips
    starts = jnp.concatenate([2 * ring_at + core, 2 * ring_at + 1 - core]) * seg_len

    live = [
        (query_pos < lengths[r]).astype(F32).reshape(seg_len, 1) for r in range(rows_here)
    ]
    grad_out = [cotangent[r].astype(F32) * live[r] for r in range(rows_here)]
    gate_up_weight = jnp.concatenate([ffn_in_weight[:, 0], ffn_in_weight[:, 1]], axis=0)
    query_proj = Weight(query_weight, chips, rows, row_at, order)
    cache_own = kv_cache.reshape(rows_here, seg_len, 2, KV, HEAD).transpose(2, 0, 3, 1, 4)
    output_proj = Weight(output_weight, chips, rows, row_at, order, dep=query_proj.token)
    cache_slots, token = ring_gather(cache_own, chips, dep=output_proj.token)
    cache_block = jnp.concatenate(cache_slots, axis=3)
    cache_block = tie(cache_block, output_proj.steps[0])
    cache_all = jnp.concatenate([cache_block, swap_core(cache_block, seq)], axis=3)
    grad_group = [
        lax.all_gather(tie(g.astype(BF16), token), "seq", axis=0, tiled=True) for g in grad_out
    ]
    per = chips // KV

    def to_slots(value):
        value = jnp.repeat(value, per, axis=2) if per > 1 else value
        value = jnp.concatenate([value, value], axis=2)
        return lax.dynamic_slice_in_dim(value, place, chips, axis=2)

    def from_slots(value):
        value = jnp.concatenate([value, value], axis=2)
        value = lax.dynamic_slice_in_dim(value, (chips - place) % chips, chips, axis=2)
        if per > 1:
            shape = value.shape
            value = value.reshape(*shape[:2], KV, per, *shape[3:]).astype(F32).sum(axis=3)
        return value.astype(BF16)

    def to_heads(halves):
        value = jnp.stack([h.reshape(rows_here, seg_len, chips, -1, HEAD) for h in halves])
        value = value.transpose(1, 3, 0, 4, 2, 5)
        return value.reshape(rows_here, chips, -1, HEAD)

    def from_heads(value):
        value = value.reshape(rows_here, chips, 2, -1, seg_len, HEAD).transpose(2, 0, 4, 1, 3, 5)
        value = value.reshape(2, rows_here * seg_len, -1)
        return [value[0], value[1]]

    def heads_dot(spec, left, right):
        return jnp.einsum(spec, left, right, preferred_element_type=F32)

    key_pos = (starts[:, None] + jnp.arange(seg_len, dtype=jnp.int32)).reshape(-1)
    limit = jnp.minimum(query_pos[None], lengths[:, None] - 1)
    limit = jnp.tile(limit, (1, HEADS // chips))
    valid = (key_pos[None, None] <= limit[:, :, None])[:, None]
    scale = HEAD ** (-0.5)

    inputs = tokens.astype(F32).reshape(rows_here * seg_len, width)
    inverse_one = lax.rsqrt(jnp.mean(inputs * inputs, axis=-1, keepdims=True) + EPS)
    normed_one = (inputs * inverse_one * gain_one).astype(BF16)
    query = query_proj.features(normed_one)
    cache_slot = to_slots(cache_all)
    keys, values = cache_slot[0], cache_slot[1]
    query_heads = to_heads(query)
    scores = heads_dot("rjqd,rjkd->rjqk", query_heads, keys) * scale
    scores = jnp.where(valid, scores, NEG)
    best = tie(jnp.max(scores, axis=-1, keepdims=True), output_proj.steps[1])
    weights = jnp.exp(scores - best)
    total = jnp.sum(weights, axis=-1, keepdims=True)
    mixed_heads = heads_dot("rjqk,rjkd->rjqd", weights.astype(BF16), values) / total
    lse = best + jnp.log(total)
    mixed = from_heads(mixed_heads.astype(BF16))
    mixed, grad_group[0] = lax.optimization_barrier((mixed, grad_group[0]))
    middle_all = inputs + output_proj.back(mixed)
    inverse_all = lax.rsqrt(jnp.mean(middle_all * middle_all, axis=-1, keepdims=True) + EPS)
    normed_all = (middle_all * inverse_all * gain_two).astype(BF16)
    normed_all, grad_group[1:] = lax.optimization_barrier((normed_all, grad_group[1:]))

    def split(value):
        return [value[r * seg_len : (r + 1) * seg_len] for r in range(rows_here)]

    middle, inverse_two, normed_two = split(middle_all), split(inverse_all), split(normed_all)
    normed_group = [lax.all_gather(n, "seq", axis=0, tiled=True) for n in normed_two]

    main, fill = Lane(), Lane()
    units = down_weight.shape[0]
    hidden, grad_gate_up, grad_part, ffn_part = [], [], [], []
    for r in range(rows_here):
        kept = dot(normed_group[r], gate_up_weight, ((1,), (1,)))
        gate, upper = kept[:, :units], kept[:, units:]
        sigma = jax.nn.sigmoid(gate)
        grad_hidden = dot(beside(grad_group[r], fill), down_weight, ((1,), (1,)))
        hidden.append((gate * sigma * upper).astype(BF16))
        grad_gate = grad_hidden * upper * sigma * (1.0 + gate * (1.0 - sigma))
        grad_up = grad_hidden * gate * sigma
        grad_gate_up.append(jnp.concatenate([grad_gate, grad_up], axis=1).astype(BF16))
        part = dot(beside(grad_gate_up[r], fill), gate_up_weight, ((1,), (0,))).astype(BF16)
        if r + 1 < rows_here:
            part, normed_group[r + 1] = lax.optimization_barrier((part, normed_group[r + 1]))
        grad_part.append(lax.psum_scatter(part, "seq", scatter_dimension=0, tiled=True))
        ffn_part.append(dot(hidden[r], down_weight, ((1,), (0,))).astype(BF16))

    def over_tokens(left, right):
        terms = [dot(a, b, ((0,), (0,))) for a, b in zip(left, right, strict=True)]
        return sum(terms).astype(BF16)

    for r in range(rows_here - 1):
        grad_part[r], grad_gate_up[-1], hidden[-1] = lax.optimization_barrier(
            (grad_part[r], grad_gate_up[-1], hidden[-1])
        )
    in_part = over_tokens(grad_gate_up, normed_group)
    down_part = over_tokens(hidden, grad_group)
    parts = (in_part, down_part)
    summed = lax.psum(parts, "rows")

    grad_middle, gain_two_grad = [], 0.0
    for r in range(rows_here):
        grad_normed_two = grad_part[r].astype(F32)
        if r:
            grad_normed_two, parts = lax.optimization_barrier((grad_normed_two, parts))
        scaled_two = middle[r] * inverse_two[r]
        gain_two_grad += jnp.sum(grad_normed_two * scaled_two, axis=0)
        grad_middle.append(
            grad_out[r] + norm_back(grad_normed_two, scaled_two, inverse_two[r], gain_two)
        )
    part = tie(ffn_part[0], grad_middle[-1])
    fill.add(("ffn", 0), scatter_tokens(part, chips, place, core))
    grad_middle = jnp.concatenate(grad_middle, axis=0)
    grad_branch = grad_middle.astype(BF16)
    output_part = [dot(half, grad_branch, ((0,), (0,))).astype(BF16) for half in mixed]

    def scatter_rows(parts):
        def take(value, j):
            return block_of(value, j, chips)

        return scatter_halves(lambda j: take(parts[0], j), parts[1], take, chips)

    main.add("output", scatter_rows(output_part))
    grad_heads = to_heads(output_proj.features(tie(grad_branch, output_part[1]), (main, fill)))
    grad_heads = beside(grad_heads, main, fill)
    delta = jnp.sum(grad_heads.astype(F32) * mixed_heads, axis=-1, keepdims=True)
    scores = heads_dot("rjqd,rjkd->rjqk", query_heads, keys) * scale
    probs = jnp.where(valid, jnp.exp(scores - lse), 0.0)
    grad_probs = heads_dot("rjqd,rjkd->rjqk", grad_heads, values)
    grad_scores = beside((probs * (grad_probs - delta)).astype(BF16), main, fill)
    query_term = from_heads(
        (heads_dot("rjqk,rjkd->rjqd", grad_scores, keys) * scale).astype(BF16)
    )
    query_part = [dot(half, normed_one, ((0,), (0,))).astype(BF16) for half in query_term]
    query_part, grad_scores = lax.optimization_barrier((query_part, grad_scores))
    output_sum = main.result("output")
    main.add("query", scatter_rows(query_part))
    sent = main.step()
    grad_keys = heads_dot("rjqk,rjqd->rjkd", grad_scores, query_heads) * scale
    grad_values = heads_dot("rjqk,rjqd->rjkd", probs.astype(BF16), grad_heads)
    cache_part = from_slots(jnp.stack([grad_keys.astype(BF16), grad_values.astype(BF16)]))
    cache_part = tie(cache_part, sent)
    half_len = cache_part.shape[3] // 2

    def positions_of(value, j):
        return value[:, :, :, j * seg_len : (j + 1) * seg_len]

    cache_lane, last_lane = Lane(), Lane()
    cache_lane.add(
        "cache",
        scatter_halves(
            lambda j: positions_of(cache_part, j), cache_part[:, :, :, half_len:], positions_of, chips
        ),
    )
    fill.result(("ffn", 0))
    for r in range(1, rows_here):
        last_lane.add(("ffn", r), scatter_tokens(tie(ffn_part[r], sent), chips, place, core))
    last_sent = [[lane.step() for _ in range(chips - 1)] for lane in (cache_lane, last_lane)]

    grad_normed_one = query_proj.back(query_term)
    scaled_one = inputs * inverse_one
    gain_one_grad = jnp.sum(grad_normed_one * scaled_one, axis=0)
    input_grad = grad_middle + norm_back(grad_normed_one, scaled_one, inverse_one, gain_one)
    gain_grad = jnp.stack([gain_one_grad, gain_two_grad])

    ffn_out = [fill.result(("ffn", 0))]
    ffn_out += [last_lane.result(("ffn", r)) for r in range(1, rows_here)]
    layer_out = [(live[r] * (middle[r] + ffn_out[r])).astype(BF16) for r in range(rows_here)]
    cache_grad = cache_lane.result("cache")
    cache_grad = cache_grad.transpose(1, 3, 0, 2, 4).reshape(rows_here, seg_len, 2, KV * HEAD)
    summed = tie(summed, [sent[-2] for sent in last_sent])
    summed, gain_grad = lax.optimization_barrier((summed, gain_grad))
    in_grad, down_grad = summed
    in_grad = in_grad.reshape(2, units, width).transpose(1, 0, 2)
    in_grad = lax.optimization_barrier(in_grad)
    gain_grad = sum_all(gain_grad, rows, seq)
    output_grad, query_grad = sum_rows((output_sum, main.result("query")), rows)
    return (
        jnp.stack(layer_out),
        input_grad.reshape(rows_here, seg_len, width),
        cache_grad,
        gain_grad,
        query_grad,
        output_grad,
        in_grad.astype(F32),
        down_grad.astype(F32),
    )


def solution(mesh):
    in_specs = (
        P("rows", "seq", None),
        P("rows", "seq", None, None),
        P("rows"),
        P(),
        P("seq", None),
        P("seq", None),
        P("seq", None, None),
        P("seq", None),
        P("rows", "seq", None),
    )
    out_specs = (
        P("rows", "seq", None),
        P("rows", "seq", None),
        P("rows", "seq", None, None),
        P(),
        P("seq", None),
        P("seq", None),
        P("seq", None, None),
        P("seq", None),
    )
    return jax.shard_map(local, mesh=mesh, in_specs=in_specs, out_specs=out_specs, check_vma=False)
```

```python
import jax
import jax.numpy as jnp
from jax import lax
from jax.sharding import PartitionSpec as P

HEADS = 16
HEAD = 128
KV = 4
GROUP = 4
EPS = 1e-05
NEG = -1e30
F32 = jnp.float32
BF16 = jnp.bfloat16


def dot(left, right, dims):
    return lax.dot_general(left, right, (dims, ((), ())), preferred_element_type=F32)


def tie(value, dep):
    if dep is None:
        return value
    return lax.optimization_barrier((value, dep))[0]


def norm_back(grad_normed, scaled, inverse, gain):
    inner = grad_normed * gain
    return inverse * (inner - scaled * jnp.mean(inner * scaled, axis=-1, keepdims=True))


def swap_core(value, seq):
    return lax.ppermute(value, "seq", [(s, s ^ 1) for s in range(seq)])


def ring(value, chips):
    pairs = [(2 * z + c, 2 * ((z + 1) % chips) + c) for z in range(chips) for c in range(2)]
    return lax.ppermute(value, "seq", pairs)


def swap_row(value, rows, mask):
    return lax.ppermute(value, "rows", [(r, r ^ mask) for r in range(rows)])


def ring_gather(own, chips, dep=None):
    got = [tie(own, dep)]
    for _ in range(1, chips):
        got.append(ring(got[-1], chips))
    return [own] + got[:0:-1], got[-1]


def ring_scatter(parts, chips):
    sent = parts[chips - 1]
    for j in range(chips - 2, -1, -1):
        after = yield sent
        total = ring(sent, chips).astype(F32) + tie(parts[j], after).astype(F32)
        sent = total.astype(BF16)
    return total


class Lane:
    def __init__(self):
        self.waiting, self.results, self.begun, self.sent = [], {}, set(), None

    def add(self, name, steps):
        self.waiting.append((name, steps))

    def step(self, after=None):
        if self.waiting:
            name, steps = self.waiting[0]
            try:
                self.sent = next(steps) if name not in self.begun else steps.send(after)
                self.begun.add(name)
                return self.sent
            except StopIteration as end:
                self.results[name] = end.value
                self.waiting.pop(0)
                return self.step(after)
        return None

    def result(self, name):
        while name not in self.results:
            self.step()
        return self.results[name]


def beside(value, *lanes):
    for lane in lanes:
        value = tie(value, lane.step(value))
    return value


def xor_order(value, at):
    shape = value.shape
    value = value.reshape(2, 2, *shape[1:])
    value = jnp.where(at % 2 == 1, value[:, ::-1], value)
    return jnp.where(at // 2 == 1, value[::-1], value).reshape(shape)


def own_order(value, chips, place, core):
    count = value.shape[0]
    value = value.reshape(count, chips, 2, -1)
    value = jnp.where(core == 0, value, value[:, :, ::-1])
    value = jnp.concatenate([value, value], axis=1)
    value = lax.dynamic_slice_in_dim(value, place, chips, axis=1)
    return value.transpose(0, 2, 1, 3).reshape(count, -1)


def index_order(value, chips, place, core):
    count = value.shape[0]
    value = value.reshape(count, 2, chips, -1).transpose(0, 2, 1, 3)
    value = jnp.concatenate([value, value], axis=1)
    value = lax.dynamic_slice_in_dim(value, (chips - place) % chips, chips, axis=1)
    value = jnp.where(core == 0, value, value[:, :, ::-1])
    return value.reshape(count, -1)


class Weight:
    def __init__(self, shard, chips, rows, row_at, order, dep=None):
        seq = 2 * chips
        self.chips, self.row_at, self.order = chips, row_at, order
        depth, width = shard.shape
        self.depth = depth
        self.split = rows == 4 and depth % 32 == 0 and width % 512 == 0
        if not self.split:
            self.whole = lax.all_gather(shard, "seq", axis=0, tiled=True)
            self.token = dep
            self.steps = [None, None]
            return
        part = width // rows
        half = part // 2
        mine = lax.dynamic_slice_in_dim(shard, row_at * part, part, axis=1)
        slots, self.token = ring_gather(mine, chips, dep=dep)
        first = jnp.stack([v[:, :half] for v in slots[1:]])
        second = jnp.stack([v[:, half:] for v in slots[1:]])
        first_x = swap_row(first, rows, 1)
        second_y = swap_row(second, rows, 2)
        first_pair = swap_row(jnp.stack([first, first_x]), rows, 2)
        second_pair = swap_row(jnp.stack([second, second_y]), rows, 1)
        parts = [first, second, first_x, second_pair[0]]
        parts += [first_pair[0], second_y, first_pair[1], second_pair[1]]
        parts = jnp.concatenate(parts, axis=0).reshape(rows * 2, (chips - 1) * depth, half)
        self.steps = [(first_x, second_y), (first_pair, second_pair)]
        self.far = [parts, swap_core(parts, seq)]
        self.near = [shard, swap_core(shard, seq)]

    def features(self, value, lanes=()):
        if not self.split:
            out = own_order(dot(value, self.whole, ((1,), (1,))), *self.order)
            half = out.shape[1] // 2
            return [out[:, :half].astype(BF16), out[:, half:].astype(BF16)]
        count = value.shape[0]
        out = []
        for near, far in zip(self.near, self.far, strict=True):
            if out:
                value = beside(value, *lanes)
            blocks = value.reshape(count, 4, 2, -1).transpose(1, 2, 0, 3)
            blocks = xor_order(blocks, self.row_at).reshape(8, count, -1)
            term = jnp.einsum("ktc,kfc->ktf", blocks, far, preferred_element_type=F32)
            term = jnp.sum(term, axis=0).astype(BF16)
            out.append(jnp.concatenate([dot(value, near, ((1,), (1,))).astype(BF16), term], axis=1))
        return out

    def back(self, halves):
        if not self.split:
            value = jnp.concatenate(halves, axis=1)
            return dot(index_order(value, *self.order), self.whole, ((1,), (0,)))
        count = halves[0].shape[0]
        near_sum = far_sum = 0.0
        for part, near, far in zip(halves, self.near, self.far, strict=True):
            near_sum += dot(part[:, : self.depth], near, ((1,), (0,)))
            far_sum += jnp.einsum(
                "tf,kfc->ktc", part[:, self.depth :], far, preferred_element_type=F32
            )
        far_sum = xor_order(far_sum.reshape(4, 2, count, -1), self.row_at)
        far_sum = jnp.concatenate([far_sum[k, h] for k in range(4) for h in range(2)], axis=1)
        return near_sum + far_sum


def scatter_halves(own, sib, got_at, chips):
    got = swap_core(sib, 2 * chips)
    parts = [own(j).astype(F32) + got_at(got, j).astype(F32) for j in range(chips)]
    return (yield from ring_scatter([p.astype(BF16) for p in parts], chips))


def block_of(value, j, chips):
    size = value.shape[0] // chips
    return value[j * size : (j + 1) * size]


def scatter_tokens(part, chips, place, core):
    size = part.shape[0] // (2 * chips)

    def block(j, at):
        start = (2 * ((place + j) % chips) + at) * size
        return lax.dynamic_slice_in_dim(part, start, size, axis=0)

    sib = jnp.concatenate([block(j, 1 - core) for j in range(chips)], axis=0)
    return scatter_halves(
        lambda j: block(j, core), sib, lambda got, j: block_of(got, j, chips), chips
    )


def sum_rows(values, rows):
    if rows != 4:
        return [lax.psum(v.astype(BF16), "rows").astype(F32) for v in values]

    def pair(item, mask):
        return item.astype(F32) + swap_row(item, rows, mask).astype(F32)

    out = []
    for value in values:
        half = value.shape[0] // 2
        first, second = value[:half].astype(BF16), value[half:].astype(BF16)
        first, second = pair(first, 1).astype(BF16), pair(second, 2).astype(BF16)
        out.append(jnp.concatenate([pair(first, 2), pair(second, 1)], axis=0))
    return out


def sum_all(value, rows, seq):
    mask = 1
    while mask < seq:
        value = value + lax.ppermute(value, "seq", [(s, s ^ mask) for s in range(seq)])
        mask *= 2
    mask = 1
    while mask < rows:
        value = value + swap_row(value, rows, mask)
        mask *= 2
    return value


def local(
    tokens,
    kv_cache,
    lengths,
    norm_gains,
    query_weight,
    output_weight,
    ffn_in_weight,
    down_weight,
    cotangent,
):
    rows_here, seg_len, width = tokens.shape
    seq = lax.axis_size("seq")
    rows = lax.axis_size("rows")
    chips = seq // 2
    seq_at = lax.axis_index("seq")
    row_at = lax.axis_index("rows")
    place, core = seq_at // 2, seq_at % 2
    order = (chips, place, core)
    gain_one, gain_two = norm_gains[0], norm_gains[1]
    query_pos = seq_at * seg_len + jnp.arange(seg_len, dtype=jnp.int32)
    chip_range = jnp.arange(chips, dtype=jnp.int32)
    ring_at = (place + chip_range) % chips
    starts = jnp.concatenate([2 * ring_at + core, 2 * ring_at + 1 - core]) * seg_len

    live = [
        (query_pos < lengths[r]).astype(F32).reshape(seg_len, 1) for r in range(rows_here)
    ]
    grad_out = [cotangent[r].astype(F32) * live[r] for r in range(rows_here)]
    gate_up_weight = jnp.concatenate([ffn_in_weight[:, 0], ffn_in_weight[:, 1]], axis=0)
    query_proj = Weight(query_weight, chips, rows, row_at, order)
    cache_own = kv_cache.reshape(rows_here, seg_len, 2, KV, HEAD).transpose(2, 0, 3, 1, 4)
    output_proj = Weight(output_weight, chips, rows, row_at, order, dep=query_proj.token)
    cache_slots, token = ring_gather(cache_own, chips, dep=output_proj.token)
    cache_block = jnp.concatenate(cache_slots, axis=3)
    cache_block = tie(cache_block, output_proj.steps[0])
    cache_all = jnp.concatenate([cache_block, swap_core(cache_block, seq)], axis=3)
    grad_group = [
        lax.all_gather(tie(g.astype(BF16), token), "seq", axis=0, tiled=True) for g in grad_out
    ]
    per = chips // KV

    def to_slots(value):
        value = jnp.repeat(value, per, axis=2) if per > 1 else value
        value = jnp.concatenate([value, value], axis=2)
        return lax.dynamic_slice_in_dim(value, place, chips, axis=2)

    def from_slots(value):
        value = jnp.concatenate([value, value], axis=2)
        value = lax.dynamic_slice_in_dim(value, (chips - place) % chips, chips, axis=2)
        if per > 1:
            shape = value.shape
            value = value.reshape(*shape[:2], KV, per, *shape[3:]).astype(F32).sum(axis=3)
        return value.astype(BF16)

    def to_heads(halves):
        value = jnp.stack([h.reshape(rows_here, seg_len, chips, -1, HEAD) for h in halves])
        value = value.transpose(1, 3, 0, 4, 2, 5)
        return value.reshape(rows_here, chips, -1, HEAD)

    def from_heads(value):
        value = value.reshape(rows_here, chips, 2, -1, seg_len, HEAD).transpose(2, 0, 4, 1, 3, 5)
        value = value.reshape(2, rows_here * seg_len, -1)
        return [value[0], value[1]]

    def heads_dot(spec, left, right):
        return jnp.einsum(spec, left, right, preferred_element_type=F32)

    key_pos = (starts[:, None] + jnp.arange(seg_len, dtype=jnp.int32)).reshape(-1)
    limit = jnp.minimum(query_pos[None], lengths[:, None] - 1)
    limit = jnp.tile(limit, (1, HEADS // chips))
    valid = (key_pos[None, None] <= limit[:, :, None])[:, None]
    scale = HEAD ** (-0.5)

    inputs = tokens.astype(F32).reshape(rows_here * seg_len, width)
    inverse_one = lax.rsqrt(jnp.mean(inputs * inputs, axis=-1, keepdims=True) + EPS)
    normed_one = (inputs * inverse_one * gain_one).astype(BF16)
    query = query_proj.features(normed_one)
    cache_slot = to_slots(cache_all)
    keys, values = cache_slot[0], cache_slot[1]
    query_heads = to_heads(query)
    scores = heads_dot("rjqd,rjkd->rjqk", query_heads, keys) * scale
    scores = jnp.where(valid, scores, NEG)
    best = tie(jnp.max(scores, axis=-1, keepdims=True), output_proj.steps[1])
    weights = jnp.exp(scores - best)
    total = jnp.sum(weights, axis=-1, keepdims=True)
    mixed_heads = heads_dot("rjqk,rjkd->rjqd", weights.astype(BF16), values) / total
    lse = best + jnp.log(total)
    mixed = from_heads(mixed_heads.astype(BF16))
    mixed, grad_group[0] = lax.optimization_barrier((mixed, grad_group[0]))
    middle_all = inputs + output_proj.back(mixed)
    inverse_all = lax.rsqrt(jnp.mean(middle_all * middle_all, axis=-1, keepdims=True) + EPS)
    normed_all = (middle_all * inverse_all * gain_two).astype(BF16)
    normed_all, grad_group[1:] = lax.optimization_barrier((normed_all, grad_group[1:]))

    def split(value):
        return [value[r * seg_len : (r + 1) * seg_len] for r in range(rows_here)]

    middle, inverse_two, normed_two = split(middle_all), split(inverse_all), split(normed_all)
    normed_group = [lax.all_gather(n, "seq", axis=0, tiled=True) for n in normed_two]

    main, fill = Lane(), Lane()
    units = down_weight.shape[0]
    hidden, grad_gate_up, grad_part, ffn_part = [], [], [], []
    for r in range(rows_here):
        kept = dot(normed_group[r], gate_up_weight, ((1,), (1,)))
        gate, upper = kept[:, :units], kept[:, units:]
        sigma = jax.nn.sigmoid(gate)
        grad_hidden = dot(beside(grad_group[r], fill), down_weight, ((1,), (1,)))
        hidden.append((gate * sigma * upper).astype(BF16))
        grad_gate = grad_hidden * upper * sigma * (1.0 + gate * (1.0 - sigma))
        grad_up = grad_hidden * gate * sigma
        grad_gate_up.append(jnp.concatenate([grad_gate, grad_up], axis=1).astype(BF16))
        part = dot(beside(grad_gate_up[r], fill), gate_up_weight, ((1,), (0,))).astype(BF16)
        if r + 1 < rows_here:
            part, normed_group[r + 1] = lax.optimization_barrier((part, normed_group[r + 1]))
        grad_part.append(lax.psum_scatter(part, "seq", scatter_dimension=0, tiled=True))
        ffn_part.append(dot(hidden[r], down_weight, ((1,), (0,))).astype(BF16))

    def over_tokens(left, right):
        terms = [dot(a, b, ((0,), (0,))) for a, b in zip(left, right, strict=True)]
        return sum(terms).astype(BF16)

    for r in range(rows_here - 1):
        grad_part[r], grad_gate_up[-1], hidden[-1] = lax.optimization_barrier(
            (grad_part[r], grad_gate_up[-1], hidden[-1])
        )
    in_part = over_tokens(grad_gate_up, normed_group)
    down_part = over_tokens(hidden, grad_group)
    parts = (in_part, down_part)
    summed = lax.psum(parts, "rows")

    grad_middle, gain_two_grad = [], 0.0
    for r in range(rows_here):
        grad_normed_two = grad_part[r].astype(F32)
        if r:
            grad_normed_two, parts = lax.optimization_barrier((grad_normed_two, parts))
        scaled_two = middle[r] * inverse_two[r]
        gain_two_grad += jnp.sum(grad_normed_two * scaled_two, axis=0)
        grad_middle.append(
            grad_out[r] + norm_back(grad_normed_two, scaled_two, inverse_two[r], gain_two)
        )
    part = tie(ffn_part[0], grad_middle[-1])
    fill.add(("ffn", 0), scatter_tokens(part, chips, place, core))
    grad_middle = jnp.concatenate(grad_middle, axis=0)
    grad_branch = grad_middle.astype(BF16)
    output_part = [dot(half, grad_branch, ((0,), (0,))).astype(BF16) for half in mixed]

    def scatter_rows(parts):
        def take(value, j):
            return block_of(value, j, chips)

        return scatter_halves(lambda j: take(parts[0], j), parts[1], take, chips)

    main.add("output", scatter_rows(output_part))
    grad_heads = to_heads(output_proj.features(tie(grad_branch, output_part[1]), (main, fill)))
    grad_heads = beside(grad_heads, main, fill)
    delta = jnp.sum(grad_heads.astype(F32) * mixed_heads, axis=-1, keepdims=True)
    scores = heads_dot("rjqd,rjkd->rjqk", query_heads, keys) * scale
    probs = jnp.where(valid, jnp.exp(scores - lse), 0.0)
    grad_probs = heads_dot("rjqd,rjkd->rjqk", grad_heads, values)
    grad_scores = beside((probs * (grad_probs - delta)).astype(BF16), main, fill)
    query_term = from_heads(
        (heads_dot("rjqk,rjkd->rjqd", grad_scores, keys) * scale).astype(BF16)
    )
    query_part = [dot(half, normed_one, ((0,), (0,))).astype(BF16) for half in query_term]
    query_part, grad_scores = lax.optimization_barrier((query_part, grad_scores))
    output_sum = main.result("output")
    main.add("query", scatter_rows(query_part))
    sent = main.step()
    grad_keys = heads_dot("rjqk,rjqd->rjkd", grad_scores, query_heads) * scale
    grad_values = heads_dot("rjqk,rjqd->rjkd", probs.astype(BF16), grad_heads)
    cache_part = from_slots(jnp.stack([grad_keys.astype(BF16), grad_values.astype(BF16)]))
    cache_part = tie(cache_part, sent)
    half_len = cache_part.shape[3] // 2

    def positions_of(value, j):
        return value[:, :, :, j * seg_len : (j + 1) * seg_len]

    cache_lane, last_lane = Lane(), Lane()
    cache_lane.add(
        "cache",
        scatter_halves(
            lambda j: positions_of(cache_part, j), cache_part[:, :, :, half_len:], positions_of, chips
        ),
    )
    fill.result(("ffn", 0))
    for r in range(1, rows_here):
        last_lane.add(("ffn", r), scatter_tokens(tie(ffn_part[r], sent), chips, place, core))
    last_sent = [[lane.step() for _ in range(chips - 1)] for lane in (cache_lane, last_lane)]

    grad_normed_one = query_proj.back(query_term)
    scaled_one = inputs * inverse_one
    gain_one_grad = jnp.sum(grad_normed_one * scaled_one, axis=0)
    input_grad = grad_middle + norm_back(grad_normed_one, scaled_one, inverse_one, gain_one)
    gain_grad = jnp.stack([gain_one_grad, gain_two_grad])

    ffn_out = [fill.result(("ffn", 0))]
    ffn_out += [last_lane.result(("ffn", r)) for r in range(1, rows_here)]
    layer_out = [(live[r] * (middle[r] + ffn_out[r])).astype(BF16) for r in range(rows_here)]
    cache_grad = cache_lane.result("cache")
    cache_grad = cache_grad.transpose(1, 3, 0, 2, 4).reshape(rows_here, seg_len, 2, KV * HEAD)
    summed = tie(summed, [sent[-1] for sent in last_sent])
    summed, gain_grad = lax.optimization_barrier((summed, gain_grad))
    in_grad, down_grad = summed
    in_grad = in_grad.reshape(2, units, width).transpose(1, 0, 2)
    in_grad = lax.optimization_barrier(in_grad)
    for _ in range(chips - 2):
        main.step()
    main.step(in_grad)
    gain_grad = sum_all(gain_grad, rows, seq)
    output_grad, query_grad = sum_rows((output_sum, main.result("query")), rows)
    return (
        jnp.stack(layer_out),
        input_grad.reshape(rows_here, seg_len, width),
        cache_grad,
        gain_grad,
        query_grad,
        output_grad,
        in_grad.astype(F32),
        down_grad.astype(F32),
    )


def solution(mesh):
    in_specs = (
        P("rows", "seq", None),
        P("rows", "seq", None, None),
        P("rows"),
        P(),
        P("seq", None),
        P("seq", None),
        P("seq", None, None),
        P("seq", None),
        P("rows", "seq", None),
    )
    out_specs = (
        P("rows", "seq", None),
        P("rows", "seq", None),
        P("rows", "seq", None, None),
        P(),
        P("seq", None),
        P("seq", None),
        P("seq", None, None),
        P("seq", None),
    )
    return jax.shard_map(local, mesh=mesh, in_specs=in_specs, out_specs=out_specs, check_vma=False)
```
